32 devices in a mesh: path: 2 (over x), dp: 4 (over y, core), mp: 4 (over z).
Axes of the slice: x: 2, y: 2, z: 4, core: 2. Of those that a mesh axis runs over, the one named last changes fastest.
Arguments:
- tokens: bfloat16 [8, 576, 1024], P('dp'), may hold values from -6 to 6
- hires: bfloat16 [8, 32, 32, 1536], P('dp', None, None, 'mp'), may hold values from -6 to 6
- valid_rows: int32 [8], P('dp'), may hold values from 1 to 24, 144 in all
- cotangent: bfloat16 [8, 576, 1024], P('dp'), may hold values from -6 to 6
- attention_norm_gain: float32 [1024], replicated, may hold values from 0.1 to 1.9
- attention_norm_bias: float32 [1024], replicated, may hold values from -1.5 to 1.5
- w_qkv: bfloat16 [1024, 3, 1024], P(None, None, 'mp'), may hold values from -0.1875 to 0.1875
- qv_bias: float32 [2, 1024], P(None, 'mp'), may hold values from -1.5 to 1.5
- w_out: bfloat16 [1024, 1024], P('mp'), may hold values from -0.75 to 0.75
- out_bias: float32 [1024], replicated, may hold values from -1.5 to 1.5
- mlp_norm_gain: float32 [1024], replicated, may hold values from 0.1 to 1.9
- mlp_norm_bias: float32 [1024], replicated, may hold values from -1.5 to 1.5
- w_fc1: bfloat16 [1024, 4096], P(None, 'mp'), may hold values from -0.1875 to 0.1875
- fc1_bias: float32 [4096], P('mp'), may hold values from -1.5 to 1.5
- down_weight: bfloat16 [4096, 1024], P('mp'), may hold values from -0.09375 to 0.09375
- fc2_bias: float32 [1024], replicated, may hold values from -1.5 to 1.5
- w_adapt: bfloat16 [1536, 1024], P('mp'), may hold values from -0.3125 to 0.3125
- gate_param: float32 [1024], replicated, may hold values from -2 to 2
- dw_kernel: float32 [49, 1536], P(None, 'mp'), may hold values from -0.875 to 0.875
- dw_bias: float32 [1536], P('mp'), may hold values from -1.5 to 1.5
- channel_norm_gain: float32 [1536], replicated, may hold values from 0.1 to 1.9
- channel_norm_bias: float32 [1536], replicated, may hold values from -1.5 to 1.5
- w_pw1: bfloat16 [1536, 6144], P(None, 'mp'), may hold values from -0.15625 to 0.15625
- pw1_bias: float32 [6144], P('mp'), may hold values from -1.5 to 1.5
- w_pw2: bfloat16 [6144, 1536], P('mp'), may hold values from -0.078125 to 0.078125
- pw2_bias: float32 [1536], P('mp'), may hold values from -1.5 to 1.5
- layer_scale: float32 [1536], P('mp'), may hold values from 0.3 to 2
Outputs:
- output: bfloat16 [8, 576, 1024], P('dp', 'path', 'mp')
- tokens_grad: bfloat16 [8, 576, 1024], P('dp', 'path', 'mp')
- hires_grad: bfloat16 [8, 32, 32, 1536], P('dp', 'path', None, 'mp')
- grad_norm1_gain: float32 [1024], replicated
- grad_norm1_bias: float32 [1024], replicated
- grad_w_qkv: float32 [1024, 3, 1024], P(('path', 'dp'), None, 'mp')
- grad_qv_bias: float32 [2, 1024], P(None, 'mp')
- grad_w_out: float32 [1024, 1024], P('mp', ('path', 'dp'))
- grad_out_bias: float32 [1024], replicated
- grad_norm2_gain: float32 [1024], replicated
- grad_norm2_bias: float32 [1024], replicated
- grad_w_fc1: float32 [1024, 4096], P(('path', 'dp'), 'mp')
- grad_fc1_bias: float32 [4096], P('mp')
- grad_w_fc2: float32 [4096, 1024], P('mp', ('path', 'dp'))
- grad_fc2_bias: float32 [1024], replicated
- grad_w_adapt: float32 [1536, 1024], P('mp', ('path', 'dp'))
- grad_gate_param: float32 [1024], replicated
- grad_dw_kernel: float32 [49, 1536], P(None, 'mp')
- grad_dw_bias: float32 [1536], P('mp')
- grad_cnorm_gain: float32 [1536], P('mp')
- grad_cnorm_bias: float32 [1536], P('mp')
- grad_w_pw1: float32 [1536, 6144], P(('path', 'dp'), 'mp')
- grad_pw1_bias: float32 [6144], P('mp')
- grad_w_pw2: float32 [6144, 1536], P('mp', ('path', 'dp'))
- grad_pw2_bias: float32 [1536], P('mp')
- grad_layer_scale: float32 [1536], P('mp')
The draws below stay inside these ranges and needn't reach their ends.
Inputs may be any that keep to these rules, and one draw needn't show every extreme that they name: `valid_rows`: some image has all 24 rows valid in every draw.
All inputs are finite; a program needn't handle non-finite values. No bound on the sum of `valid_rows` on one device may be relied on, other than what follows from the above.
Results may differ from the reference program's by a relative error of at most 0.02.
Values may be sent and summed in bfloat16 or wider, within the bound.
No kernel may reach another device: no remote copies, remote signals or barrier semaphores. Data moves between devices by JAX's collectives and lax.ppermute only.
A program may use at most 448 MiB of HBM per device.

```python
import math
import jax
import jax.numpy as jnp
import numpy as np
from jax import lax

D = 1024
HEADS = 16
HEAD_DIM = 64
FF = 4096
C = 1536
FF_C = 6144
GRID_LO = 24
GRID_HI = 32
IMAGES = 8
N_MP = 4


def levels(key, dims, shards, low, largest):
    def one(position, shards_of):
        draws = jax.random.uniform(jax.random.fold_in(jax.random.fold_in(key, 6), position), (shards_of,), jnp.float32, low / len(shards), largest / len(shards))
        return jnp.repeat(jnp.exp(draws), dims[position] // shards_of).reshape((-1,) + (1,) * (len(dims) - position - 1))

    level = one(*shards[0])
    for cut in shards[1:]:
        level = level * one(*cut)
    return level


def profile(number_of, total, bound, skew):
    portions = [(1 << 20) // math.isqrt(standing ** skew) + 1 for standing in range(2, number_of + 1)]
    surplus, given = total - bound - (number_of - 1), [1] * (number_of - 1)
    while surplus > 0:
        candidates = [i for i in range(number_of - 1) if given[i] < bound]
        whole, left = sum([portions[i] for i in candidates]), surplus
        for i in candidates:
            more = min(bound - given[i], max(1, left * portions[i] // whole), surplus)
            given[i] = given[i] + more
            surplus = surplus - more
    return np.array([bound] + given)


def uneven(key, count, total, bound, skew):
    if count == 2:
        one = jax.random.randint(key, (), max(1, total - bound), min(bound, total - 1) + 1)
        return jnp.stack([one, total - one])
    sizes = jnp.asarray(profile(count, total, bound, skew), jnp.int32)
    twos = (count - 1) // 2
    source_of, sink = sizes[1:1 + 2 * twos:2], sizes[2:2 + 2 * twos:2]
    room = jnp.minimum(source_of - 1, bound - sink)
    passed = jax.random.randint(jax.random.fold_in(key, 1), (twos,), 0, 1 << 20) % (room + 1)
    sizes = sizes.at[1:1 + 2 * twos:2].set(source_of - passed).at[2:2 + 2 * twos:2].set(sink + passed)
    return sizes[jax.random.permutation(jax.random.fold_in(key, 2), count)]


def bell_draw(rng, extent, scale, reach, pieces=(), held_as=jnp.bfloat16):
    entries = jax.random.normal(rng, extent, jnp.float32) * scale
    if len(pieces) > 0:
        entries = levels(rng, extent, pieces, -0.22, 0.18) * entries
    return jnp.clip(entries, min=-reach, max=reach).astype(held_as)


def setup_inputs(seed: int = 0) -> dict:
    splits = jax.random.split(jax.random.key(seed), 28)
    return {
        "tokens": bell_draw(splits[0], (IMAGES, GRID_LO * GRID_LO, D), 1.0, 6.0, ((0, 4),)),
        "hires": bell_draw(splits[1], (IMAGES, GRID_HI, GRID_HI, C), 1.0, 6.0, ((0, 4), (3, 4))),
        "valid_rows": uneven(splits[2], IMAGES, GRID_LO * 3 // 4 * IMAGES, GRID_LO, 2).astype(jnp.int32),
        "cotangent": bell_draw(splits[3], (IMAGES, GRID_LO * GRID_LO, D), 1.0, 6.0, ((0, 4),)),
        "attention_norm_gain": jnp.clip(1.0 + 0.18 * jax.random.normal(splits[4], (D,), jnp.float32), 0.1, 1.9),
        "attention_norm_bias": bell_draw(splits[5], (D,), 0.3, 1.5, (), jnp.float32),
        "w_qkv": bell_draw(splits[6], (D, 3, D), D ** -0.5, 0.1875, ((2, 4),)),
        "qv_bias": bell_draw(splits[7], (2, D), 0.3, 1.5, ((1, 4),), jnp.float32),
        "w_out": bell_draw(splits[8], (D, D), HEAD_DIM ** -0.5, 0.75, ((0, 4),)),
        "out_bias": bell_draw(splits[9], (D,), 0.3, 1.5, (), jnp.float32),
        "mlp_norm_gain": jnp.clip(1.0 + 0.18 * jax.random.normal(splits[10], (D,), jnp.float32), 0.1, 1.9),
        "mlp_norm_bias": bell_draw(splits[11], (D,), 0.3, 1.5, (), jnp.float32),
        "w_fc1": bell_draw(splits[12], (D, FF), D ** -0.5, 0.1875, ((1, 4),)),
        "fc1_bias": bell_draw(splits[13], (FF,), 0.3, 1.5, ((0, 4),), jnp.float32),
        "down_weight": bell_draw(splits[14], (FF, D), FF ** -0.5, 0.09375, ((0, 4),)),
        "fc2_bias": bell_draw(splits[15], (D,), 0.3, 1.5, (), jnp.float32),
        "w_adapt": bell_draw(splits[16], (C, D), (C // 4) ** -0.5, 0.3125, ((0, 4),)),
        "gate_param": jnp.clip(jax.random.uniform(splits[17], (D,), jnp.float32, -2.0, 2.0), -2.0, 2.0),
        "dw_kernel": bell_draw(splits[18], (49, C), 49 ** -0.5, 0.875, ((1, 4),), jnp.float32),
        "dw_bias": bell_draw(splits[19], (C,), 0.3, 1.5, ((0, 4),), jnp.float32),
        "channel_norm_gain": jnp.clip(1.0 + 0.18 * jax.random.normal(splits[20], (C,), jnp.float32), 0.1, 1.9),
        "channel_norm_bias": bell_draw(splits[21], (C,), 0.3, 1.5, (), jnp.float32),
        "w_pw1": bell_draw(splits[22], (C, FF_C), C ** -0.5, 0.15625, ((1, 4),)),
        "pw1_bias": bell_draw(splits[23], (FF_C,), 0.3, 1.5, ((0, 4),), jnp.float32),
        "w_pw2": bell_draw(splits[24], (FF_C, C), FF_C ** -0.5, 0.078125, ((0, 4),)),
        "pw2_bias": bell_draw(splits[25], (C,), 0.3, 1.5, ((0, 4),), jnp.float32),
        "layer_scale": jnp.clip(jnp.exp(math.log(2.0) - 1.89712 * jax.random.uniform(splits[26], (C,), jnp.float32) ** levels(splits[26], (C,), ((0, 4),), -0.2, 0.2)), 0.3, 2.0),
    }


@jax.custom_vjp
def low(v):
    return lax.optimization_barrier(v.astype(jnp.bfloat16)).astype(jnp.float32)

@jax.custom_vjp
def low_back(v):
    return v

def low_keep(v):
    return (low(v), None)

def low_pass(kept, grad):
    return (grad,)

def back_keep(v):
    return (v, None)

def back_low(kept, grad):
    return (low(grad),)
low.defvjp(low_keep, low_pass)
low_back.defvjp(back_keep, back_low)
highest = lax.Precision.HIGHEST

def matmul(left, right):
    return jnp.dot(left, right, precision=highest, preferred_element_type=jnp.float32)

def gelu(tensor):
    return 0.5 * tensor * (1.0 + jnp.tanh(0.7978845608028654 * (tensor + 0.044715 * tensor * tensor * tensor)))

def layer_norm(tensor, gain, shift, eps):
    centred = tensor - lax.optimization_barrier(jnp.mean(tensor, axis=-1, keepdims=True))
    return centred * lax.rsqrt(lax.optimization_barrier(jnp.mean(centred * centred, axis=-1, keepdims=True)) + eps) * gain + shift

def pool_weights():
    ratio = GRID_HI / GRID_LO
    target = jnp.arange(GRID_LO, dtype=jnp.float32)[:, None]
    source = jnp.arange(GRID_HI, dtype=jnp.float32)[None, :]
    lower = jnp.maximum(source, target * ratio)
    upper = jnp.minimum(source + 1.0, (target + 1.0) * ratio)
    return jnp.maximum(upper - lower, 0.0) / ratio

def depthwise(field, kernel, bias):
    padded = jnp.pad(field, ((3, 3), (3, 3), (0, 0)))
    result = jnp.zeros_like(field) + bias
    for offset_row in range(7):
        for offset_col in range(7):
            result = result + padded[offset_row:offset_row + GRID_HI, offset_col:offset_col + GRID_HI, :] * kernel[offset_row * 7 + offset_col]
    return result

def image_forward(params, item):
    attention_norm_gain, attention_norm_bias, w_qkv, qv_bias, w_out, out_bias, mlp_norm_gain, mlp_norm_bias, w_fc1, fc1_bias, down_weight, fc2_bias, w_adapt, gate_param, dw_kernel, dw_bias, channel_norm_gain, channel_norm_bias, w_pw1, pw1_bias, w_pw2, pw2_bias, layer_scale = params
    tokens, hires, rows = item
    lo_mask = (jnp.arange(GRID_LO) < rows).astype(jnp.float32)
    hi_rows = (rows * GRID_HI + GRID_LO - 1) // GRID_LO
    hi_mask = (jnp.arange(GRID_HI) < hi_rows).astype(jnp.float32)
    masked = hires * hi_mask[:, None, None]
    spatial = low(depthwise(masked, dw_kernel, dw_bias))
    conv_normed = low(layer_norm(spatial, channel_norm_gain, channel_norm_bias, 1e-06)).reshape(GRID_HI * GRID_HI, C)
    conv_inner = low_back(matmul(conv_normed, w_pw1) + pw1_bias)
    conv_active = low(gelu(conv_inner))
    conv_branch = low_back(matmul(conv_active, w_pw2) + pw2_bias).reshape(GRID_HI, GRID_HI, C)
    refined = masked + layer_scale * conv_branch
    area = pool_weights()
    pooled = jnp.einsum('ia,abc->ibc', area, refined, precision=highest)
    pooled = jnp.einsum('jb,ibc->ijc', area, pooled, precision=highest) * lo_mask[:, None, None]
    pooled = low(low_back(pooled)).reshape(GRID_LO * GRID_LO, C)
    key_valid = jnp.repeat(lo_mask, GRID_LO) > 0.5
    first_normalized = low(layer_norm(tokens, attention_norm_gain, attention_norm_bias, 1e-05))
    mixed = matmul(first_normalized, w_qkv.reshape(D, 3 * D)).reshape(-1, 3, D)
    query_matrix = low(low_back(mixed[:, 0] + qv_bias[0])).reshape(-1, HEADS, HEAD_DIM)
    keys = low(low_back(mixed[:, 1])).reshape(-1, HEADS, HEAD_DIM)
    values = low(low_back(mixed[:, 2] + qv_bias[1])).reshape(-1, HEADS, HEAD_DIM)
    scores = low_back(jnp.einsum('thd,shd->hts', query_matrix, keys, precision=highest) * HEAD_DIM ** (-0.5))
    scores = jnp.where(key_valid[None, None, :], scores, -1e+30)
    row_max = lax.optimization_barrier(jnp.max(scores, axis=-1, keepdims=True))
    exp_scores = jnp.exp(scores - row_max)
    probs = low(exp_scores / lax.optimization_barrier(jnp.sum(exp_scores, axis=-1, keepdims=True)))
    attended_rows = jnp.einsum('hts,shd->thd', probs, values, precision=highest).reshape(-1, D)
    attended_rows = low(low_back(attended_rows))
    parts = jnp.einsum('tgk,gkd->gtd', attended_rows.reshape(-1, N_MP, D // N_MP), w_out.reshape(N_MP, D // N_MP, D), precision=highest)
    attn_out = low_back(lax.optimization_barrier(jnp.sum(low(parts), axis=0)) + out_bias)
    first_hidden = tokens + attn_out
    second_normalized = low(layer_norm(first_hidden, mlp_norm_gain, mlp_norm_bias, 1e-05))
    dense_hidden = low_back(matmul(second_normalized, w_fc1) + fc1_bias)
    dense_activated = low(gelu(dense_hidden))
    gate_value = jnp.tanh(gate_param)
    feedforward_result = jnp.einsum('tgk,gkd->gtd', dense_activated.reshape(-1, N_MP, FF // N_MP), down_weight.reshape(N_MP, FF // N_MP, D), precision=highest)
    adapted = low_back(jnp.einsum('tgk,gkd->gtd', pooled.reshape(-1, N_MP, C // N_MP), w_adapt.reshape(N_MP, C // N_MP, D), precision=highest))
    branch_sum = lax.optimization_barrier(jnp.sum(low(feedforward_result + gate_value * adapted), axis=0))
    return first_hidden + branch_sum + fc2_bias

def reference(tokens, hires, valid_rows, cotangent, attention_norm_gain, attention_norm_bias, w_qkv, qv_bias, w_out, out_bias, mlp_norm_gain, mlp_norm_bias, w_fc1, fc1_bias, down_weight, fc2_bias, w_adapt, gate_param, dw_kernel, dw_bias, channel_norm_gain, channel_norm_bias, w_pw1, pw1_bias, w_pw2, pw2_bias, layer_scale):
    listed = (attention_norm_gain, attention_norm_bias, w_qkv, qv_bias, w_out, out_bias, mlp_norm_gain, mlp_norm_bias, w_fc1, fc1_bias, down_weight, fc2_bias, w_adapt, gate_param, dw_kernel, dw_bias, channel_norm_gain, channel_norm_bias, w_pw1, pw1_bias, w_pw2, pw2_bias, layer_scale)
    params = tuple((param.astype(jnp.float32) for param in listed))

    def whole(token_in, hires_in, weights):

        def single(item):
            return image_forward(weights, item)
        return lax.map(jax.checkpoint(single), (token_in, hires_in, valid_rows))
    result, pullback = jax.vjp(whole, tokens.astype(jnp.float32), hires.astype(jnp.float32), params)
    token_grad, hires_grad, weight_grads = pullback(cotangent.astype(jnp.float32))
    g_norm1_gain, g_norm1_bias, g_qkv, g_qv_bias, g_out, g_out_bias, g_norm2_gain, g_norm2_bias, g_fc1, g_fc1_bias, g_fc2, g_fc2_bias, g_adapt, g_gate, g_kernel, g_dw_bias, g_cnorm_gain, g_cnorm_bias, g_pw1, g_pw1_bias, g_pw2, g_pw2_bias, g_scale = weight_grads
    return (result.astype(jnp.bfloat16), token_grad.astype(jnp.bfloat16), hires_grad.astype(jnp.bfloat16), g_norm1_gain, g_norm1_bias, g_qkv, g_qv_bias, g_out, g_out_bias, g_norm2_gain, g_norm2_bias, g_fc1, g_fc1_bias, g_fc2, g_fc2_bias, g_adapt, g_gate, g_kernel, g_dw_bias, g_cnorm_gain, g_cnorm_bias, g_pw1, g_pw1_bias, g_pw2, g_pw2_bias, g_scale)
```

```python
import jax
import jax.numpy as jnp
import numpy as np
from jax import lax
from jax.sharding import PartitionSpec as P

HEAD_DIM = 64
GRID_LO = 24
GRID_HI = 32
TOKENS = GRID_LO * GRID_LO
CELLS = GRID_HI * GRID_HI

norm_epsilon = 1e-05
channel_epsilon = 1e-06
F32 = jnp.float32
BF16 = jnp.bfloat16


def gelu(v):
    return 0.5 * v * (1.0 + jnp.tanh(0.7978845608028654 * (v + 0.044715 * v * v * v)))


def gelu_pair(v):
    c = 0.7978845608028654
    square = v * v
    t = jnp.tanh(c * v * (1.0 + 0.044715 * square))
    half = 0.5 * (1.0 + t)
    return v * half, half + 0.5 * v * (1.0 - t * t) * c * (1.0 + 3 * 0.044715 * square)


def pool_rows():
    ratio = GRID_HI / GRID_LO
    target = np.arange(GRID_LO, dtype=np.float64)[:, None]
    source = np.arange(GRID_HI, dtype=np.float64)[None, :]
    lower = np.maximum(source, target * ratio)
    upper = np.minimum(source + 1.0, (target + 1.0) * ratio)
    return np.round(np.maximum(upper - lower, 0.0) / ratio * 4) / 4


def pool_matrix():
    side = pool_rows()
    return jnp.asarray(np.kron(side, side), BF16)


def dot(a, b):
    return jnp.dot(a, b, preferred_element_type=F32)


def dot_nt(a, b):
    return lax.dot_general(a, b, (((1,), (1,)), ((), ())), preferred_element_type=F32)


def dot_tn(a, b):
    return lax.dot_general(a, b, (((0,), (0,)), ((), ())), preferred_element_type=F32)


def standardize(v, eps):
    centred = v - jnp.mean(v, axis=-1, keepdims=True)
    inv = lax.rsqrt(jnp.mean(centred * centred, axis=-1, keepdims=True) + eps)
    return centred * inv, inv


def depthwise(field, kernel, bias):
    extent = field.shape[0]
    padded = jnp.pad(field, ((3, 3), (3, 3), (0, 0)))
    result = jnp.zeros_like(field) + bias
    for r in range(7):
        for s in range(7):
            result = result + padded[r : r + extent, s : s + extent, :] * kernel[r * 7 + s]
    return result


def swap(value, axis, apart):
    n = lax.axis_size(axis)
    return lax.ppermute(value, axis, [(i, i ^ apart) for i in range(n)])


def pick(value, axis, index):
    return lax.dynamic_index_in_dim(value, index, axis, keepdims=False)


def halve(value, dim, axis, apart, bit):
    received = swap(pick(value, dim, 1 - bit), axis, apart)
    return pick(value, dim, bit).astype(F32) + received.astype(F32)


def sum_blocks(value, last_dtype=F32):
    n_path, n_dp = lax.axis_size("path"), lax.axis_size("dp")
    me_path, me_dp = lax.axis_index("path"), lax.axis_index("dp")
    rest = value.shape[1:]
    value = value.astype(BF16)
    size = n_dp
    bit = 0
    while size > 1:
        size //= 2
        value = halve(
            value.reshape((n_path, size, 2) + rest), 2, "dp", 1 << bit, (me_dp >> bit) & 1
        )
        if size > 1 or n_path > 1:
            value = value.astype(BF16)
        bit += 1
    if n_path > 1:
        value = value.reshape((n_path,) + rest)
        value = halve(value, 0, "path", 1, me_path)
    return value.reshape(rest)


def body(
    tokens,
    hires,
    valid_rows,
    cotangent,
    attention_norm_gain,
    attention_norm_bias,
    w_qkv,
    qv_bias,
    w_out,
    out_bias,
    mlp_norm_gain,
    mlp_norm_bias,
    w_fc1,
    fc1_bias,
    down_weight,
    fc2_bias,
    w_adapt,
    gate_param,
    dw_kernel,
    dw_bias,
    channel_norm_gain,
    channel_norm_bias,
    w_pw1,
    pw1_bias,
    w_pw2,
    pw2_bias,
    layer_scale,
):
    path = lax.axis_index("path")
    n_path = lax.axis_size("path")
    mp = lax.axis_index("mp")
    n_mp = lax.axis_size("mp")
    groups = n_path * lax.axis_size("dp")
    assert tokens.shape[0] == n_path == 2
    width = tokens.shape[2]
    heads_width = w_qkv.shape[2]
    head_count = heads_width // HEAD_DIM
    channels = hires.shape[3]
    all_channels = w_pw1.shape[0]
    part_rows = TOKENS // n_mp
    score_scale = HEAD_DIM ** (-0.5)
    pool = pool_matrix()

    valid = pick(valid_rows, 0, path)
    hi_valid = (valid * GRID_HI + GRID_LO - 1) // GRID_LO
    lo_mask = (jnp.arange(TOKENS) < valid * GRID_LO).astype(F32)[:, None]
    hi_mask = (jnp.arange(GRID_HI) < hi_valid).astype(F32)[:, None, None]
    key_valid = jnp.arange(TOKENS) < valid * GRID_LO

    x_rows = pick(tokens, 0, path)
    dy = pick(cotangent, 0, path)
    field = pick(hires, 0, path)
    gate = jnp.tanh(gate_param)

    d_adapted = (gate * dy.astype(F32)).astype(BF16)
    d_pooled = dot_nt(d_adapted, w_adapt).astype(BF16).astype(F32) * lo_mask
    scaled_back = (d_pooled * layer_scale).astype(BF16)
    d_pooled = d_pooled.astype(BF16)

    masked = field.astype(F32) * hi_mask
    spatial = depthwise(masked, dw_kernel, dw_bias).astype(BF16).reshape(CELLS, channels)
    spatial_all = lax.all_gather(spatial, "mp", axis=0, tiled=False)
    scaled_back_all = lax.all_gather(scaled_back, "mp", axis=0, tiled=False)

    xhat1, inv1 = standardize(x_rows.astype(F32), norm_epsilon)
    normed1 = (xhat1 * attention_norm_gain + attention_norm_bias).astype(BF16)
    qkv_flat = w_qkv.reshape(width, 3 * heads_width)
    mixed = dot(normed1, qkv_flat)
    query = (mixed[:, :heads_width] + qv_bias[0]).astype(BF16)
    keys = mixed[:, heads_width : 2 * heads_width].astype(BF16)
    values = (mixed[:, 2 * heads_width :] + qv_bias[1]).astype(BF16)

    def split_heads(v):
        return v.reshape(TOKENS, head_count, HEAD_DIM)

    def scores_of():
        raw = jnp.einsum(
            "thd,shd->hts", split_heads(query), split_heads(keys), preferred_element_type=F32
        )
        return jnp.where(key_valid[None, None, :], raw * score_scale, -1e30)

    scores = scores_of()
    row_max = jnp.max(scores, axis=-1, keepdims=True)
    exp_scores = jnp.exp(scores - row_max)
    exp_total = jnp.sum(exp_scores, axis=-1, keepdims=True)
    probs = (exp_scores / exp_total).astype(BF16)
    log_total = row_max + jnp.log(exp_total)
    attended = (
        jnp.einsum("hts,shd->thd", probs, split_heads(values), preferred_element_type=F32)
        .reshape(TOKENS, heads_width)
        .astype(BF16)
    )
    attention_part = dot(attended, w_out)
    attn_sum = lax.psum(attention_part.astype(BF16), "mp").astype(F32)

    spatial_full = spatial_all.transpose(1, 0, 2).reshape(CELLS, all_channels).astype(F32)
    chat, cinv = standardize(spatial_full, channel_epsilon)
    conv_normed = (chat * channel_norm_gain + channel_norm_bias).astype(BF16)
    conv_active, conv_slope = gelu_pair(dot(conv_normed, w_pw1) + pw1_bias)
    conv_active = conv_active.astype(BF16)
    back_full = scaled_back_all.transpose(1, 0, 2).reshape(TOKENS, all_channels)
    pooled_active = dot(pool, conv_active).astype(BF16)
    w_pw2_blocks = w_pw2.reshape(-1, n_mp, channels)
    branch_part = jnp.einsum("rh,hgc->grc", pooled_active, w_pw2_blocks, preferred_element_type=F32)
    branch_pooled = lax.psum_scatter(
        branch_part.astype(BF16), "mp", scatter_dimension=0, tiled=False
    ).astype(F32)
    branch_pooled = branch_pooled + pw2_bias

    d_active_low = dot_nt(back_full, w_pw2).astype(BF16)
    d_active = dot_tn(pool, d_active_low)
    d_conv_inner = (conv_slope * d_active).astype(BF16)
    w_pw1_blocks = w_pw1.reshape(n_mp, channels, -1)
    d_normed_c = jnp.einsum("rh,gch->grc", d_conv_inner, w_pw1_blocks, preferred_element_type=F32)
    gain_blocks = channel_norm_gain.reshape(n_mp, 1, channels)
    weighted = d_normed_c * gain_blocks
    chat_blocks = (spatial_all.astype(F32) - jnp.mean(spatial_full, axis=-1)[None, :, None]) * cinv
    conv_stats = jnp.stack(
        [jnp.sum(weighted, axis=(0, 2)), jnp.sum(weighted * chat_blocks, axis=(0, 2))]
    )
    d_normed_mine = lax.psum_scatter(
        d_normed_c.astype(BF16), "mp", scatter_dimension=0, tiled=False
    ).astype(F32)
    conv_stats = lax.psum(conv_stats, "mp")

    g_pw1 = dot_tn(conv_normed, d_conv_inner)
    g_pw1_bias = jnp.sum(d_conv_inner.astype(F32), axis=0)
    g_pw2_t = dot_tn(back_full, pooled_active)
    g_pw2_bias = jnp.sum(scaled_back.astype(F32), axis=0)
    g_pw1_mine = sum_blocks(g_pw1.reshape(groups, -1, g_pw1.shape[1]))
    g_pw2_mine = sum_blocks(g_pw2_t.reshape(groups, -1, g_pw2_t.shape[1])).T

    hidden1 = x_rows.astype(F32) + attn_sum + out_bias
    xhat2, inv2 = standardize(hidden1, norm_epsilon)
    normed2 = (xhat2 * mlp_norm_gain + mlp_norm_bias).astype(BF16)
    fc_active, fc_slope = gelu_pair(dot(normed2, w_fc1) + fc1_bias)
    fc_active = fc_active.astype(BF16)
    d_fc_inner = (fc_slope * dot_nt(dy, down_weight)).astype(BF16)
    d_normed2_part = dot_nt(d_fc_inner, w_fc1).reshape(n_mp, part_rows, width)
    d_normed2 = lax.psum_scatter(
        d_normed2_part.astype(BF16), "mp", scatter_dimension=0, tiled=False
    ).astype(F32)
    xhat2_part = lax.dynamic_slice_in_dim(xhat2, mp * part_rows, part_rows, 0)
    inv2_part = lax.dynamic_slice_in_dim(inv2, mp * part_rows, part_rows, 0)
    dy_part = lax.dynamic_slice_in_dim(dy, mp * part_rows, part_rows, 0).astype(F32)
    dxhat2 = d_normed2 * mlp_norm_gain
    d_hidden_part = dy_part + inv2_part * (
        dxhat2
        - jnp.mean(dxhat2, axis=-1, keepdims=True)
        - xhat2_part * jnp.mean(dxhat2 * xhat2_part, axis=-1, keepdims=True)
    )
    d_attn_part = d_hidden_part.astype(BF16)
    d_attn = lax.all_gather(d_attn_part, "mp", axis=0, tiled=True)
    g_norm2_gain = jnp.sum(d_normed2 * xhat2_part, axis=0)
    g_norm2_bias = jnp.sum(d_normed2, axis=0)
    g_out_bias = jnp.sum(d_attn_part.astype(F32), axis=0)

    g_fc1_mine = sum_blocks(dot_tn(normed2, d_fc_inner).reshape(groups, -1, d_fc_inner.shape[1]))
    g_fc2_mine = sum_blocks(dot_tn(dy, fc_active).reshape(groups, -1, fc_active.shape[1])).T
    g_fc1_bias = jnp.sum(d_fc_inner.astype(F32), axis=0)

    field_low = (field.astype(F32) * hi_mask).astype(BF16).reshape(CELLS, channels)
    pooled = (lo_mask * (dot(pool, field_low) + layer_scale * branch_pooled)).astype(BF16)
    g_scale = jnp.sum(d_pooled.astype(F32) * branch_pooled, axis=0)
    adapted = dot(pooled, w_adapt)
    g_gate = (1.0 - gate * gate) * jnp.sum(dy.astype(F32) * adapted, axis=0)
    term = (dot(fc_active, down_weight) + gate * adapted).astype(BF16)
    term = term.reshape(TOKENS, n_mp, heads_width).transpose(1, 0, 2)
    branch_sum = lax.psum_scatter(term, "mp", scatter_dimension=0, tiled=False).astype(F32)
    g_adapt_mine = sum_blocks(dot_tn(d_adapted, pooled).reshape(groups, -1, channels)).T

    def my_features(v):
        return lax.dynamic_slice_in_dim(v, mp * heads_width, heads_width, v.ndim - 1)

    output_rows = (my_features(hidden1 + fc2_bias) + branch_sum).astype(BF16)
    g_fc2_bias = jnp.sum(my_features(dy).astype(F32), axis=0)

    d_att = dot_nt(d_attn, w_out).astype(BF16)
    probs32 = jnp.exp(scores_of() - log_total)
    d_probs = jnp.einsum(
        "thd,shd->hts", split_heads(d_att), split_heads(values), preferred_element_type=F32
    )
    delta = jnp.sum(probs32 * d_probs, axis=-1, keepdims=True)
    d_scores = (probs32 * (d_probs - delta)).astype(BF16)
    d_query = jnp.einsum("hts,shd->thd", d_scores, split_heads(keys), preferred_element_type=F32)
    d_keys = jnp.einsum("hts,thd->shd", d_scores, split_heads(query), preferred_element_type=F32)
    d_values = jnp.einsum(
        "hts,thd->shd", probs32.astype(BF16), split_heads(d_att), preferred_element_type=F32
    )
    d_mixed = jnp.concatenate(
        [
            (d_query * score_scale).astype(BF16).reshape(TOKENS, heads_width),
            (d_keys * score_scale).astype(BF16).reshape(TOKENS, heads_width),
            d_values.astype(BF16).reshape(TOKENS, heads_width),
        ],
        axis=1,
    )
    d_normed1_part = dot_nt(d_mixed, qkv_flat)
    weighted1 = d_normed1_part * attention_norm_gain
    stats1 = jnp.stack([jnp.sum(weighted1, axis=-1), jnp.sum(weighted1 * xhat1, axis=-1)])
    d_normed1 = lax.psum_scatter(
        d_normed1_part.astype(BF16).reshape(TOKENS, n_mp, heads_width).transpose(1, 0, 2),
        "mp",
        scatter_dimension=0,
        tiled=False,
    ).astype(F32)
    stats1 = lax.psum(stats1, "mp") / width
    xhat1_mine = my_features(xhat1)
    tokens_grad_rows = (
        my_features(d_attn).astype(F32)
        + inv1
        * (
            d_normed1 * my_features(attention_norm_gain)
            - stats1[0][:, None]
            - xhat1_mine * stats1[1][:, None]
        )
    ).astype(BF16)
    g_norm1_gain = jnp.sum(d_normed1 * xhat1_mine, axis=0)
    g_norm1_bias = jnp.sum(d_normed1, axis=0)
    d_mixed32 = d_mixed.astype(F32)
    g_qv_bias = jnp.stack(
        [
            jnp.sum(d_mixed32[:, :heads_width], axis=0),
            jnp.sum(d_mixed32[:, 2 * heads_width :], axis=0),
        ]
    )
    g_qkv_mine = sum_blocks(dot_tn(normed1, d_mixed).reshape(groups, -1, 3 * heads_width))
    g_qkv_mine = g_qkv_mine.reshape(-1, 3, heads_width)
    g_out_mine = sum_blocks(dot_tn(d_attn, attended).reshape(groups, -1, heads_width)).T

    chat_mine = pick(chat_blocks, 0, mp)
    my_gain = pick(channel_norm_gain.reshape(n_mp, channels), 0, mp)
    d_spatial = cinv * (
        d_normed_mine * my_gain
        - conv_stats[0][:, None] / all_channels
        - chat_mine * conv_stats[1][:, None] / all_channels
    )
    g_cnorm_gain = jnp.sum(d_normed_mine * chat_mine, axis=0)
    g_cnorm_bias = jnp.sum(d_normed_mine, axis=0)
    d_spatial = d_spatial.reshape(GRID_HI, GRID_HI, channels)
    _, conv_pull = jax.vjp(depthwise, masked, dw_kernel, dw_bias)
    d_masked, g_kernel, g_dw_bias = conv_pull(d_spatial)
    d_refined = dot_tn(pool, d_pooled).reshape(GRID_HI, GRID_HI, channels)
    d_field = ((d_masked + d_refined) * hi_mask).astype(BF16)

    def keep_half(rows):
        halves = rows.reshape((2, rows.shape[0] // 2) + rows.shape[1:])
        other = swap(pick(halves, 0, 1 - path), "path", 1)
        mine = pick(halves, 0, path)
        first = path == 0
        return jnp.stack([jnp.where(first, mine, other), jnp.where(first, other, mine)])

    output = keep_half(output_rows)
    tokens_grad = keep_half(tokens_grad_rows)
    hires_grad = keep_half(d_field)

    def placed(v):
        whole = jnp.zeros((n_mp, v.shape[0]), F32)
        return lax.dynamic_update_slice(whole, v[None], (mp, 0)).reshape(-1)

    wide = jnp.stack(
        [
            placed(g_norm1_gain),
            placed(g_norm1_bias),
            g_out_bias,
            g_norm2_gain,
            g_norm2_bias,
            placed(g_fc2_bias),
            g_gate,
        ]
    )
    wide = lax.psum(wide, ("path", "dp", "mp"))
    local_list = [
        g_qv_bias,
        g_fc1_bias,
        g_kernel,
        g_dw_bias,
        g_cnorm_gain,
        g_cnorm_bias,
        g_pw1_bias,
        g_pw2_bias,
        g_scale,
    ]
    local = lax.psum(tuple(local_list), ("path", "dp"))
    (
        g_qv_bias,
        g_fc1_bias,
        g_kernel,
        g_dw_bias,
        g_cnorm_gain,
        g_cnorm_bias,
        g_pw1_bias,
        g_pw2_bias,
        g_scale,
    ) = local
    return (
        output,
        tokens_grad,
        hires_grad,
        wide[0],
        wide[1],
        g_qkv_mine,
        g_qv_bias,
        g_out_mine,
        wide[2],
        wide[3],
        wide[4],
        g_fc1_mine,
        g_fc1_bias,
        g_fc2_mine,
        wide[5],
        g_adapt_mine,
        wide[6],
        g_kernel,
        g_dw_bias,
        g_cnorm_gain,
        g_cnorm_bias,
        g_pw1_mine,
        g_pw1_bias,
        g_pw2_mine,
        g_pw2_bias,
        g_scale,
    )


def solution(mesh):
    in_specs = (
        P("dp", None, None),
        P("dp", None, None, "mp"),
        P("dp"),
        P("dp", None, None),
        P(),
        P(),
        P(None, None, "mp"),
        P(None, "mp"),
        P("mp", None),
        P(),
        P(),
        P(),
        P(None, "mp"),
        P("mp"),
        P("mp", None),
        P(),
        P("mp", None),
        P(),
        P(None, "mp"),
        P("mp"),
        P(),
        P(),
        P(None, "mp"),
        P("mp"),
        P("mp", None),
        P("mp"),
        P("mp"),
    )
    out_specs = (
        P("dp", "path", "mp"),
        P("dp", "path", "mp"),
        P("dp", "path", None, "mp"),
        P(),
        P(),
        P(("path", "dp"), None, "mp"),
        P(None, "mp"),
        P("mp", ("path", "dp")),
        P(),
        P(),
        P(),
        P(("path", "dp"), "mp"),
        P("mp"),
        P("mp", ("path", "dp")),
        P(),
        P("mp", ("path", "dp")),
        P(),
        P(None, "mp"),
        P("mp"),
        P("mp"),
        P("mp"),
        P(("path", "dp"), "mp"),
        P("mp"),
        P("mp", ("path", "dp")),
        P("mp"),
        P("mp"),
    )
    return jax.shard_map(body, mesh=mesh, in_specs=in_specs, out_specs=out_specs, check_vma=False)
```

```python
import functools

import jax
import jax.numpy as jnp
import numpy as np
from jax import lax
from jax.experimental import pallas as pl
from jax.experimental.pallas import tpu as pltpu
from jax.sharding import PartitionSpec as P

HEAD_DIM = 64
GRID_LO = 24
GRID_HI = 32
TOKENS = GRID_LO * GRID_LO
CELLS = GRID_HI * GRID_HI
LANES = 128
STAT_ROWS = 16
CELL_BLOCK = 256
POOL_BLOCK = CELL_BLOCK * 9 // 16

norm_epsilon = 1e-05
channel_epsilon = 1e-06
F32 = jnp.float32
BF16 = jnp.bfloat16
VMEM_BYTES = 60 * 1024 * 1024
CHUNKS = 2


def gelu_pair(v):
    c = 0.7978845608028654
    square = v * v
    t = jnp.tanh(c * v * (1.0 + 0.044715 * square))
    half = 0.5 + 0.5 * t
    return v * half, half + (0.5 * c) * v * (1.0 - t * t) * (1.0 + 3 * 0.044715 * square)


def pool_rows(lo, hi):
    ratio = hi / lo
    target = np.arange(lo, dtype=np.float64)[:, None]
    source = np.arange(hi, dtype=np.float64)[None, :]
    lower = np.maximum(source, target * ratio)
    upper = np.minimum(source + 1.0, (target + 1.0) * ratio)
    return np.round(np.maximum(upper - lower, 0.0) / ratio * 4) / 4


def pool_block():
    rows = CELL_BLOCK // GRID_HI
    return jnp.asarray(np.kron(pool_rows(rows * 3 // 4, rows), pool_rows(GRID_LO, GRID_HI)), BF16)


def dot(a, b):
    return jnp.dot(a, b, preferred_element_type=F32)


def dot_nt(a, b):
    return lax.dot_general(a, b, (((1,), (1,)), ((), ())), preferred_element_type=F32)


def dot_tn(a, b):
    return lax.dot_general(a, b, (((0,), (0,)), ((), ())), preferred_element_type=F32)


def standardize(v, eps):
    centred = v - jnp.mean(v, axis=-1, keepdims=True)
    inv = lax.rsqrt(jnp.mean(centred * centred, axis=-1, keepdims=True) + eps)
    return centred * inv, inv


KERNEL_US = {
    "front": 8,
    "attention_forward": 10,
    "conv_mlp": 21,
    "vit_mlp": 15,
    "norm2_backward": 4,
    "attention_backward": 42,
    "norm1_backward": 3,
    "output_halves": 3,
    "pack": 3,
    "unpack": 3,
    "adapter": 7,
    "conv_backward": 21,
    "grad_fc": 8,
    "grad_pw": 8,
    "grad_qkv": 6,
    "grad_adapt": 5,
    "fold_fc": 2,
    "fold_pw": 2,
    "fold_qkv": 1,
    "fold_adapt": 3,
    "fold_fc_last": 1,
    "fold_pw_last": 5,
    "fold_qkv_last": 3,
    "fold_adapt_last": 3,
}
FLOPS_PER_US = 1.15e9


def call(
    kernel, name, grid, ins, outs, operands, scratch=(), after=(), prefetch=None
):
    lead = 0 if prefetch is None else 1
    count = lead + len(ins)

    def run(*refs):
        kernel(*refs[:count], *refs[count + len(after) :])

    in_specs = list(ins) + [pl.BlockSpec(memory_space=pl.ANY)] * len(after)
    return pl.pallas_call(
        run,
        grid_spec=pltpu.PrefetchScalarGridSpec(
            num_scalar_prefetch=lead,
            grid=grid,
            in_specs=in_specs,
            out_specs=[spec for spec, _ in outs],
            scratch_shapes=list(scratch),
        ),
        out_shape=[shape for _, shape in outs],
        compiler_params=pltpu.CompilerParams(
            dimension_semantics=("arbitrary",) * len(grid), vmem_limit_bytes=VMEM_BYTES
        ),
        name=name,
        cost_estimate=pl.CostEstimate(
            flops=int(KERNEL_US[name] * FLOPS_PER_US), bytes_accessed=1, transcendentals=0
        ),
    )(*(() if prefetch is None else (prefetch,)), *operands, *after)


SCALARS = pl.BlockSpec(memory_space=pltpu.SMEM)


def array(shape, dtype=BF16):
    return jax.ShapeDtypeStruct(shape, dtype)


def held(shape):
    return pl.BlockSpec(shape, lambda *_: (0,) * len(shape), pipeline_mode=pl.Buffered(1))


def whole(shape):
    return pl.BlockSpec(shape, lambda *_: (0,) * len(shape))


def rows_to_lanes(columns):
    rows = columns[0].shape[0]
    lane = lax.broadcasted_iota(jnp.int32, (rows, LANES), 1)
    packed = jnp.zeros((rows, LANES), F32)
    for i, column in enumerate(columns):
        packed = jnp.where(lane == i, column, packed)
    return packed.T


def stat_rows(columns, width):
    lanes = rows_to_lanes(columns)
    pieces = [
        lanes[i : i + 1, t * LANES : (t + 1) * LANES]
        for i in range(2)
        for t in range(lanes.shape[1] // LANES)
    ]
    pieces.append(jnp.zeros((STAT_ROWS - len(pieces), LANES), F32))
    stats = jnp.concatenate(pieces, axis=0).astype(BF16)
    if width % LANES:
        return jnp.concatenate([stats, jnp.zeros((STAT_ROWS, width - LANES), BF16)], axis=1)
    return jnp.concatenate([stats] * (width // LANES), axis=1)


def channel_block(channels):
    return LANES if channels % LANES == 0 else channels


def store_shifted(shifted, a, row):
    column = lax.broadcasted_iota(jnp.int32, row.shape, 0)
    for s in range(7):
        move = s - 3
        if move == 0:
            shifted[s, a] = row
        else:
            rolled = pltpu.roll(row, (-move) % GRID_HI, 0)
            inside = (column + move >= 0) & (column + move < GRID_HI)
            shifted[s, a] = jnp.where(inside, rolled, 0.0)


def correlate(shifted, a0, count, taps, start):
    sums = [start] * count
    for r_in in range(count + 6):
        for s in range(7):
            value = shifted[s, a0 + r_in]
            for o in range(count):
                r = r_in - o
                if 0 <= r < 7:
                    sums[o] = sums[o] + value * taps(r, s)
    return sums


def front_kernel(
    base, count, s_ref, field_ref, k_ref, bias_ref, pool_ref, dy_ref, gate_ref, wa_ref, scale_ref,
    send_ref, field_pooled_ref, d_pooled_ref, d_adapted_ref, sums_ref, shifted,
):
    hi_valid = s_ref[5]
    cb = field_ref.shape[2]

    @pl.when(pl.program_id(0) == 0)
    def _():
        d_adapted_ref[...] = (gate_ref[...] * dy_ref[...].astype(F32)).astype(BF16)

    @pl.loop(0, count + 6)
    def _(a):
        source = base + a - 3
        keep = (source >= 0) & (source < hi_valid)
        row = field_ref[jnp.clip(source, 0, GRID_HI - 1)].astype(F32)
        store_shifted(shifted, a, jnp.where(keep, row, 0.0))

    start = jnp.broadcast_to(bias_ref[...], (GRID_HI, cb))

    @pl.loop(0, count, step=4)
    def _(a0):
        sums = correlate(
            shifted, a0, 4, lambda r, s: k_ref[r * 7 + s : r * 7 + s + 1, :], start
        )
        for o in range(4):
            at = pl.multiple_of((a0 + o) * GRID_HI, GRID_HI)
            send_ref[pl.ds(at, GRID_HI), :] = sums[o].astype(BF16)

    block_rows = CELL_BLOCK // GRID_HI
    for i in range(count // block_rows):
        first = base + i * block_rows
        rows = field_ref[first : first + block_rows]
        row = lax.broadcasted_iota(jnp.int32, rows.shape, 0) + first
        rows = jnp.where(row < hi_valid, rows.astype(F32), 0.0).astype(BF16)
        field_pooled_ref[i * POOL_BLOCK : (i + 1) * POOL_BLOCK] = dot(
            pool_ref[...], rows.reshape(CELL_BLOCK, cb)
        )
    d_pooled = dot_nt(d_adapted_ref[...], wa_ref[...]).astype(BF16).astype(F32)
    row = lax.broadcasted_iota(jnp.int32, d_pooled.shape, 0) + base * GRID_HI * 9 // 16
    d_pooled = jnp.where(row < s_ref[0] * GRID_LO, d_pooled, 0.0)
    d_pooled_ref[...] = d_pooled.astype(BF16)
    scaled = (d_pooled * scale_ref[...]).astype(BF16)
    send_ref[count * GRID_HI :, :] = scaled
    sums_ref[...] = jnp.sum(scaled.astype(F32), axis=0, keepdims=True)


def front(hires, kernel, bias, cotangent, gate, w_adapt, layer_scale, scalars, base, count, after=()):
    channels = hires.shape[3]
    width = cotangent.shape[2]
    cb = channel_block(channels)
    cells = count * GRID_HI
    pooled_rows = cells * 9 // 16
    chunk = base // count

    def column(rows):
        return pl.BlockSpec((rows, cb), lambda j, s: (0, j))

    return call(
        functools.partial(front_kernel, base, count),
        "front",
        (channels // cb,),
        [
            pl.BlockSpec((None, GRID_HI, GRID_HI, cb), lambda j, s: (s[3], 0, 0, j)),
            column(49),
            column(1),
            held((POOL_BLOCK, CELL_BLOCK)),
            pl.BlockSpec((None, pooled_rows, width), lambda j, s: (s[3], chunk, 0)),
            held((1, width)),
            pl.BlockSpec((cb, width), lambda j, s: (j, 0)),
            column(1),
        ],
        [
            (column(cells + pooled_rows), array((cells + pooled_rows, channels))),
            (column(pooled_rows), array((pooled_rows, channels), F32)),
            (column(pooled_rows), array((pooled_rows, channels))),
            (whole((pooled_rows, width)), array((pooled_rows, width))),
            (column(1), array((1, channels), F32)),
        ],
        (hires, kernel, bias.reshape(1, -1), pool_block(), cotangent, gate.reshape(1, -1), w_adapt)
        + (layer_scale.reshape(1, -1),),
        [pltpu.VMEM((7, count + 6, GRID_HI, cb), F32)],
        after,
        prefetch=scalars,
    )


def softmax_rows(q, k, key_valid):
    scores = jnp.where(key_valid, dot_nt(q, k) * HEAD_DIM ** (-0.5), -1e30)
    e = jnp.exp(scores - jnp.max(scores, axis=-1, keepdims=True))
    return e * (1.0 / jnp.sum(e, axis=-1, keepdims=True))


def attention_kernel(
    s_ref, x_ref, gain_ref, shift_ref, wq_ref, wk_ref, wv_ref, bias_ref,
    normed_ref, q_ref, k_ref, v_ref, att_ref,
):
    @pl.when(pl.program_id(0) == 0)
    def _():
        xhat, _ = standardize(x_ref[...].astype(F32), norm_epsilon)
        normed_ref[...] = (xhat * gain_ref[...] + shift_ref[...]).astype(BF16)

    normed = normed_ref[...]
    q_ref[...] = (dot(normed, wq_ref[...]) + bias_ref[0:1]).astype(BF16)
    k_ref[...] = dot(normed, wk_ref[...]).astype(BF16)
    v_ref[...] = (dot(normed, wv_ref[...]) + bias_ref[1:2]).astype(BF16)
    key = lax.broadcasted_iota(jnp.int32, (1, TOKENS), 1)
    key_valid = key < s_ref[0] * GRID_LO
    for h in range(q_ref.shape[1] // HEAD_DIM):
        cut = slice(h * HEAD_DIM, (h + 1) * HEAD_DIM)
        probs = softmax_rows(q_ref[:, cut], k_ref[:, cut], key_valid)
        att_ref[:, cut] = dot(probs.astype(BF16), v_ref[:, cut]).astype(BF16)


def image(width):
    return pl.BlockSpec((None, TOKENS, width), lambda j, s: (s[3], 0, 0))


def attention_forward(tokens, gain, shift, w_flat, qv_bias, scalars, after=()):
    width = tokens.shape[2]
    heads_width = w_flat.shape[1] // 3
    blocks = heads_width // LANES
    column = (pl.BlockSpec((TOKENS, LANES), lambda j, s: (0, j)), array((TOKENS, heads_width)))

    def weight(t):
        return pl.BlockSpec((width, LANES), lambda j, s: (0, t * blocks + j))

    return call(
        attention_kernel,
        "attention_forward",
        (blocks,),
        [image(width), held((1, width)), held((1, width)), weight(0), weight(1), weight(2)]
        + [pl.BlockSpec((2, LANES), lambda j, s: (0, j))],
        [(whole((TOKENS, width)), array((TOKENS, width)))] + [column] * 4,
        (tokens, gain.reshape(1, -1), shift.reshape(1, -1)) + (w_flat,) * 3 + (qv_bias,),
        after=after,
        prefetch=scalars,
    )


def attention_back_kernel(n_mp, scalars_ref, *refs):
    pieces, refs = refs[:n_mp], refs[n_mp:]
    x_ref, gain_ref, w_out_ref, q_ref, k_ref, v_ref, wq_ref, wk_ref, wv_ref = refs[:9]
    d_attn_ref, dq_ref, dk_ref, dv_ref = refs[9:13]
    sends, total = refs[13 : 13 + n_mp], refs[13 + n_mp]
    step = pl.program_id(0)
    mp = scalars_ref[1]
    part = pieces[0].shape[0]

    @pl.when(step == 0)
    def _():
        for k in range(n_mp):
            at = pl.multiple_of((mp ^ k) * part, part)
            total[pl.ds(at, part), :] = pieces[k][...].astype(F32)
        d_attn_ref[...] = total[...].astype(BF16)

    d_att_all = dot_nt(d_attn_ref[...], w_out_ref[...]).astype(BF16)
    key = lax.broadcasted_iota(jnp.int32, (1, TOKENS), 1)
    key_valid = key < scalars_ref[0] * GRID_LO
    scale = HEAD_DIM ** (-0.5)
    for h in range(q_ref.shape[1] // HEAD_DIM):
        cut = slice(h * HEAD_DIM, (h + 1) * HEAD_DIM)
        q, k, v, d_att = q_ref[:, cut], k_ref[:, cut], v_ref[:, cut], d_att_all[:, cut]
        probs = softmax_rows(q, k, key_valid)
        d_probs = dot_nt(d_att, v)
        delta = jnp.sum(probs * d_probs, axis=-1, keepdims=True)
        d_scores = (probs * (d_probs - delta)).astype(BF16)
        dq_ref[:, cut] = (dot(d_scores, k) * scale).astype(BF16)
        dk_ref[:, cut] = (dot_tn(d_scores, q) * scale).astype(BF16)
        dv_ref[:, cut] = dot_tn(probs.astype(BF16), d_att).astype(BF16)
    share = dot_nt(dq_ref[...], wq_ref[...]) + dot_nt(dk_ref[...], wk_ref[...])
    share = share + dot_nt(dv_ref[...], wv_ref[...])

    @pl.when(step == 0)
    def _():
        total[...] = share

    @pl.when(step > 0)
    def _():
        total[...] += share

    @pl.when(step == pl.num_programs(0) - 1)
    def _():
        features = sends[0].shape[1]
        xhat, _ = standardize(x_ref[...].astype(F32), norm_epsilon)
        weighted = total[...] * gain_ref[...]
        ones = jnp.sum(weighted, axis=-1, keepdims=True)
        twos = jnp.sum(weighted * xhat, axis=-1, keepdims=True)
        pad = jnp.zeros((-TOKENS % LANES, 1), F32)
        stats = stat_rows([jnp.concatenate([ones, pad]), jnp.concatenate([twos, pad])], features)
        for k in range(n_mp):
            at = pl.multiple_of((mp ^ k) * features, features)
            sends[k][:TOKENS, :] = total[:, pl.ds(at, features)].astype(BF16)
            sends[k][TOKENS:, :] = stats


def attention_backward(
    n_mp, tokens, gain, d_attn_pieces, w_out, q, k, v, w_flat, scalars, after=()
):
    width = tokens.shape[2]
    heads_width = q.shape[1]
    blocks = heads_width // LANES
    column = pl.BlockSpec((TOKENS, LANES), lambda j, s: (0, j))

    def weight(t):
        return pl.BlockSpec((width, LANES), lambda j, s: (0, t * blocks + j))

    send_shape = (TOKENS + STAT_ROWS, width // n_mp)
    return call(
        functools.partial(attention_back_kernel, n_mp),
        "attention_backward",
        (blocks,),
        [held(d_attn_pieces[0].shape)] * n_mp
        + [image(width), held((1, width)), pl.BlockSpec((LANES, width), lambda j, s: (j, 0))]
        + [column, column, column, weight(0), weight(1), weight(2)],
        [(whole((TOKENS, width)), array((TOKENS, width)))]
        + [(column, array((TOKENS, heads_width)))] * 3
        + [(whole(send_shape), array(send_shape))] * n_mp,
        (*d_attn_pieces, tokens, gain.reshape(1, -1), w_out, q, k, v, w_flat, w_flat, w_flat),
        [pltpu.VMEM((TOKENS, width), F32)],
        after,
        prefetch=scalars,
    )


def conv_mlp_kernel(
    n_mp, cells, rows_ref, gain_ref, shift_ref, w1_hbm, b_ref, w2_hbm, pool_ref,
    normed_ref, inner_ref, pooled_ref, back_ref, send_ref, mean_ref, inv_ref, bias_ref,
    full, w1_ref, w2_ref, sems,
):
    channels = rows_ref.shape[2]
    cut = 256
    steps = w1_ref.shape[1] // cut
    cuts = [slice(j * cut, (j + 1) * cut) for j in range(steps)]
    loads = []
    for j, at in enumerate(cuts):
        loads.append(pltpu.make_async_copy(w1_hbm.at[:, at], w1_ref.at[:, at], sems.at[j]))
        loads.append(pltpu.make_async_copy(w2_hbm.at[at, :], w2_ref.at[at, :], sems.at[steps + j]))
    for load in loads:
        load.start()
    for g in range(n_mp):
        mine = slice(g * channels, (g + 1) * channels)
        full[:, mine] = rows_ref[g, :cells].astype(F32)
        back_ref[:, mine] = rows_ref[g, cells:]
    spatial = full[...]
    mean = jnp.mean(spatial, axis=-1, keepdims=True)
    centred = spatial - mean
    inv = lax.rsqrt(jnp.mean(centred * centred, axis=-1, keepdims=True) + channel_epsilon)
    xhat = centred * inv
    full[...] = xhat
    mean_ref[...] = jnp.broadcast_to(mean, mean_ref.shape)
    inv_ref[...] = jnp.broadcast_to(inv, inv_ref.shape)
    normed_ref[...] = (xhat * gain_ref[...] + shift_ref[...]).astype(BF16)
    for j, at in enumerate(cuts):
        loads[2 * j].wait()
        active, slope = gelu_pair(dot(normed_ref[...], w1_ref[:, at]) + b_ref[:, at])
        active = active.astype(BF16)
        loads[2 * j + 1].wait()
        d_active = dot_nt(back_ref[...], w2_ref[at, :]).astype(BF16)
        backs = []
        for i in range(cells // CELL_BLOCK):
            lo = slice(i * POOL_BLOCK, (i + 1) * POOL_BLOCK)
            hi = slice(i * CELL_BLOCK, (i + 1) * CELL_BLOCK)
            pooled_ref[lo, at] = dot(pool_ref[...], active[hi]).astype(BF16)
            backs.append(dot_tn(pool_ref[...], d_active[lo]))
        d_inner = (slope * jnp.concatenate(backs, axis=0)).astype(BF16)
        inner_ref[:, at] = d_inner
        bias_ref[:, at] = jnp.sum(d_inner.astype(F32), axis=0, keepdims=True)

    branch = dot(pooled_ref[...], w2_ref[...]).astype(BF16)
    d_normed = dot_nt(inner_ref[...], w1_ref[...])
    weighted = d_normed * gain_ref[...]
    ones = jnp.sum(weighted, axis=-1, keepdims=True)
    twos = jnp.sum(weighted * full[...], axis=-1, keepdims=True)
    stats = stat_rows([ones, twos], channels)
    for g in range(n_mp):
        mine = slice(g * channels, (g + 1) * channels)
        send_ref[g, :cells, :] = d_normed[:, mine].astype(BF16)
        send_ref[g, cells : cells + STAT_ROWS, :] = stats
        send_ref[g, cells + STAT_ROWS :, :] = branch[:, mine]


def conv_mlp(rows, gain, shift, w1, b, w2, after=()):
    n_mp, both, channels = rows.shape
    total, hidden = w1.shape
    cells = both * 16 // 25
    pooled = both - cells
    send_shape = (n_mp, both + STAT_ROWS, channels)
    anywhere = pl.BlockSpec(memory_space=pl.ANY)

    def out(shape, dtype=BF16):
        return (held(shape), array(shape, dtype))

    return call(
        functools.partial(conv_mlp_kernel, n_mp, cells),
        "conv_mlp",
        (1,),
        [held((n_mp, both, channels)), held((1, total)), held((1, total)), anywhere]
        + [held((1, hidden)), anywhere, held((POOL_BLOCK, CELL_BLOCK))],
        [
            out((cells, total)),
            out((cells, hidden)),
            out((pooled, hidden)),
            out((pooled, total)),
            out(send_shape),
            out((cells, LANES), F32),
            out((cells, LANES), F32),
            out((1, hidden), F32),
        ],
        (rows, gain.reshape(1, -1), shift.reshape(1, -1), w1, b.reshape(1, -1), w2, pool_block()),
        [
            pltpu.VMEM((cells, total), F32),
            pltpu.VMEM((total, hidden), BF16),
            pltpu.VMEM((hidden, total), BF16),
            pltpu.SemaphoreType.DMA((2 * (hidden // 256),)),
        ],
        after,
    )


def conv_back_kernel(chunks, total_channels, s_ref, *refs):
    (received, spatial, means, invs, d_pooled) = (
        refs[i * chunks : (i + 1) * chunks] for i in range(5)
    )
    refs = refs[5 * chunks :]
    field_ref, k_ref, gain_ref, pool_ref, out_ref, g_kernel_ref, sums_ref, shifted, moved = refs
    hi_valid = s_ref[5]
    cb = field_ref.shape[2]
    gain = gain_ref[...]
    zeros = jnp.zeros((GRID_HI, cb), F32)
    for a in (0, 1, 2, GRID_HI + 3, GRID_HI + 4, GRID_HI + 5):
        for s in range(7):
            shifted[s, a] = zeros
            moved[s, a] = zeros
    g_gain = jnp.zeros((1, cb), F32)
    g_shift = jnp.zeros((1, cb), F32)
    g_bias = jnp.zeros((1, cb), F32)
    block_rows = CELL_BLOCK // GRID_HI
    first = 0
    for c in range(chunks):
        cells = means[c].shape[0]
        per = cells // LANES
        stats = received[c][cells : cells + STAT_ROWS, :LANES].astype(F32)
        rows = [
            jnp.concatenate([stats[k * per + t : k * per + t + 1] for t in range(per)], axis=1)
            for k in range(2)
        ]
        rows.append(jnp.zeros((LANES - 2, cells), F32))
        columns = jnp.concatenate(rows, axis=0).T * (1.0 / total_channels)
        for i in range(cells // CELL_BLOCK):
            at = slice(i * CELL_BLOCK, (i + 1) * CELL_BLOCK)
            d_normed = received[c][at, :].astype(F32)
            column = columns[at]
            if cb > LANES:
                mean, inv = means[c][at, :1], invs[c][at, :1]
            else:
                mean, inv = means[c][at], invs[c][at]
            xhat = (spatial[c][at].astype(F32) - mean) * inv
            d_spatial = inv * (d_normed * gain - column[:, 0:1] - xhat * column[:, 1:2])
            g_gain = g_gain + jnp.sum(d_normed * xhat, axis=0, keepdims=True)
            g_shift = g_shift + jnp.sum(d_normed, axis=0, keepdims=True)
            g_bias = g_bias + jnp.sum(d_spatial, axis=0, keepdims=True)
            for a in range(block_rows):
                store_shifted(moved, first + a + 3, d_spatial[a * GRID_HI : (a + 1) * GRID_HI])
            first += block_rows

    @pl.loop(0, GRID_HI)
    def _(a):
        row = jnp.where(a < hi_valid, field_ref[a].astype(F32), 0.0)
        store_shifted(shifted, a + 3, row)

    g_kernel_ref[...] = jnp.zeros(g_kernel_ref.shape, F32)
    for s in range(7):
        def rows_of(i, sums):
            a0 = i * 2
            grads = [moved[3, a0 + o + 3] for o in range(2)]
            sums = list(sums)
            for r_in in range(8):
                value = shifted[s, a0 + r_in]
                for o in range(2):
                    r = r_in - o
                    if 0 <= r < 7:
                        product = value * grads[o]
                        sums[r] = sums[r] + jnp.sum(product.reshape(GRID_HI // 8, 8, cb), axis=0)
            return tuple(sums)

        sums = lax.fori_loop(0, GRID_HI // 2, rows_of, tuple(jnp.zeros((8, cb), F32) for _ in range(7)))
        for r in range(7):
            t = r * 7 + s
            g_kernel_ref[t : t + 1, :] = jnp.sum(sums[r], axis=0, keepdims=True)
    sums_ref[...] = jnp.concatenate([g_bias, g_gain, g_shift, jnp.zeros((5, cb), F32)], axis=0)

    for i in range(CELLS // CELL_BLOCK):
        each = CELLS // CELL_BLOCK // chunks
        lo = slice((i % each) * POOL_BLOCK, (i % each + 1) * POOL_BLOCK)
        refined = dot_tn(pool_ref[...], d_pooled[i // each][lo, :])
        shifted[0, i * block_rows : (i + 1) * block_rows] = refined.reshape(block_rows, GRID_HI, cb)

    @pl.loop(0, GRID_HI, step=4)
    def _(a0):
        sums = correlate(
            moved, a0, 4, lambda r, s: k_ref[48 - (r * 7 + s) : 49 - (r * 7 + s), :], jnp.zeros((GRID_HI, cb), F32)
        )
        for o in range(4):
            value = sums[o] + shifted[0, a0 + o]
            out_ref[a0 + o] = jnp.where(a0 + o < hi_valid, value, 0.0).astype(BF16)


def conv_backward(
    received, spatial, means, invs, d_pooled, hires, kernel, my_gain, total_channels, scalars, after=()
):
    chunks = len(received)
    channels = hires.shape[3]
    cb = channel_block(channels)
    cells = means[0].shape[0]

    def column(rows):
        return pl.BlockSpec((rows, cb), lambda j, s: (0, j))

    map_block = pl.BlockSpec((GRID_HI, GRID_HI, cb), lambda j, s: (0, 0, j))
    return call(
        functools.partial(conv_back_kernel, chunks, total_channels),
        "conv_backward",
        (channels // cb,),
        [column(cells + STAT_ROWS)] * chunks
        + [column(cells)] * chunks
        + [held((cells, LANES))] * (2 * chunks)
        + [column(d_pooled[0].shape[0])] * chunks
        + [
            pl.BlockSpec((None, GRID_HI, GRID_HI, cb), lambda j, s: (s[3], 0, 0, j)),
            column(49),
            column(1),
            held((POOL_BLOCK, CELL_BLOCK)),
        ],
        [
            (map_block, array((GRID_HI, GRID_HI, channels))),
            (column(49), array((49, channels), F32)),
            (column(8), array((8, channels), F32)),
        ],
        (*received, *spatial, *means, *invs, *d_pooled)
        + (hires, kernel, my_gain.reshape(1, -1), pool_block()),
        [pltpu.VMEM((7, GRID_HI + 6, GRID_HI, cb), F32)] * 2,
        after,
        prefetch=scalars,
    )


def vit_mlp_kernel(n_mp, scalars_ref, *refs):
    pieces, refs = refs[:n_mp], refs[n_mp:]
    x_ref, wo_hbm, ob_ref, gain_ref, shift_ref, w1_hbm, b1_ref, w2_hbm, dy_ref = refs[:9]
    hidden_ref, normed_ref, active_ref, inner_ref, bias_ref = refs[9:14]
    sends, refs = refs[14 : 14 + n_mp], refs[14 + n_mp :]
    d_normed, wo_ref, w1_ref, w2_ref, sems = refs
    step = pl.program_id(0)
    rows = x_ref.shape[0]
    cut = 256
    cuts = [slice(j * cut, (j + 1) * cut) for j in range(w1_ref.shape[1] // cut)]
    loads = [pltpu.make_async_copy(wo_hbm, wo_ref, sems.at[0])]
    for j, at in enumerate(cuts):
        loads.append(pltpu.make_async_copy(w1_hbm.at[:, at], w1_ref.at[:, at], sems.at[2 * j + 1]))
        loads.append(pltpu.make_async_copy(w2_hbm.at[at, :], w2_ref.at[at, :], sems.at[2 * j + 2]))

    @pl.when(step == 0)
    def _():
        for load in loads:
            load.start()
        loads[0].wait()

    hidden = x_ref[...].astype(F32) + ob_ref[...]
    for k in range(n_mp):
        hidden = hidden + dot(pieces[k][...], wo_ref[k])
    hidden_ref[...] = hidden
    xhat, _ = standardize(hidden, norm_epsilon)
    normed_ref[...] = (xhat * gain_ref[...] + shift_ref[...]).astype(BF16)

    @pl.when(step == 0)
    def _():
        for load in loads[1:]:
            load.wait()

    for j, at in enumerate(cuts):
        active, slope = gelu_pair(dot(normed_ref[...], w1_ref[:, at]) + b1_ref[:, at])
        active_ref[:, at] = active.astype(BF16)
        d_inner = (slope * dot_nt(dy_ref[...], w2_ref[at, :])).astype(BF16)
        inner_ref[:, at] = d_inner
        sums = jnp.sum(d_inner.astype(F32), axis=0, keepdims=True)

        @pl.when(step == 0)
        def _():
            bias_ref[:, at] = sums

        @pl.when(step > 0)
        def _():
            bias_ref[:, at] += sums

    d_normed[pl.ds(pl.multiple_of(step * rows, rows), rows), :] = dot_nt(inner_ref[...], w1_ref[...])

    @pl.when(step == pl.num_programs(0) - 1)
    def _():
        part = sends[0].shape[0]
        for k in range(n_mp):
            at = pl.multiple_of((scalars_ref[1] ^ k) * part, part)
            sends[k][...] = d_normed[pl.ds(at, part), :].astype(BF16)


def vit_mlp(
    tokens, attended_pieces, w_out_pieces, out_bias, gain, shift, w1, b1, w2, cotangent, scalars, after=()
):
    n_mp = len(attended_pieces)
    heads_width = attended_pieces[0].shape[1]
    width, hidden = w1.shape
    rows = TOKENS // 2
    image_rows = pl.BlockSpec((None, rows, width), lambda j, s: (s[3], j, 0))
    row = pl.BlockSpec((rows, width), lambda j, s: (j, 0))
    row_hidden = pl.BlockSpec((rows, hidden), lambda j, s: (j, 0))
    one = held((1, width))
    anywhere = pl.BlockSpec(memory_space=pl.ANY)
    send_shape = (TOKENS // n_mp, width)
    return call(
        functools.partial(vit_mlp_kernel, n_mp),
        "vit_mlp",
        (TOKENS // rows,),
        [pl.BlockSpec((rows, heads_width), lambda j, s: (j, 0))] * n_mp
        + [image_rows, anywhere, one, one, one, anywhere, held((1, hidden)), anywhere, image_rows],
        [
            (row, array((TOKENS, width), F32)),
            (row, array((TOKENS, width))),
            (row_hidden, array((TOKENS, hidden))),
            (row_hidden, array((TOKENS, hidden))),
            (whole((1, hidden)), array((1, hidden), F32)),
        ]
        + [(whole(send_shape), array(send_shape))] * n_mp,
        (*attended_pieces, tokens, w_out_pieces, out_bias.reshape(1, -1), gain.reshape(1, -1))
        + (shift.reshape(1, -1), w1, b1.reshape(1, -1), w2, cotangent),
        [
            pltpu.VMEM((TOKENS, width), F32),
            pltpu.VMEM((n_mp, heads_width, width), BF16),
            pltpu.VMEM((width, hidden), BF16),
            pltpu.VMEM((hidden, width), BF16),
            pltpu.SemaphoreType.DMA((1 + 2 * (hidden // 256),)),
        ],
        after,
        prefetch=scalars,
    )


def adapter_kernel(chunks, scalars_ref, *refs):
    received, d_pooled, fields = (refs[i * chunks : (i + 1) * chunks] for i in range(3))
    refs = refs[3 * chunks :]
    pb_ref, scale_ref, wa_ref, active_ref, w2_ref, gate_ref, dy_ref = refs[:7]
    pooled_ref, scale_sum_ref, gate_sum_ref = refs[7:10]
    sends, total = refs[10:-1], refs[-1]
    sums = jnp.zeros(scale_sum_ref.shape, F32)
    first = 0
    for c in range(chunks):
        count = fields[c].shape[0]
        branch = received[c][received[c].shape[0] - count :, :].astype(F32) + pb_ref[...]
        sums = sums + jnp.sum(d_pooled[c][...].astype(F32) * branch, axis=0, keepdims=True)
        value = fields[c][...] + scale_ref[...] * branch
        row = lax.broadcasted_iota(jnp.int32, value.shape, 0) + first
        value = jnp.where(row < scalars_ref[0] * GRID_LO, value, 0.0)
        pooled_ref[first : first + count, :] = value.astype(BF16)
        first += count
    scale_sum_ref[...] = sums
    gate = gate_ref[...]
    adapted = dot(pooled_ref[...], wa_ref[...])
    sums = jnp.sum(dy_ref[...].astype(F32) * adapted, axis=0, keepdims=True)
    gate_sum_ref[...] = (1.0 - gate * gate) * sums
    total[...] = dot(active_ref[...], w2_ref[...]) + gate * adapted
    features = sends[0].shape[1]
    for k, send in enumerate(sends):
        at = pl.multiple_of((scalars_ref[1] ^ k) * features, features)
        send[...] = total[:, pl.ds(at, features)].astype(BF16)


def adapter(
    n_mp, received, d_pooled, fields, pw2_bias, layer_scale, w_adapt, active, w2, gate, cotangent, scalars, after=()
):
    channels, width = w_adapt.shape
    hidden = w2.shape[0]
    send_shape = (TOKENS, width // n_mp)
    return call(
        functools.partial(adapter_kernel, len(fields)),
        "adapter",
        (1,),
        [held(v.shape) for v in (*received, *d_pooled, *fields)]
        + [held((1, channels)), held((1, channels)), held((channels, width))]
        + [held((TOKENS, hidden)), held((hidden, width)), held((1, width)), image(width)],
        [
            (held((TOKENS, channels)), array((TOKENS, channels))),
            (held((1, channels)), array((1, channels), F32)),
            (held((1, width)), array((1, width), F32)),
        ]
        + [(held(send_shape), array(send_shape))] * n_mp,
        (*received, *d_pooled, *fields, pw2_bias.reshape(1, -1), layer_scale.reshape(1, -1), w_adapt)
        + (active, w2, gate.reshape(1, -1), cotangent),
        [pltpu.VMEM((TOKENS, width), F32)],
        after,
        prefetch=scalars,
    )


def weight_grad_kernel(counts, block, scalars_ref, *refs):
    pairs = sum(counts)
    lefts, rights = refs[:pairs], refs[pairs : 2 * pairs]
    keep_ref, send_ref = refs[2 * pairs :]
    core = scalars_ref[2]
    at = 0
    used = sum(refs[pairs + sum(counts[:i])].shape[1] for i in range(len(counts)))
    if used < keep_ref.shape[2]:
        rest = jnp.zeros(keep_ref.shape[:2] + (keep_ref.shape[2] - used,), BF16)
        keep_ref[:, :, used:] = rest
        send_ref[:, :, used:] = rest
    first = 0
    for count in counts:
        total = dot_tn(lefts[first][...], rights[first][...])
        for i in range(first + 1, first + count):
            total = total + dot_tn(lefts[i][...], rights[i][...])
        first += count
        lanes = slice(at, at + total.shape[1])
        at += total.shape[1]
        total = total.astype(BF16)
        for q in range(keep_ref.shape[0]):
            halves = [total[(2 * q + h) * block : (2 * q + h + 1) * block] for h in range(2)]

            @pl.when(core == 0)
            def _():
                keep_ref[q, :, lanes] = halves[0]
                send_ref[q, :, lanes] = halves[1]

            @pl.when(core != 0)
            def _():
                keep_ref[q, :, lanes] = halves[1]
                send_ref[q, :, lanes] = halves[0]


def weight_grads(name, groups, grads, scalars, after=(), lanes=None):
    block = grads[0][0][0].shape[1] // groups
    pairs = [pair for grad in grads for pair in grad]
    quads = 1
    while (2 * block * quads) % LANES:
        quads += 1
    total = lanes or sum(grad[0][1].shape[1] for grad in grads)
    out = (
        pl.BlockSpec((quads, block, total), lambda j: (j, 0, 0)),
        array((groups // 2, block, total)),
    )
    return call(
        functools.partial(weight_grad_kernel, [len(grad) for grad in grads], block),
        name,
        (groups // 2 // quads,),
        [SCALARS]
        + [pl.BlockSpec((left.shape[0], 2 * block * quads), lambda j: (0, j)) for left, _ in pairs]
        + [held(right.shape) for _, right in pairs],
        [out, out],
        (scalars, *(left for left, _ in pairs), *(right for _, right in pairs)),
        after=after,
    )


def fold_kernel(_, *refs):
    count = len(refs) // 4
    for p in range(count):
        keep, got = refs[2 * p : 2 * p + 2]
        send, hold = refs[2 * (count + p) : 2 * (count + p) + 2]

        def total():
            return (keep[...].astype(F32) + got[...].astype(F32)).astype(BF16)

        @pl.when(pl.program_id(0) == 0)
        def _():
            send[...] = total().reshape(send.shape)

        @pl.when(pl.program_id(0) == 1)
        def _():
            hold[...] = total().reshape(hold.shape)


def fold(name, parts, scalars, after=()):
    ins, operands, outs = [], [], []
    for keep, got, dim, slot, lanes, block in parts:
        shape = list(keep.shape)
        shape[dim] //= 2
        shape[-1] = lanes
        assert keep.shape[dim] == 2

        def at(j, s, dim=dim, slot=slot, rank=len(shape), block=block):
            index = [0] * rank
            index[dim] = s[slot] ^ (1 - j)
            index[-1] = block
            return tuple(index)

        ins += [pl.BlockSpec(tuple(shape), at)] * 2
        operands += [keep, got]
        out = tuple(shape[:dim] + shape[dim + 1 :])
        outs += [(whole(out), array(out))] * 2
    return call(
        fold_kernel, name, (2,), ins, outs, operands, after=after, prefetch=scalars
    )


def norm2_back_kernel(n_mp, scalars_ref, *refs):
    got, refs = refs[:n_mp], refs[n_mp:]
    hidden_ref, dy_ref, gain_ref, d_attn_ref, sums_ref = refs
    d_normed = got[0][...].astype(F32)
    for value in got[1:]:
        d_normed = d_normed + value[...].astype(F32)
    xhat, inv = standardize(hidden_ref[...], norm_epsilon)
    dxhat = d_normed * gain_ref[...]
    d_hidden = dy_ref[...].astype(F32) + inv * (
        dxhat
        - jnp.mean(dxhat, axis=-1, keepdims=True)
        - xhat * jnp.mean(dxhat * xhat, axis=-1, keepdims=True)
    )
    d_attn = d_hidden.astype(BF16)
    d_attn_ref[...] = d_attn
    sums_ref[0:1, :] = jnp.sum(d_attn.astype(F32), axis=0, keepdims=True)
    sums_ref[1:2, :] = jnp.sum(d_normed * xhat, axis=0, keepdims=True)
    sums_ref[2:3, :] = jnp.sum(d_normed, axis=0, keepdims=True)
    sums_ref[3:, :] = jnp.zeros((5, sums_ref.shape[1]), F32)


def norm2_backward(got, hidden, cotangent, gain, scalars, after=()):
    n_mp = len(got)
    rows, width = got[0].shape
    mine = pl.BlockSpec((None, rows, width), lambda j, s: (s[1], 0, 0))
    image_rows = pl.BlockSpec((None, None, rows, width), lambda j, s: (s[3], s[1], 0, 0))
    return call(
        functools.partial(norm2_back_kernel, n_mp),
        "norm2_backward",
        (1,),
        [held((rows, width))] * n_mp + [mine, image_rows, held((1, width))],
        [
            (held((rows, width)), array((rows, width))),
            (held((8, width)), array((8, width), F32)),
        ],
        (*got, hidden.reshape(n_mp, rows, width), cotangent.reshape(-1, n_mp, rows, width))
        + (gain.reshape(1, -1),),
        after=after,
        prefetch=scalars,
    )


def norm1_back_kernel(n_mp, scalars_ref, *refs):
    got, refs = refs[:n_mp], refs[n_mp:]
    x_ref, mine_ref, d_attn_ref, gain_ref, dy_ref, keep_ref, send_ref, sums_ref, total = refs
    width = x_ref.shape[1]
    value = got[0][...].astype(F32)
    for piece in got[1:]:
        value = value + piece[...].astype(F32)
    d_normed, stats = value[:TOKENS], value[TOKENS:, :LANES]
    count = -(-TOKENS // LANES)
    rows = [
        jnp.concatenate([stats[k * count + t : k * count + t + 1] for t in range(count)], axis=1)
        for k in range(2)
    ]
    rows.append(jnp.zeros((LANES - 2, count * LANES), F32))
    columns = jnp.concatenate(rows, axis=0).T[:TOKENS] * (1.0 / width)
    x = x_ref[...].astype(F32)
    mean = jnp.mean(x, axis=-1, keepdims=True)
    inv = lax.rsqrt(jnp.mean((x - mean) * (x - mean), axis=-1, keepdims=True) + norm_epsilon)
    xhat = (mine_ref[...].astype(F32) - mean) * inv
    total[...] = d_attn_ref[...].astype(F32) + inv * (
        d_normed * gain_ref[...] - columns[:, 0:1] - xhat * columns[:, 1:2]
    )
    half = TOKENS // 2
    path = scalars_ref[3]
    keep_ref[...] = total[pl.ds(pl.multiple_of(path * half, half), half), :].astype(BF16)
    send_ref[...] = total[pl.ds(pl.multiple_of((1 - path) * half, half), half), :].astype(BF16)
    sums_ref[0:1, :] = jnp.sum(d_normed * xhat, axis=0, keepdims=True)
    sums_ref[1:2, :] = jnp.sum(d_normed, axis=0, keepdims=True)
    sums_ref[2:3, :] = jnp.sum(dy_ref[...].astype(F32), axis=0, keepdims=True)
    sums_ref[3:, :] = jnp.zeros((5, sums_ref.shape[1]), F32)


def norm1_backward(got, tokens, d_attn, gain, cotangent, scalars, after=()):
    n_mp = len(got)
    rows, features = got[0].shape
    width = tokens.shape[2]
    mine = pl.BlockSpec((TOKENS, features), lambda j, s: (0, s[1]))
    mine_of = pl.BlockSpec((None, TOKENS, features), lambda j, s: (s[3], 0, s[1]))
    half = (held((TOKENS // 2, features)), array((TOKENS // 2, features)))
    return call(
        functools.partial(norm1_back_kernel, n_mp),
        "norm1_backward",
        (1,),
        [held((rows, features))] * n_mp
        + [image(width), mine_of, mine]
        + [pl.BlockSpec((1, features), lambda j, s: (0, s[1])), mine_of],
        [half, half, (held((8, features)), array((8, features), F32))],
        (*got, tokens, tokens, d_attn, gain.reshape(1, -1), cotangent),
        [pltpu.VMEM((TOKENS, features), F32)],
        after=after,
        prefetch=scalars,
    )


def output_kernel(n_mp, scalars_ref, *refs):
    got, refs = refs[:n_mp], refs[n_mp:]
    hidden_ref, bias_ref, keep_ref, send_ref, total = refs
    value = hidden_ref[...] + bias_ref[...]
    for piece in got:
        value = value + piece[...].astype(F32)
    total[...] = value
    half = TOKENS // 2
    path = scalars_ref[3]
    keep_ref[...] = total[pl.ds(pl.multiple_of(path * half, half), half), :].astype(BF16)
    send_ref[...] = total[pl.ds(pl.multiple_of((1 - path) * half, half), half), :].astype(BF16)


def output_halves(got, hidden, fc2_bias, scalars, after=()):
    n_mp = len(got)
    features = got[0].shape[1]
    half = (held((TOKENS // 2, features)), array((TOKENS // 2, features)))
    return call(
        functools.partial(output_kernel, n_mp),
        "output_halves",
        (1,),
        [held((TOKENS, features))] * n_mp
        + [pl.BlockSpec((TOKENS, features), lambda j, s: (0, s[1]))]
        + [pl.BlockSpec((1, features), lambda j, s: (0, s[1]))],
        [half, half],
        (*got, hidden, fc2_bias.reshape(1, -1)),
        [pltpu.VMEM((TOKENS, features), F32)],
        after=after,
        prefetch=scalars,
    )


def slots_of(shapes, width):
    row, lane, slots = 0, 0, []
    for rows, n in shapes:
        mine = []
        for _ in range(rows):
            pieces = []
            for at in range(0, n, width):
                size = min(width, n - at)
                if lane + size > width:
                    row, lane = row + 1, 0
                pieces.append((row, lane, at, size))
                lane += size
            mine.append(pieces)
        slots.append(mine)
    return slots, -(-(row + 1) // 8) * 8


def pack_kernel(n_mp, slots, *refs):
    wide, arrays, packed_ref = refs[:n_mp], refs[n_mp:-1], refs[-1]
    packed_ref[...] = jnp.zeros(packed_ref.shape, F32)
    total = wide[0][...]
    for piece in wide[1:]:
        total = total + piece[...]
    for r, pieces in enumerate(slots[0]):
        for row, lane, at, n in pieces:
            packed_ref[row : row + 1, lane : lane + n] = total[r : r + 1, at : at + n]
    for array_ref, mine in zip(arrays, slots[1:]):
        for r, pieces in enumerate(mine):
            for row, lane, at, n in pieces:
                packed_ref[row : row + 1, lane : lane + n] = array_ref[r : r + 1, at : at + n]


def pack(wide_pieces, arrays, rows, after=()):
    width = wide_pieces[0].shape[1]
    shapes = [wide_pieces[0].shape] + [(count, v.shape[1]) for v, count in zip(arrays, rows)]
    slots, total = slots_of(shapes, width)
    packed = call(
        functools.partial(pack_kernel, len(wide_pieces), slots),
        "pack",
        (1,),
        [held(v.shape) for v in (*wide_pieces, *arrays)],
        [(held((total, width)), array((total, width), F32))],
        (*wide_pieces, *arrays),
        after=after,
    )[0]
    return packed, slots


def unpack_kernel(slots, a_ref, b_ref, *outs):
    for out, mine in zip(outs, slots):
        for r, pieces in enumerate(mine):
            for row, lane, at, n in pieces:
                out[r : r + 1, at : at + n] = (
                    a_ref[row : row + 1, lane : lane + n] + b_ref[row : row + 1, lane : lane + n]
                )


def unpack(a, b, slots, after=()):
    shapes = [(len(mine), sum(n for *_, n in mine[0])) for mine in slots]
    return call(
        functools.partial(unpack_kernel, slots),
        "unpack",
        (1,),
        [held(a.shape)] * 2,
        [(held(shape), array(shape, F32)) for shape in shapes],
        (a, b),
        after=after,
    )


def swap(value, axis, apart):
    n = lax.axis_size(axis)
    return lax.ppermute(value, axis, [(i, i ^ apart) for i in range(n)])


def pick(value, axis, index):
    return lax.dynamic_index_in_dim(value, index, axis, keepdims=False)


def gathered(value, axis):
    return [value] + [swap(value, axis, k) for k in range(1, lax.axis_size(axis))]


def exchanged(blocks, axis):
    return blocks[:1] + [swap(block, axis, k) for k, block in enumerate(blocks) if k]


def spread(value, axis):
    value = value[:, None]
    apart = 1
    while apart < lax.axis_size(axis):
        other = swap(value, axis, apart)
        turned = (lax.axis_index(axis) & apart) > 0
        value = jnp.concatenate(
            [jnp.where(turned, other, value), jnp.where(turned, value, other)], axis=1
        )
        apart *= 2
    return value.reshape((value.shape[0], -1) + value.shape[3:])


def halve(value, dim, axis, apart, bit):
    received = swap(pick(value, dim, 1 - bit), axis, apart)
    return pick(value, dim, bit).astype(F32) + received.astype(F32)


def across(halves):
    keep, send = halves
    return keep, swap(send, "dp", 1)


def first_fold(name, keep, got, scalars, after, cut=False):
    n_path, n_dp = lax.axis_size("path"), lax.axis_size("dp")
    block, lanes = keep.shape[1:]
    shape = (n_path, n_dp // 4, 2, block, lanes)
    got = got.reshape(shape)
    keep = keep.reshape(shape)
    if cut:
        half = lanes // 2
        parts = [(keep, got, 0, 3, half, 0), (keep, got, 2, 4, half, 1)]
    else:
        parts = [(keep, got, 0, 3, lanes, 0)]
    out = fold(name, parts, scalars, after)
    result = [(out[1], swap(out[0], "path", 1), False)]
    if cut:
        result.append((out[3], swap(out[2], "dp", 2), True))
    return result


def second_fold(name, parts, scalars, after):
    ins = []
    for hold, got, path_next in parts:
        dim, slot = (0, 3) if path_next else (1, 4)
        ins.append((hold, got, dim, slot, hold.shape[-1], 0))
    out = fold(name, ins, scalars, after)
    result = []
    for i, (_, _, path_next) in enumerate(parts):
        send, hold = out[2 * i : 2 * i + 2]
        result.append((hold, swap(send, *(("path", 1) if path_next else ("dp", 2)))))
    return result


def arrived(parts):
    return tuple(part[1] for part in parts)


def last_sum(hold, got):
    n_dp, me_dp = lax.axis_size("dp"), lax.axis_index("dp")
    value = hold.astype(F32) + got.astype(F32)
    size = value.shape[0]
    b = 2
    while size > 1:
        size //= 2
        shape = (size, 2) + value.shape[1:]
        value = halve(value.astype(BF16).reshape(shape), 1, "dp", 1 << b, (me_dp >> b) & 1)
        b += 1
    return value[0]


def summed_at_once(value, axis):
    return sum(gathered(value, axis))


def summed(value, axes):
    for axis in axes:
        apart = 1
        while apart < lax.axis_size(axis):
            value = value + swap(value, axis, apart)
            apart *= 2
    return value


def body(
    tokens,
    hires,
    valid_rows,
    cotangent,
    attention_norm_gain,
    attention_norm_bias,
    w_qkv,
    qv_bias,
    w_out,
    out_bias,
    mlp_norm_gain,
    mlp_norm_bias,
    w_fc1,
    fc1_bias,
    down_weight,
    fc2_bias,
    w_adapt,
    gate_param,
    dw_kernel,
    dw_bias,
    channel_norm_gain,
    channel_norm_bias,
    w_pw1,
    pw1_bias,
    w_pw2,
    pw2_bias,
    layer_scale,
):
    path = lax.axis_index("path")
    n_path = lax.axis_size("path")
    dp = lax.axis_index("dp")
    mp = lax.axis_index("mp")
    n_mp = lax.axis_size("mp")
    groups = n_path * lax.axis_size("dp")
    assert tokens.shape[0] == n_path == 2
    width = tokens.shape[2]
    heads_width = w_qkv.shape[2]
    features = width // n_mp
    channels = hires.shape[3]
    all_channels = w_pw1.shape[0]
    part_rows = TOKENS // n_mp
    chunk_rows = GRID_HI // CHUNKS

    valid = pick(valid_rows, 0, path)
    hi_valid = (valid * GRID_HI + GRID_LO - 1) // GRID_LO
    scalars = jnp.stack([valid, mp, dp & 1, path, (dp >> 1) & 1, hi_valid])
    gate = jnp.tanh(gate_param)

    def my_features(v):
        return lax.dynamic_slice_in_dim(v, mp * features, features, v.ndim - 1)

    share_rows = heads_width // groups
    share = lax.dynamic_slice_in_dim(
        w_out, (path * lax.axis_size("dp") + dp) * share_rows, share_rows, 0
    )
    w_out_pieces = jnp.stack(gathered(share, "mp"))
    w_out_pieces = spread(spread(w_out_pieces, "dp"), "path")

    rows, rows_all, pooled_field, d_pooled, d_adapted = [], [], [], [], []
    g_pw2_bias = 0.0
    last = ()
    for c in range(CHUNKS):
        send, *chunk, sums = front(
            hires,
            dw_kernel,
            dw_bias,
            cotangent,
            gate,
            w_adapt,
            layer_scale,
            scalars,
            c * chunk_rows,
            chunk_rows,
            last,
        )
        last = (sums,)
        g_pw2_bias = g_pw2_bias + sums
        rows.append(send)
        rows_all.append(lax.all_gather(send, "mp", axis=0, tiled=False))
        for kept, value in zip((pooled_field, d_pooled, d_adapted), chunk):
            kept.append(value)

    w_flat = w_qkv.reshape(width, 3 * heads_width)
    normed1, query, keys, values, attended = attention_forward(
        tokens, attention_norm_gain, attention_norm_bias, w_flat, qv_bias, scalars, last
    )
    attended_pieces = gathered(attended, "mp")
    last = (attended,)

    def conv(c, after):
        out = conv_mlp(
            rows_all[c],
            channel_norm_gain,
            channel_norm_bias,
            w_pw1,
            pw1_bias,
            w_pw2,
            after,
        )
        return out, lax.psum_scatter(out[4], "mp", scatter_dimension=0, tiled=False), (out[7],)

    conv_out, received = [], []
    out, got, last = conv(0, last)
    conv_out.append(out)
    received.append(got)
    hidden1, normed2, fc_active, d_fc_inner, g_fc1_bias, *sends = vit_mlp(
        tokens,
        attended_pieces,
        w_out_pieces,
        out_bias,
        mlp_norm_gain,
        mlp_norm_bias,
        w_fc1,
        fc1_bias,
        down_weight,
        cotangent,
        scalars,
        last,
    )
    last = (g_fc1_bias,)
    d_normed2_pieces = exchanged(sends, "mp")
    dy = pick(cotangent, 0, path)
    fc_halves = weight_grads(
        "grad_fc", groups, [[(normed2, d_fc_inner)], [(dy, fc_active)]], scalars, last
    )
    fc_halves = across(fc_halves)
    last = (fc_halves[0],)
    d_attn_part, norm2_sums = norm2_backward(
        d_normed2_pieces, hidden1, cotangent, mlp_norm_gain, scalars, last
    )
    d_attn_pieces = gathered(d_attn_part, "mp")
    last = (norm2_sums,)
    for c in range(1, CHUNKS):
        out, got, last = conv(c, last)
        conv_out.append(out)
        received.append(got)
    conv_normed, conv_inner, pooled_active, backs, _, means, invs, bias_sums = zip(*conv_out)
    g_pw1_bias = sum(bias_sums)
    pw_halves = weight_grads(
        "grad_pw",
        groups,
        [list(zip(conv_normed, conv_inner)), list(zip(backs, pooled_active))],
        scalars,
        last,
    )
    pw_halves = across(pw_halves)
    last = (pw_halves[0],)

    d_attn, d_query, d_keys, d_values, *sends = attention_backward(
        n_mp,
        tokens,
        attention_norm_gain,
        d_attn_pieces,
        w_out,
        query,
        keys,
        values,
        w_flat,
        scalars,
        last,
    )
    d_normed1_pieces = exchanged(sends, "mp")
    last = (d_query,)
    fc_parts = first_fold("fold_fc", *fc_halves, scalars, last)
    last = (fc_parts[0][0],)
    pw_parts = first_fold("fold_pw", *pw_halves, scalars, last, True)
    last = (pw_parts[0][0],)
    qkv_halves = weight_grads(
        "grad_qkv",
        groups,
        [
            [(normed1, d_query)],
            [(normed1, d_keys)],
            [(normed1, d_values)],
            [(d_attn, attended)],
        ],
        scalars,
        last,
    )
    qkv_halves = across(qkv_halves)
    last = (qkv_halves[0],)
    g_qv_bias = jnp.stack(
        [jnp.sum(d_query.astype(F32), axis=0), jnp.sum(d_values.astype(F32), axis=0)]
    )
    tokens_keep, tokens_send, norm1_sums = norm1_backward(
        d_normed1_pieces,
        tokens,
        d_attn,
        attention_norm_gain,
        cotangent,
        scalars,
        last + arrived(fc_parts)
    )
    last = (norm1_sums,)
    fc_parts = second_fold("fold_fc_last", fc_parts, scalars, last)
    last = (fc_parts[0][0],)
    qkv_parts = first_fold("fold_qkv", *qkv_halves, scalars, last)
    last = (qkv_parts[0][0],)

    pooled, g_scale, g_gate, *sends = adapter(
        n_mp,
        received,
        d_pooled,
        pooled_field,
        pw2_bias,
        layer_scale,
        w_adapt,
        fc_active,
        down_weight,
        gate,
        cotangent,
        scalars,
        last,
    )
    branch_pieces = exchanged(sends, "mp")
    pooled_rows = d_adapted[0].shape[0]
    adapt_halves = weight_grads(
        "grad_adapt",
        groups,
        [
            [
                (d_adapted[c], pooled[c * pooled_rows : (c + 1) * pooled_rows])
                for c in range(CHUNKS)
            ]
        ],
        scalars,
        (g_scale,),
    )
    adapt_halves = across(adapt_halves)
    last = (adapt_halves[0],)
    def placed(v):
        return lax.dynamic_update_slice(jnp.zeros((width,), F32), v, (mp * features,))

    wide = jnp.concatenate(
        [norm2_sums[:3]] + [placed(norm1_sums[i])[None] for i in range(3)] + [g_gate]
    )
    wide_pieces = gathered(wide, "mp")

    d_field, g_kernel, conv_sums = conv_backward(
        received,
        rows,
        means,
        invs,
        d_pooled,
        hires,
        dw_kernel,
        lax.dynamic_slice_in_dim(channel_norm_gain, mp * channels, channels, 0),
        all_channels,
        scalars,
        last + arrived(pw_parts) + arrived(qkv_parts),
    )
    last = (conv_sums,)
    small = [g_qv_bias, g_fc1_bias, g_pw1_bias, g_kernel, conv_sums, g_pw2_bias, g_scale]
    packed, slots = pack(wide_pieces, small, (2, 1, 1, 49, 3, 1, 1), last)
    last = (packed,)
    packed = summed(packed, ("dp",))
    pw_parts = second_fold("fold_pw_last", pw_parts, scalars, last)
    last = (pw_parts[0][0],)
    output_keep, output_send = output_halves(branch_pieces, hidden1, fc2_bias, scalars, last)
    last = (output_keep,)
    qkv_parts = second_fold("fold_qkv_last", qkv_parts, scalars, last)
    last = (qkv_parts[0][0],)
    adapt_parts = first_fold("fold_adapt", *adapt_halves, scalars, last)
    last = (adapt_parts[0][0],)

    def both_images(mine, send):
        other = swap(send, "path", 1)
        first = path == 0
        return jnp.stack([jnp.where(first, mine, other), jnp.where(first, other, mine)])

    def keep_half(rows):
        halves = rows.reshape((2, rows.shape[0] // 2) + rows.shape[1:])
        return both_images(pick(halves, 0, path), pick(halves, 0, 1 - path))

    output = both_images(output_keep, output_send)
    tokens_grad = both_images(tokens_keep, tokens_send)
    hires_grad = keep_half(d_field)
    adapt_parts = second_fold("fold_adapt_last", adapt_parts, scalars, last)

    (both,) = (last_sum(*part) for part in fc_parts)
    g_fc1_mine, g_fc2_mine = both[:, : w_fc1.shape[1]], both[:, w_fc1.shape[1] :]
    g_pw1_mine, g_pw2_mine = (last_sum(*part) for part in pw_parts)
    (g_rest,) = (last_sum(*part) for part in qkv_parts)
    g_qkv_mine = g_rest[:, : 3 * heads_width].reshape(-1, 3, heads_width)
    g_out_mine = g_rest[:, 3 * heads_width :]
    (g_adapt_mine,) = (last_sum(*part) for part in adapt_parts)


    small = unpack(packed, swap(packed, "path", 1), slots)
    wide, g_qv_bias, g_fc1_bias, g_pw1_bias, g_kernel, conv_sums, g_pw2_bias, g_scale = small
    g_out_bias, g_norm2_gain, g_norm2_bias, g_norm1_gain, g_norm1_bias, g_fc2_bias, g_gate = wide
    g_dw_bias, g_cnorm_gain, g_cnorm_bias = conv_sums
    return (
        output,
        tokens_grad,
        hires_grad,
        g_norm1_gain,
        g_norm1_bias,
        g_qkv_mine,
        g_qv_bias,
        g_out_mine.T,
        g_out_bias,
        g_norm2_gain,
        g_norm2_bias,
        g_fc1_mine,
        g_fc1_bias[0],
        g_fc2_mine.T,
        g_fc2_bias,
        g_adapt_mine.T,
        g_gate,
        g_kernel,
        g_dw_bias,
        g_cnorm_gain,
        g_cnorm_bias,
        g_pw1_mine,
        g_pw1_bias[0],
        g_pw2_mine.T,
        g_pw2_bias[0],
        g_scale[0],
    )


def solution(mesh):
    in_specs = (
        P("dp", None, None),
        P("dp", None, None, "mp"),
        P("dp"),
        P("dp", None, None),
        P(),
        P(),
        P(None, None, "mp"),
        P(None, "mp"),
        P("mp", None),
        P(),
        P(),
        P(),
        P(None, "mp"),
        P("mp"),
        P("mp", None),
        P(),
        P("mp", None),
        P(),
        P(None, "mp"),
        P("mp"),
        P(),
        P(),
        P(None, "mp"),
        P("mp"),
        P("mp", None),
        P("mp"),
        P("mp"),
    )
    out_specs = (
        P("dp", "path", "mp"),
        P("dp", "path", "mp"),
        P("dp", "path", None, "mp"),
        P(),
        P(),
        P(("path", "dp"), None, "mp"),
        P(None, "mp"),
        P("mp", ("path", "dp")),
        P(),
        P(),
        P(),
        P(("path", "dp"), "mp"),
        P("mp"),
        P("mp", ("path", "dp")),
        P(),
        P("mp", ("path", "dp")),
        P(),
        P(None, "mp"),
        P("mp"),
        P("mp"),
        P("mp"),
        P(("path", "dp"), "mp"),
        P("mp"),
        P("mp", ("path", "dp")),
        P("mp"),
        P("mp"),
    )
    return jax.shard_map(body, mesh=mesh, in_specs=in_specs, out_specs=out_specs, check_vma=False)
```

```python
import functools

import jax
import jax.numpy as jnp
import numpy as np
from jax import lax
from jax.experimental import pallas as pl
from jax.experimental.pallas import tpu as pltpu
from jax.sharding import PartitionSpec as P

HEAD_DIM = 64
GRID_LO = 24
GRID_HI = 32
TOKENS = GRID_LO * GRID_LO
CELLS = GRID_HI * GRID_HI
LANES = 128
STAT_ROWS = 16
CELL_BLOCK = 256
POOL_BLOCK = CELL_BLOCK * 9 // 16

norm_epsilon = 1e-05
channel_epsilon = 1e-06
F32 = jnp.float32
BF16 = jnp.bfloat16
VMEM_BYTES = 60 * 1024 * 1024
CHUNKS = 2


def gelu_pair(v):
    c = 0.7978845608028654
    square = v * v
    t = jnp.tanh(c * v * (1.0 + 0.044715 * square))
    half = 0.5 + 0.5 * t
    return v * half, half + (0.5 * c) * v * (1.0 - t * t) * (1.0 + 3 * 0.044715 * square)


def pool_rows(lo, hi):
    ratio = hi / lo
    target = np.arange(lo, dtype=np.float64)[:, None]
    source = np.arange(hi, dtype=np.float64)[None, :]
    lower = np.maximum(source, target * ratio)
    upper = np.minimum(source + 1.0, (target + 1.0) * ratio)
    return np.round(np.maximum(upper - lower, 0.0) / ratio * 4) / 4


def pool_block():
    rows = CELL_BLOCK // GRID_HI
    return jnp.asarray(np.kron(pool_rows(rows * 3 // 4, rows), pool_rows(GRID_LO, GRID_HI)), BF16)


def dot(a, b):
    return jnp.dot(a, b, preferred_element_type=F32)


def dot_nt(a, b):
    return lax.dot_general(a, b, (((1,), (1,)), ((), ())), preferred_element_type=F32)


def dot_tn(a, b):
    return lax.dot_general(a, b, (((0,), (0,)), ((), ())), preferred_element_type=F32)


def standardize(v, eps):
    centred = v - jnp.mean(v, axis=-1, keepdims=True)
    inv = lax.rsqrt(jnp.mean(centred * centred, axis=-1, keepdims=True) + eps)
    return centred * inv, inv


KERNEL_US = {
    "front": 0.5,
    "attention_forward": 10,
    "conv_mlp": 0.5,
    "vit_mlp": 33,
    "norm2_backward": 0.5,
    "attention_backward": 31,
    "norm1_backward": 0.5,
    "adapter": 0.5,
    "conv_backward": 0.5,
    "output_halves": 3,
    "pack": 3,
    "unpack": 3,
    "grad_fc": 0.5,
    "grad_pw1": 0.5,
    "grad_pw2": 0.5,
    "grad_qkv": 0.5,
    "grad_adapt": 0.5,
    "fold_fc": 0.5,
    "fold_pw1": 0.5,
    "fold_pw2": 0.5,
    "fold_qkv": 3,
    "fold_adapt": 0.5,
    "fold_fc_last": 3,
    "fold_pw1_last": 3,
    "fold_pw2_last": 3,
    "fold_qkv_last": 3,
    "fold_adapt_last": 3,
}
FLOPS_PER_US = 1.15e9


def call(
    kernel, name, grid, ins, outs, operands, scratch=(), after=(), prefetch=None
):
    lead = 0 if prefetch is None else 1
    count = lead + len(ins)

    def run(*refs):
        kernel(*refs[:count], *refs[count + len(after) :])

    in_specs = list(ins) + [pl.BlockSpec(memory_space=pl.ANY)] * len(after)
    return pl.pallas_call(
        run,
        grid_spec=pltpu.PrefetchScalarGridSpec(
            num_scalar_prefetch=lead,
            grid=grid,
            in_specs=in_specs,
            out_specs=[spec for spec, _ in outs],
            scratch_shapes=list(scratch),
        ),
        out_shape=[shape for _, shape in outs],
        compiler_params=pltpu.CompilerParams(
            dimension_semantics=("arbitrary",) * len(grid), vmem_limit_bytes=VMEM_BYTES
        ),
        name=name,
        cost_estimate=pl.CostEstimate(
            flops=int(KERNEL_US[name] * FLOPS_PER_US), bytes_accessed=1, transcendentals=0
        ),
    )(*(() if prefetch is None else (prefetch,)), *operands, *after)


SCALARS = pl.BlockSpec(memory_space=pltpu.SMEM)


def array(shape, dtype=BF16):
    return jax.ShapeDtypeStruct(shape, dtype)


def held(shape):
    return pl.BlockSpec(shape, lambda *_: (0,) * len(shape), pipeline_mode=pl.Buffered(1))


def whole(shape):
    return pl.BlockSpec(shape, lambda *_: (0,) * len(shape))


def rows_to_lanes(columns):
    rows = columns[0].shape[0]
    lane = lax.broadcasted_iota(jnp.int32, (rows, LANES), 1)
    packed = jnp.zeros((rows, LANES), F32)
    for i, column in enumerate(columns):
        packed = jnp.where(lane == i, column, packed)
    return packed.T


def stat_rows(columns, width):
    lanes = rows_to_lanes(columns)
    pieces = [
        lanes[i : i + 1, t * LANES : (t + 1) * LANES]
        for i in range(2)
        for t in range(lanes.shape[1] // LANES)
    ]
    pieces.append(jnp.zeros((STAT_ROWS - len(pieces), LANES), F32))
    stats = jnp.concatenate(pieces, axis=0).astype(BF16)
    if width % LANES:
        return jnp.concatenate([stats, jnp.zeros((STAT_ROWS, width - LANES), BF16)], axis=1)
    return jnp.concatenate([stats] * (width // LANES), axis=1)


def channel_block(channels):
    return LANES if channels % LANES == 0 else channels


def store_shifted(shifted, a, row):
    column = lax.broadcasted_iota(jnp.int32, row.shape, 0)
    for s in range(7):
        move = s - 3
        if move == 0:
            shifted[s, a] = row
        else:
            rolled = pltpu.roll(row, (-move) % GRID_HI, 0)
            inside = (column + move >= 0) & (column + move < GRID_HI)
            shifted[s, a] = jnp.where(inside, rolled, 0.0)


def correlate(shifted, a0, count, taps, start):
    sums = [start] * count
    for r_in in range(count + 6):
        for s in range(7):
            value = shifted[s, a0 + r_in]
            for o in range(count):
                r = r_in - o
                if 0 <= r < 7:
                    sums[o] = sums[o] + value * taps(r, s)
    return sums


def front_kernel(
    base, count, s_ref, field_ref, k_ref, bias_ref, pool_ref, dy_ref, gate_ref, wa_ref, scale_ref,
    send_ref, field_pooled_ref, d_pooled_ref, d_adapted_ref, sums_ref, rank_ref, shifted,
):
    hi_valid = s_ref[5]
    cb = field_ref.shape[2]
    rank_ref[...] = jnp.full(rank_ref.shape, s_ref[6], jnp.int32)

    @pl.when(pl.program_id(0) == 0)
    def _():
        d_adapted_ref[...] = (gate_ref[...] * dy_ref[...].astype(F32)).astype(BF16)

    @pl.loop(0, count + 6)
    def _(a):
        source = base + a - 3
        keep = (source >= 0) & (source < hi_valid)
        row = field_ref[jnp.clip(source, 0, GRID_HI - 1)].astype(F32)
        store_shifted(shifted, a, jnp.where(keep, row, 0.0))

    start = jnp.broadcast_to(bias_ref[...], (GRID_HI, cb))

    @pl.loop(0, count, step=4)
    def _(a0):
        sums = correlate(
            shifted, a0, 4, lambda r, s: k_ref[r * 7 + s : r * 7 + s + 1, :], start
        )
        for o in range(4):
            at = pl.multiple_of((a0 + o) * GRID_HI, GRID_HI)
            send_ref[pl.ds(at, GRID_HI), :] = sums[o].astype(BF16)

    block_rows = CELL_BLOCK // GRID_HI
    for i in range(count // block_rows):
        first = base + i * block_rows
        rows = field_ref[first : first + block_rows]
        row = lax.broadcasted_iota(jnp.int32, rows.shape, 0) + first
        rows = jnp.where(row < hi_valid, rows.astype(F32), 0.0).astype(BF16)
        field_pooled_ref[i * POOL_BLOCK : (i + 1) * POOL_BLOCK] = dot(
            pool_ref[...], rows.reshape(CELL_BLOCK, cb)
        )
    d_pooled = dot_nt(d_adapted_ref[...], wa_ref[...]).astype(BF16).astype(F32)
    row = lax.broadcasted_iota(jnp.int32, d_pooled.shape, 0) + base * GRID_HI * 9 // 16
    d_pooled = jnp.where(row < s_ref[0] * GRID_LO, d_pooled, 0.0)
    d_pooled_ref[...] = d_pooled.astype(BF16)
    scaled = (d_pooled * scale_ref[...]).astype(BF16)
    sums_ref[0:1, :] = jnp.sum(scaled.astype(F32), axis=0, keepdims=True)
    sums_ref[1:2, :] = jnp.sum(d_pooled, axis=0, keepdims=True)
    sums_ref[2:, :] = jnp.zeros((6, cb), F32)


def front(hires, kernel, bias, cotangent, gate, w_adapt, layer_scale, scalars, base, count, after=()):
    channels = hires.shape[3]
    width = cotangent.shape[2]
    cb = channel_block(channels)
    cells = count * GRID_HI
    pooled_rows = cells * 9 // 16
    chunk = base // count

    def column(rows):
        return pl.BlockSpec((rows, cb), lambda j, s: (0, j))

    return call(
        functools.partial(front_kernel, base, count),
        "front",
        (channels // cb,),
        [
            pl.BlockSpec((None, GRID_HI, GRID_HI, cb), lambda j, s: (s[3], 0, 0, j)),
            column(49),
            column(1),
            held((POOL_BLOCK, CELL_BLOCK)),
            pl.BlockSpec((None, pooled_rows, width), lambda j, s: (s[3], chunk, 0)),
            held((1, width)),
            pl.BlockSpec((cb, width), lambda j, s: (j, 0)),
            column(1),
        ],
        [
            (column(cells), array((cells, channels))),
            (column(pooled_rows), array((pooled_rows, channels), F32)),
            (column(pooled_rows), array((pooled_rows, channels))),
            (whole((pooled_rows, width)), array((pooled_rows, width))),
            (column(8), array((8, channels), F32)),
            (whole((8, LANES)), array((8, LANES), jnp.int32)),
        ],
        (hires, kernel, bias.reshape(1, -1), pool_block(), cotangent, gate.reshape(1, -1), w_adapt)
        + (layer_scale.reshape(1, -1),),
        [pltpu.VMEM((7, count + 6, GRID_HI, cb), F32)],
        after,
        prefetch=scalars,
    )


def softmax_rows(q, k, key_valid):
    scores = jnp.where(key_valid, dot_nt(q, k) * HEAD_DIM ** (-0.5), -1e30)
    e = jnp.exp(scores - jnp.max(scores, axis=-1, keepdims=True))
    return e * (1.0 / jnp.sum(e, axis=-1, keepdims=True))


def attention_kernel(
    s_ref, x_ref, gain_ref, shift_ref, wq_ref, wk_ref, wv_ref, bias_ref,
    normed_ref, q_ref, k_ref, v_ref, att_ref,
):
    @pl.when(pl.program_id(0) == 0)
    def _():
        xhat, _ = standardize(x_ref[...].astype(F32), norm_epsilon)
        normed_ref[...] = (xhat * gain_ref[...] + shift_ref[...]).astype(BF16)

    normed = normed_ref[...]
    q_ref[...] = (dot(normed, wq_ref[...]) + bias_ref[0:1]).astype(BF16)
    k_ref[...] = dot(normed, wk_ref[...]).astype(BF16)
    v_ref[...] = (dot(normed, wv_ref[...]) + bias_ref[1:2]).astype(BF16)
    key = lax.broadcasted_iota(jnp.int32, (1, TOKENS), 1)
    key_valid = key < s_ref[0] * GRID_LO
    for h in range(q_ref.shape[1] // HEAD_DIM):
        cut = slice(h * HEAD_DIM, (h + 1) * HEAD_DIM)
        probs = softmax_rows(q_ref[:, cut], k_ref[:, cut], key_valid)
        att_ref[:, cut] = dot(probs.astype(BF16), v_ref[:, cut]).astype(BF16)


def image(width):
    return pl.BlockSpec((None, TOKENS, width), lambda j, s: (s[3], 0, 0))


def attention_forward(tokens, gain, shift, w_flat, qv_bias, scalars, after=()):
    width = tokens.shape[2]
    heads_width = w_flat.shape[1] // 3
    blocks = heads_width // LANES
    column = (pl.BlockSpec((TOKENS, LANES), lambda j, s: (0, j)), array((TOKENS, heads_width)))

    def weight(t):
        return pl.BlockSpec((width, LANES), lambda j, s: (0, t * blocks + j))

    return call(
        attention_kernel,
        "attention_forward",
        (blocks,),
        [image(width), held((1, width)), held((1, width)), weight(0), weight(1), weight(2)]
        + [pl.BlockSpec((2, LANES), lambda j, s: (0, j))],
        [(whole((TOKENS, width)), array((TOKENS, width)))] + [column] * 4,
        (tokens, gain.reshape(1, -1), shift.reshape(1, -1)) + (w_flat,) * 3 + (qv_bias,),
        after=after,
        prefetch=scalars,
    )


def attention_back_kernel(n_mp, scalars_ref, *refs):
    pieces, refs = refs[:n_mp], refs[n_mp:]
    x_ref, gain_ref, w_out_ref, q_ref, k_ref, v_ref, wq_ref, wk_ref, wv_ref = refs[:9]
    d_attn_ref, dq_ref, dk_ref, dv_ref = refs[9:13]
    send_ref, total = refs[13:]
    step = pl.program_id(0)
    mp = scalars_ref[1]
    part = pieces[0].shape[0]

    @pl.when(step == 0)
    def _():
        for k in range(n_mp):
            at = pl.multiple_of((mp ^ k) * part, part)
            total[pl.ds(at, part), :] = pieces[k][...].astype(F32)
        d_attn_ref[...] = total[...].astype(BF16)

    d_att_all = dot_nt(d_attn_ref[...], w_out_ref[...]).astype(BF16)
    key = lax.broadcasted_iota(jnp.int32, (1, TOKENS), 1)
    key_valid = key < scalars_ref[0] * GRID_LO
    scale = HEAD_DIM ** (-0.5)
    for h in range(q_ref.shape[1] // HEAD_DIM):
        cut = slice(h * HEAD_DIM, (h + 1) * HEAD_DIM)
        q, k, v, d_att = q_ref[:, cut], k_ref[:, cut], v_ref[:, cut], d_att_all[:, cut]
        probs = softmax_rows(q, k, key_valid)
        d_probs = dot_nt(d_att, v)
        delta = jnp.sum(probs * d_probs, axis=-1, keepdims=True)
        d_scores = (probs * (d_probs - delta)).astype(BF16)
        dq_ref[:, cut] = (dot(d_scores, k) * scale).astype(BF16)
        dk_ref[:, cut] = (dot_tn(d_scores, q) * scale).astype(BF16)
        dv_ref[:, cut] = dot_tn(probs.astype(BF16), d_att).astype(BF16)
    share = dot_nt(dq_ref[...], wq_ref[...]) + dot_nt(dk_ref[...], wk_ref[...])
    share = share + dot_nt(dv_ref[...], wv_ref[...])

    @pl.when(step == 0)
    def _():
        total[...] = share

    @pl.when(step > 0)
    def _():
        total[...] += share

    @pl.when(step == pl.num_programs(0) - 1)
    def _():
        features = send_ref.shape[2]
        xhat, _ = standardize(x_ref[...].astype(F32), norm_epsilon)
        weighted = total[...] * gain_ref[...]
        ones = jnp.sum(weighted, axis=-1, keepdims=True)
        twos = jnp.sum(weighted * xhat, axis=-1, keepdims=True)
        pad = jnp.zeros((-TOKENS % LANES, 1), F32)
        stats = stat_rows([jnp.concatenate([ones, pad]), jnp.concatenate([twos, pad])], features)
        for g in range(n_mp):
            mine = slice(g * features, (g + 1) * features)
            send_ref[g, :TOKENS, :] = total[:, mine].astype(BF16)
            send_ref[g, TOKENS:, :] = stats


def attention_backward(
    n_mp, tokens, gain, d_attn_pieces, w_out, q, k, v, w_flat, scalars, after=()
):
    width = tokens.shape[2]
    heads_width = q.shape[1]
    blocks = heads_width // LANES
    column = pl.BlockSpec((TOKENS, LANES), lambda j, s: (0, j))

    def weight(t):
        return pl.BlockSpec((width, LANES), lambda j, s: (0, t * blocks + j))

    send_shape = (n_mp, TOKENS + STAT_ROWS, width // n_mp)
    return call(
        functools.partial(attention_back_kernel, n_mp),
        "attention_backward",
        (blocks,),
        [held(d_attn_pieces[0].shape)] * n_mp
        + [image(width), held((1, width)), pl.BlockSpec((LANES, width), lambda j, s: (j, 0))]
        + [column, column, column, weight(0), weight(1), weight(2)],
        [(whole((TOKENS, width)), array((TOKENS, width)))]
        + [(column, array((TOKENS, heads_width)))] * 3
        + [(held(send_shape), array(send_shape))],
        (*d_attn_pieces, tokens, gain.reshape(1, -1), w_out, q, k, v, w_flat, w_flat, w_flat),
        [pltpu.VMEM((TOKENS, width), F32)],
        after,
        prefetch=scalars,
    )


def conv_mlp_kernel(
    n_mp, chunk, s_ref, rows_ref, gain_ref, shift_ref, w1_hbm, b_ref, w2_hbm, wa_hbm, d_adapted_ref, pool_ref,
    normed_ref, inner_ref, pooled_ref, back_ref, send_ref, mean_ref, inv_ref, bias_ref,
    branch_ref, adapted_ref, scale_ref, full, w1_ref, w2_ref, wa_ref, sems,
):
    cells, channels = rows_ref.shape[1:]
    cut = 256
    steps = w1_ref.shape[1] // cut
    cuts = [slice(j * cut, (j + 1) * cut) for j in range(steps)]
    loads = [pltpu.make_async_copy(wa_hbm, wa_ref, sems.at[2 * steps])]
    for j, at in enumerate(cuts):
        loads.append(pltpu.make_async_copy(w1_hbm.at[:, at], w1_ref.at[:, at], sems.at[j]))
        loads.append(pltpu.make_async_copy(w2_hbm.at[at, :], w2_ref.at[at, :], sems.at[steps + j]))
    for load in loads:
        load.start()
    for g in range(n_mp):
        full[:, g * channels : (g + 1) * channels] = rows_ref[g].astype(F32)
    spatial = full[...]
    mean = jnp.mean(spatial, axis=-1, keepdims=True)
    centred = spatial - mean
    inv = lax.rsqrt(jnp.mean(centred * centred, axis=-1, keepdims=True) + channel_epsilon)
    xhat = centred * inv
    full[...] = xhat
    mean_ref[...] = jnp.broadcast_to(mean, mean_ref.shape)
    inv_ref[...] = jnp.broadcast_to(inv, inv_ref.shape)
    normed_ref[...] = (xhat * gain_ref[...] + shift_ref[...]).astype(BF16)
    loads[0].wait()
    count = back_ref.shape[0]
    valid = lax.broadcasted_iota(jnp.int32, (count, 1), 0) + chunk * count < s_ref[0] * GRID_LO
    back = dot_nt(d_adapted_ref[...], wa_ref[...])
    back_ref[...] = jnp.where(valid, back, 0.0).astype(BF16)
    for j, at in enumerate(cuts):
        loads[2 * j + 1].wait()
        active, slope = gelu_pair(dot(normed_ref[...], w1_ref[:, at]) + b_ref[:, at])
        active = active.astype(BF16)
        loads[2 * j + 2].wait()
        d_active = dot_nt(back_ref[...], w2_ref[at, :]).astype(BF16)
        backs = []
        for i in range(cells // CELL_BLOCK):
            lo = slice(i * POOL_BLOCK, (i + 1) * POOL_BLOCK)
            hi = slice(i * CELL_BLOCK, (i + 1) * CELL_BLOCK)
            pooled_ref[lo, at] = dot(pool_ref[...], active[hi]).astype(BF16)
            backs.append(dot_tn(pool_ref[...], d_active[lo]))
        d_inner = (slope * jnp.concatenate(backs, axis=0)).astype(BF16)
        inner_ref[:, at] = d_inner
        bias_ref[:, at] = jnp.sum(d_inner.astype(F32), axis=0, keepdims=True)

    d_normed = dot_nt(inner_ref[...], w1_ref[...])
    weighted = d_normed * gain_ref[...]
    ones = jnp.sum(weighted, axis=-1, keepdims=True)
    twos = jnp.sum(weighted * full[...], axis=-1, keepdims=True)
    stats = stat_rows([ones, twos], channels)
    for g in range(n_mp):
        send_ref[g, :cells, :] = d_normed[:, g * channels : (g + 1) * channels].astype(BF16)
        send_ref[g, cells:, :] = stats
    branch = dot(pooled_ref[...], w2_ref[...])
    scale_ref[...] = jnp.sum(back_ref[...].astype(F32) * branch, axis=0, keepdims=True)
    branch_ref[...] = jnp.where(valid, branch, 0.0).astype(BF16)
    adapted_ref[...] = dot(branch_ref[...], wa_ref[...])


def conv_mlp(rows, gain, shift, w1, b, w2, wa, d_adapted, chunk, scalars, after=()):
    n_mp, cells, channels = rows.shape
    total, hidden = w1.shape
    width = wa.shape[1]
    pooled = cells * 9 // 16
    send_shape = (n_mp, cells + STAT_ROWS, channels)
    anywhere = pl.BlockSpec(memory_space=pl.ANY)

    def out(shape, dtype=BF16):
        return (held(shape), array(shape, dtype))

    return call(
        functools.partial(conv_mlp_kernel, n_mp, chunk),
        "conv_mlp",
        (1,),
        [held((n_mp, cells, channels)), held((1, total)), held((1, total)), anywhere]
        + [held((1, hidden)), anywhere, anywhere, held((pooled, width))]
        + [held((POOL_BLOCK, CELL_BLOCK))],
        [
            out((cells, total)),
            out((cells, hidden)),
            out((pooled, hidden)),
            out((pooled, total)),
            out(send_shape),
            out((cells, LANES), F32),
            out((cells, LANES), F32),
            out((1, hidden), F32),
            out((pooled, total)),
            out((pooled, width), F32),
            out((1, total), F32),
        ],
        (rows, gain.reshape(1, -1), shift.reshape(1, -1), w1, b.reshape(1, -1), w2, wa, d_adapted)
        + (pool_block(),),
        [
            pltpu.VMEM((cells, total), F32),
            pltpu.VMEM((total, hidden), BF16),
            pltpu.VMEM((hidden, total), BF16),
            pltpu.VMEM((total, width), BF16),
            pltpu.SemaphoreType.DMA((2 * (hidden // 256) + 1,)),
        ],
        after,
        prefetch=scalars,
    )


def conv_back_kernel(chunks, total_channels, s_ref, *refs):
    (received, spatial, means, invs, d_pooled) = (
        refs[i * chunks : (i + 1) * chunks] for i in range(5)
    )
    refs = refs[5 * chunks :]
    field_ref, k_ref, gain_ref, pool_ref, out_ref, g_kernel_ref, sums_ref, shifted, moved = refs
    hi_valid = s_ref[5]
    cb = field_ref.shape[2]
    gain = gain_ref[...]
    zeros = jnp.zeros((GRID_HI, cb), F32)
    for a in (0, 1, 2, GRID_HI + 3, GRID_HI + 4, GRID_HI + 5):
        for s in range(7):
            shifted[s, a] = zeros
            moved[s, a] = zeros
    g_gain = jnp.zeros((1, cb), F32)
    g_shift = jnp.zeros((1, cb), F32)
    g_bias = jnp.zeros((1, cb), F32)
    block_rows = CELL_BLOCK // GRID_HI
    first = 0
    for c in range(chunks):
        cells = means[c].shape[0]
        per = cells // LANES
        stats = received[c][cells : cells + STAT_ROWS, :LANES].astype(F32)
        rows = [
            jnp.concatenate([stats[k * per + t : k * per + t + 1] for t in range(per)], axis=1)
            for k in range(2)
        ]
        rows.append(jnp.zeros((LANES - 2, cells), F32))
        columns = jnp.concatenate(rows, axis=0).T * (1.0 / total_channels)
        for i in range(cells // CELL_BLOCK):
            at = slice(i * CELL_BLOCK, (i + 1) * CELL_BLOCK)
            d_normed = received[c][at, :].astype(F32)
            column = columns[at]
            if cb > LANES:
                mean, inv = means[c][at, :1], invs[c][at, :1]
            else:
                mean, inv = means[c][at], invs[c][at]
            xhat = (spatial[c][at].astype(F32) - mean) * inv
            d_spatial = inv * (d_normed * gain - column[:, 0:1] - xhat * column[:, 1:2])
            g_gain = g_gain + jnp.sum(d_normed * xhat, axis=0, keepdims=True)
            g_shift = g_shift + jnp.sum(d_normed, axis=0, keepdims=True)
            g_bias = g_bias + jnp.sum(d_spatial, axis=0, keepdims=True)
            for a in range(block_rows):
                store_shifted(moved, first + a + 3, d_spatial[a * GRID_HI : (a + 1) * GRID_HI])
            first += block_rows

    @pl.loop(0, GRID_HI)
    def _(a):
        row = jnp.where(a < hi_valid, field_ref[a].astype(F32), 0.0)
        store_shifted(shifted, a + 3, row)

    g_kernel_ref[...] = jnp.zeros(g_kernel_ref.shape, F32)
    for s in range(7):
        def rows_of(i, sums):
            a0 = i * 2
            grads = [moved[3, a0 + o + 3] for o in range(2)]
            sums = list(sums)
            for r_in in range(8):
                value = shifted[s, a0 + r_in]
                for o in range(2):
                    r = r_in - o
                    if 0 <= r < 7:
                        product = value * grads[o]
                        sums[r] = sums[r] + jnp.sum(product.reshape(GRID_HI // 8, 8, cb), axis=0)
            return tuple(sums)

        sums = lax.fori_loop(0, GRID_HI // 2, rows_of, tuple(jnp.zeros((8, cb), F32) for _ in range(7)))
        for r in range(7):
            t = r * 7 + s
            g_kernel_ref[t : t + 1, :] = jnp.sum(sums[r], axis=0, keepdims=True)
    sums_ref[...] = jnp.concatenate([g_bias, g_gain, g_shift, jnp.zeros((5, cb), F32)], axis=0)

    for i in range(CELLS // CELL_BLOCK):
        each = CELLS // CELL_BLOCK // chunks
        lo = slice((i % each) * POOL_BLOCK, (i % each + 1) * POOL_BLOCK)
        refined = dot_tn(pool_ref[...], d_pooled[i // each][lo, :])
        shifted[0, i * block_rows : (i + 1) * block_rows] = refined.reshape(block_rows, GRID_HI, cb)

    @pl.loop(0, GRID_HI, step=4)
    def _(a0):
        sums = correlate(
            moved, a0, 4, lambda r, s: k_ref[48 - (r * 7 + s) : 49 - (r * 7 + s), :], jnp.zeros((GRID_HI, cb), F32)
        )
        for o in range(4):
            value = sums[o] + shifted[0, a0 + o]
            out_ref[a0 + o] = jnp.where(a0 + o < hi_valid, value, 0.0).astype(BF16)


def conv_backward(
    received, spatial, means, invs, d_pooled, hires, kernel, my_gain, total_channels, scalars, after=()
):
    chunks = len(received)
    channels = hires.shape[3]
    cb = channel_block(channels)
    cells = means[0].shape[0]

    def column(rows):
        return pl.BlockSpec((rows, cb), lambda j, s: (0, j))

    map_block = pl.BlockSpec((GRID_HI, GRID_HI, cb), lambda j, s: (0, 0, j))
    return call(
        functools.partial(conv_back_kernel, chunks, total_channels),
        "conv_backward",
        (channels // cb,),
        [column(cells + STAT_ROWS)] * chunks
        + [column(cells)] * chunks
        + [held((cells, LANES))] * (2 * chunks)
        + [column(d_pooled[0].shape[0])] * chunks
        + [
            pl.BlockSpec((None, GRID_HI, GRID_HI, cb), lambda j, s: (s[3], 0, 0, j)),
            column(49),
            column(1),
            held((POOL_BLOCK, CELL_BLOCK)),
        ],
        [
            (map_block, array((GRID_HI, GRID_HI, channels))),
            (column(49), array((49, channels), F32)),
            (column(8), array((8, channels), F32)),
        ],
        (*received, *spatial, *means, *invs, *d_pooled)
        + (hires, kernel, my_gain.reshape(1, -1), pool_block()),
        [pltpu.VMEM((7, GRID_HI + 6, GRID_HI, cb), F32)] * 2,
        after,
        prefetch=scalars,
    )


def vit_mlp_kernel(n_mp, scalars_ref, *refs):
    pieces, refs = refs[:n_mp], refs[n_mp:]
    x_ref, wo_hbm, ob_ref, gain_ref, shift_ref, w1_hbm, b1_ref, w2_hbm, dy_ref = refs[:9]
    hidden_ref, normed_ref, active_ref, inner_ref, bias_ref = refs[9:14]
    sends, refs = refs[14 : 14 + n_mp], refs[14 + n_mp :]
    d_normed, wo_ref, w1_ref, w2_ref, sems = refs
    step = pl.program_id(0)
    rows = x_ref.shape[0]
    cut = 256
    cuts = [slice(j * cut, (j + 1) * cut) for j in range(w1_ref.shape[1] // cut)]
    loads = [pltpu.make_async_copy(wo_hbm, wo_ref, sems.at[0])]
    for j, at in enumerate(cuts):
        loads.append(pltpu.make_async_copy(w1_hbm.at[:, at], w1_ref.at[:, at], sems.at[2 * j + 1]))
        loads.append(pltpu.make_async_copy(w2_hbm.at[at, :], w2_ref.at[at, :], sems.at[2 * j + 2]))

    @pl.when(step == 0)
    def _():
        for load in loads:
            load.start()
        loads[0].wait()

    hidden = x_ref[...].astype(F32) + ob_ref[...]
    for k in range(n_mp):
        hidden = hidden + dot(pieces[k][...], wo_ref[k])
    hidden_ref[...] = hidden
    xhat, _ = standardize(hidden, norm_epsilon)
    normed_ref[...] = (xhat * gain_ref[...] + shift_ref[...]).astype(BF16)

    @pl.when(step == 0)
    def _():
        for load in loads[1:]:
            load.wait()

    for j, at in enumerate(cuts):
        active, slope = gelu_pair(dot(normed_ref[...], w1_ref[:, at]) + b1_ref[:, at])
        active_ref[:, at] = active.astype(BF16)
        d_inner = (slope * dot_nt(dy_ref[...], w2_ref[at, :])).astype(BF16)
        inner_ref[:, at] = d_inner
        sums = jnp.sum(d_inner.astype(F32), axis=0, keepdims=True)

        @pl.when(step == 0)
        def _():
            bias_ref[:, at] = sums

        @pl.when(step > 0)
        def _():
            bias_ref[:, at] += sums

    d_normed[pl.ds(pl.multiple_of(step * rows, rows), rows), :] = dot_nt(inner_ref[...], w1_ref[...])

    @pl.when(step == pl.num_programs(0) - 1)
    def _():
        part = sends[0].shape[0]
        for k in range(n_mp):
            at = pl.multiple_of((scalars_ref[1] ^ k) * part, part)
            sends[k][...] = d_normed[pl.ds(at, part), :].astype(BF16)


def vit_mlp(
    tokens, attended_pieces, w_out_pieces, out_bias, gain, shift, w1, b1, w2, cotangent, scalars, after=()
):
    n_mp = len(attended_pieces)
    heads_width = attended_pieces[0].shape[1]
    width, hidden = w1.shape
    rows = TOKENS // 2
    image_rows = pl.BlockSpec((None, rows, width), lambda j, s: (s[3], j, 0))
    row = pl.BlockSpec((rows, width), lambda j, s: (j, 0))
    row_hidden = pl.BlockSpec((rows, hidden), lambda j, s: (j, 0))
    one = held((1, width))
    anywhere = pl.BlockSpec(memory_space=pl.ANY)
    send_shape = (TOKENS // n_mp, width)
    return call(
        functools.partial(vit_mlp_kernel, n_mp),
        "vit_mlp",
        (TOKENS // rows,),
        [pl.BlockSpec((rows, heads_width), lambda j, s: (j, 0))] * n_mp
        + [image_rows, anywhere, one, one, one, anywhere, held((1, hidden)), anywhere, image_rows],
        [
            (row, array((TOKENS, width), F32)),
            (row, array((TOKENS, width))),
            (row_hidden, array((TOKENS, hidden))),
            (row_hidden, array((TOKENS, hidden))),
            (whole((1, hidden)), array((1, hidden), F32)),
        ]
        + [(whole(send_shape), array(send_shape))] * n_mp,
        (*attended_pieces, tokens, w_out_pieces, out_bias.reshape(1, -1), gain.reshape(1, -1))
        + (shift.reshape(1, -1), w1, b1.reshape(1, -1), w2, cotangent),
        [
            pltpu.VMEM((TOKENS, width), F32),
            pltpu.VMEM((n_mp, heads_width, width), BF16),
            pltpu.VMEM((width, hidden), BF16),
            pltpu.VMEM((hidden, width), BF16),
            pltpu.SemaphoreType.DMA((1 + 2 * (hidden // 256),)),
        ],
        after,
        prefetch=scalars,
    )


def adapter_kernel(chunks, scalars_ref, *refs):
    parts, fields = refs[:chunks], refs[chunks : 2 * chunks]
    refs = refs[2 * chunks :]
    pb_ref, scale_ref, wa_ref, active_ref, w2_ref, gate_ref, dy_ref = refs[:7]
    pooled_ref, gate_sum_ref = refs[7:9]
    send_ref, total = refs[9:]
    first = 0
    for field in fields:
        rows = slice(first, first + field.shape[0])
        value = field[...] + scale_ref[...] * pb_ref[...]
        row = lax.broadcasted_iota(jnp.int32, value.shape, 0) + first
        value = jnp.where(row < scalars_ref[0] * GRID_LO, value, 0.0)
        pooled_ref[rows, :] = value.astype(BF16)
        first += field.shape[0]
    total[...] = dot(pooled_ref[...], wa_ref[...])
    first = 0
    for part in parts:
        total[first : first + part.shape[0], :] += part[...]
        first += part.shape[0]
    gate = gate_ref[...]
    adapted = total[...]
    sums = jnp.sum(dy_ref[...].astype(F32) * adapted, axis=0, keepdims=True)
    gate_sum_ref[...] = (1.0 - gate * gate) * sums
    total[...] = dot(active_ref[...], w2_ref[...]) + gate * adapted
    features = send_ref.shape[2]
    for g in range(send_ref.shape[0]):
        send_ref[g] = total[:, g * features : (g + 1) * features].astype(BF16)


def adapter(n_mp, parts, fields, pw2_bias, layer_scale, w_adapt, active, w2, gate, cotangent, scalars, after=()):
    channels, width = w_adapt.shape
    hidden = w2.shape[0]
    send_shape = (n_mp, TOKENS, width // n_mp)
    return call(
        functools.partial(adapter_kernel, len(fields)),
        "adapter",
        (1,),
        [held(v.shape) for v in (*parts, *fields)]
        + [held((1, channels)), held((1, channels)), held((channels, width))]
        + [held((TOKENS, hidden)), held((hidden, width)), held((1, width)), image(width)],
        [
            (held((TOKENS, channels)), array((TOKENS, channels))),
            (held((1, width)), array((1, width), F32)),
            (held(send_shape), array(send_shape)),
        ],
        (*parts, *fields, pw2_bias.reshape(1, -1), layer_scale.reshape(1, -1), w_adapt)
        + (active, w2, gate.reshape(1, -1), cotangent),
        [pltpu.VMEM((TOKENS, width), F32)],
        after,
        prefetch=scalars,
    )


def weight_grad_kernel(counts, block, scalars_ref, *refs):
    pairs = sum(counts)
    lefts, rights = refs[:pairs], refs[pairs : 2 * pairs]
    keep_ref, send_ref = refs[2 * pairs :]
    core = scalars_ref[2]
    at = 0
    used = sum(refs[pairs + sum(counts[:i])].shape[1] for i in range(len(counts)))
    if used < keep_ref.shape[2]:
        rest = jnp.zeros(keep_ref.shape[:2] + (keep_ref.shape[2] - used,), BF16)
        keep_ref[:, :, used:] = rest
        send_ref[:, :, used:] = rest
    first = 0
    for count in counts:
        total = dot_tn(lefts[first][...], rights[first][...])
        for i in range(first + 1, first + count):
            total = total + dot_tn(lefts[i][...], rights[i][...])
        first += count
        lanes = slice(at, at + total.shape[1])
        at += total.shape[1]
        total = total.astype(BF16)
        for q in range(keep_ref.shape[0]):
            halves = [total[(2 * q + h) * block : (2 * q + h + 1) * block] for h in range(2)]

            @pl.when(core == 0)
            def _():
                keep_ref[q, :, lanes] = halves[0]
                send_ref[q, :, lanes] = halves[1]

            @pl.when(core != 0)
            def _():
                keep_ref[q, :, lanes] = halves[1]
                send_ref[q, :, lanes] = halves[0]


def weight_grads(name, groups, grads, scalars, after=(), lanes=None):
    block = grads[0][0][0].shape[1] // groups
    pairs = [pair for grad in grads for pair in grad]
    quads = 1
    while (2 * block * quads) % LANES:
        quads += 1
    total = lanes or sum(grad[0][1].shape[1] for grad in grads)
    out = (
        pl.BlockSpec((quads, block, total), lambda j: (j, 0, 0)),
        array((groups // 2, block, total)),
    )
    return call(
        functools.partial(weight_grad_kernel, [len(grad) for grad in grads], block),
        name,
        (groups // 2 // quads,),
        [SCALARS]
        + [pl.BlockSpec((left.shape[0], 2 * block * quads), lambda j: (0, j)) for left, _ in pairs]
        + [held(right.shape) for _, right in pairs],
        [out, out],
        (scalars, *(left for left, _ in pairs), *(right for _, right in pairs)),
        after=after,
    )


def fold_kernel(_, *refs):
    count = len(refs) // 4
    for p in range(count):
        keep, got = refs[2 * p : 2 * p + 2]
        send, hold = refs[2 * (count + p) : 2 * (count + p) + 2]

        def total():
            return (keep[...].astype(F32) + got[...].astype(F32)).astype(BF16)

        @pl.when(pl.program_id(0) == 0)
        def _():
            send[...] = total().reshape(send.shape)

        @pl.when(pl.program_id(0) == 1)
        def _():
            hold[...] = total().reshape(hold.shape)


def fold(name, parts, scalars, after=()):
    ins, operands, outs = [], [], []
    for keep, got, dim, slot, lanes, block in parts:
        shape = list(keep.shape)
        shape[dim] //= 2
        shape[-1] = lanes
        assert keep.shape[dim] == 2

        def at(j, s, dim=dim, slot=slot, rank=len(shape), block=block):
            index = [0] * rank
            index[dim] = s[slot] ^ (1 - j)
            index[-1] = block
            return tuple(index)

        ins += [pl.BlockSpec(tuple(shape), at)] * 2
        operands += [keep, got]
        out = tuple(shape[:dim] + shape[dim + 1 :])
        outs += [(whole(out), array(out))] * 2
    return call(
        fold_kernel, name, (2,), ins, outs, operands, after=after, prefetch=scalars
    )


def norm2_back_kernel(n_mp, scalars_ref, *refs):
    got, refs = refs[:n_mp], refs[n_mp:]
    hidden_ref, dy_ref, gain_ref, d_attn_ref, sums_ref = refs
    d_normed = got[0][...].astype(F32)
    for value in got[1:]:
        d_normed = d_normed + value[...].astype(F32)
    xhat, inv = standardize(hidden_ref[...], norm_epsilon)
    dxhat = d_normed * gain_ref[...]
    d_hidden = dy_ref[...].astype(F32) + inv * (
        dxhat
        - jnp.mean(dxhat, axis=-1, keepdims=True)
        - xhat * jnp.mean(dxhat * xhat, axis=-1, keepdims=True)
    )
    d_attn = d_hidden.astype(BF16)
    d_attn_ref[...] = d_attn
    sums_ref[0:1, :] = jnp.sum(d_attn.astype(F32), axis=0, keepdims=True)
    sums_ref[1:2, :] = jnp.sum(d_normed * xhat, axis=0, keepdims=True)
    sums_ref[2:3, :] = jnp.sum(d_normed, axis=0, keepdims=True)
    sums_ref[3:, :] = jnp.zeros((5, sums_ref.shape[1]), F32)


def norm2_backward(got, hidden, cotangent, gain, scalars, after=()):
    n_mp = len(got)
    rows, width = got[0].shape
    mine = pl.BlockSpec((None, rows, width), lambda j, s: (s[1], 0, 0))
    image_rows = pl.BlockSpec((None, None, rows, width), lambda j, s: (s[3], s[1], 0, 0))
    return call(
        functools.partial(norm2_back_kernel, n_mp),
        "norm2_backward",
        (1,),
        [held((rows, width))] * n_mp + [mine, image_rows, held((1, width))],
        [
            (held((rows, width)), array((rows, width))),
            (held((8, width)), array((8, width), F32)),
        ],
        (*got, hidden.reshape(n_mp, rows, width), cotangent.reshape(-1, n_mp, rows, width))
        + (gain.reshape(1, -1),),
        after=after,
        prefetch=scalars,
    )


def norm1_back_kernel(n_mp, scalars_ref, *refs):
    got, refs = refs[:n_mp], refs[n_mp:]
    x_ref, mine_ref, d_attn_ref, gain_ref, dy_ref, keep_ref, send_ref, sums_ref, total = refs
    width = x_ref.shape[1]
    value = got[0][...].astype(F32)
    for piece in got[1:]:
        value = value + piece[...].astype(F32)
    d_normed, stats = value[:TOKENS], value[TOKENS:, :LANES]
    count = -(-TOKENS // LANES)
    rows = [
        jnp.concatenate([stats[k * count + t : k * count + t + 1] for t in range(count)], axis=1)
        for k in range(2)
    ]
    rows.append(jnp.zeros((LANES - 2, count * LANES), F32))
    columns = jnp.concatenate(rows, axis=0).T[:TOKENS] * (1.0 / width)
    x = x_ref[...].astype(F32)
    mean = jnp.mean(x, axis=-1, keepdims=True)
    inv = lax.rsqrt(jnp.mean((x - mean) * (x - mean), axis=-1, keepdims=True) + norm_epsilon)
    xhat = (mine_ref[...].astype(F32) - mean) * inv
    total[...] = d_attn_ref[...].astype(F32) + inv * (
        d_normed * gain_ref[...] - columns[:, 0:1] - xhat * columns[:, 1:2]
    )
    half = TOKENS // 2
    path = scalars_ref[3]
    keep_ref[...] = total[pl.ds(pl.multiple_of(path * half, half), half), :].astype(BF16)
    send_ref[...] = total[pl.ds(pl.multiple_of((1 - path) * half, half), half), :].astype(BF16)
    sums_ref[0:1, :] = jnp.sum(d_normed * xhat, axis=0, keepdims=True)
    sums_ref[1:2, :] = jnp.sum(d_normed, axis=0, keepdims=True)
    sums_ref[2:3, :] = jnp.sum(dy_ref[...].astype(F32), axis=0, keepdims=True)
    sums_ref[3:, :] = jnp.zeros((5, sums_ref.shape[1]), F32)


def norm1_backward(got, tokens, d_attn, gain, cotangent, scalars, after=()):
    rows, features = got[0].shape
    width = tokens.shape[2]
    mine = pl.BlockSpec((TOKENS, features), lambda j, s: (0, s[1]))
    mine_of = pl.BlockSpec((None, TOKENS, features), lambda j, s: (s[3], 0, s[1]))
    half = (held((TOKENS // 2, features)), array((TOKENS // 2, features)))
    return call(
        functools.partial(norm1_back_kernel, len(got)),
        "norm1_backward",
        (1,),
        [held((rows, features))] * len(got)
        + [image(width), mine_of, mine]
        + [pl.BlockSpec((1, features), lambda j, s: (0, s[1])), mine_of],
        [half, half, (held((8, features)), array((8, features), F32))],
        (*got, tokens, tokens, d_attn, gain.reshape(1, -1), cotangent),
        [pltpu.VMEM((TOKENS, features), F32)],
        after=after,
        prefetch=scalars,
    )


def output_kernel(n_mp, scalars_ref, *refs):
    got, refs = refs[:n_mp], refs[n_mp:]
    hidden_ref, bias_ref, keep_ref, send_ref, total = refs
    value = hidden_ref[...] + bias_ref[...]
    for piece in got:
        value = value + piece[...].astype(F32)
    total[...] = value
    half = TOKENS // 2
    path = scalars_ref[3]
    keep_ref[...] = total[pl.ds(pl.multiple_of(path * half, half), half), :].astype(BF16)
    send_ref[...] = total[pl.ds(pl.multiple_of((1 - path) * half, half), half), :].astype(BF16)


def output_halves(got, hidden, fc2_bias, scalars, after=()):
    n_mp = len(got)
    features = got[0].shape[1]
    half = (held((TOKENS // 2, features)), array((TOKENS // 2, features)))
    return call(
        functools.partial(output_kernel, n_mp),
        "output_halves",
        (1,),
        [held((TOKENS, features))] * n_mp
        + [pl.BlockSpec((TOKENS, features), lambda j, s: (0, s[1]))]
        + [pl.BlockSpec((1, features), lambda j, s: (0, s[1]))],
        [half, half],
        (*got, hidden, fc2_bias.reshape(1, -1)),
        [pltpu.VMEM((TOKENS, features), F32)],
        after=after,
        prefetch=scalars,
    )


WIDE_ROWS = 7


def slots_of(shapes, width):
    row, lane, slots = 0, 0, []
    for rows, n in shapes:
        mine = []
        for _ in range(rows):
            pieces = []
            for at in range(0, n, width):
                size = min(width, n - at)
                if lane + size > width:
                    row, lane = row + 1, 0
                pieces.append((row, lane, at, size))
                lane += size
            mine.append(pieces)
        slots.append(mine)
    return slots, -(-(row + 1) // 8) * 8


def pack_kernel(n_mp, slots, s_ref, *refs):
    wide, refs = refs[:n_mp], refs[n_mp:]
    sums_ref, bias_ref, scale_ref, *arrays, packed_ref, total_ref = refs
    packed_ref[...] = jnp.zeros(packed_ref.shape, F32)
    total = wide[0][...]
    for piece in wide[1:]:
        total = total + piece[...]
    total_ref[...] = total
    channels = scale_ref.shape[1]
    mine = total_ref[pl.ds(WIDE_ROWS + s_ref[1], 1), :][:, :channels]
    g_scale = mine / scale_ref[...] + bias_ref[...] * sums_ref[1:2, :]
    values = [total[:WIDE_ROWS], g_scale, sums_ref[0:1, :]] + [v[...] for v in arrays]
    for value, mine in zip(values, slots):
        for r, pieces in enumerate(mine):
            for row, lane, at, n in pieces:
                packed_ref[row : row + 1, lane : lane + n] = value[r : r + 1, at : at + n]


def pack(wide_pieces, sums, pw2_bias, layer_scale, arrays, rows, scalars, after=()):
    n_mp = len(wide_pieces)
    width = wide_pieces[0].shape[1]
    channels = sums.shape[1]
    shapes = [(WIDE_ROWS, width), (1, channels), (1, channels)]
    shapes += [(count, v.shape[1]) for v, count in zip(arrays, rows)]
    slots, total = slots_of(shapes, width)
    operands = (*wide_pieces, sums, pw2_bias.reshape(1, -1), layer_scale.reshape(1, -1), *arrays)
    packed = call(
        functools.partial(pack_kernel, n_mp, slots),
        "pack",
        (1,),
        [held(v.shape) for v in operands],
        [(held((total, width)), array((total, width), F32))],
        operands,
        [pltpu.VMEM(wide_pieces[0].shape, F32)],
        after=after,
        prefetch=scalars,
    )[0]
    return packed, slots


def unpack_kernel(slots, a_ref, b_ref, *outs):
    for out, mine in zip(outs, slots):
        for r, pieces in enumerate(mine):
            for row, lane, at, n in pieces:
                out[r : r + 1, at : at + n] = (
                    a_ref[row : row + 1, lane : lane + n] + b_ref[row : row + 1, lane : lane + n]
                )


def unpack(a, b, slots, after=()):
    shapes = [(len(mine), sum(n for *_, n in mine[0])) for mine in slots]
    return call(
        functools.partial(unpack_kernel, slots),
        "unpack",
        (1,),
        [held(a.shape)] * 2,
        [(held(shape), array(shape, F32)) for shape in shapes],
        (a, b),
        after=after,
    )


def swap(value, axis, apart):
    n = lax.axis_size(axis)
    return lax.ppermute(value, axis, [(i, i ^ apart) for i in range(n)])


def pick(value, axis, index):
    return lax.dynamic_index_in_dim(value, index, axis, keepdims=False)


def gathered(value, axis):
    return [value] + [swap(value, axis, k) for k in range(1, lax.axis_size(axis))]


def exchanged(blocks, axis):
    return blocks[:1] + [swap(block, axis, k) for k, block in enumerate(blocks) if k]


def in_order(values, axis):
    me = lax.axis_index(axis)
    apart = 1
    while apart < len(values):
        turned = (me & apart) > 0
        values = [jnp.where(turned, values[i ^ apart], values[i]) for i in range(len(values))]
        apart *= 2
    return values


def spread(value, steps):
    for axis, apart, place in steps:
        other = swap(value, axis, apart)
        turned = (lax.axis_index(axis) & apart) > 0
        pair = [jnp.where(turned, other, value), jnp.where(turned, value, other)]
        value = jnp.stack(pair, axis=place)
    return value.reshape(value.shape[0], -1, value.shape[-1])


def halve(value, dim, axis, apart, bit):
    received = swap(pick(value, dim, 1 - bit), axis, apart)
    return pick(value, dim, bit).astype(F32) + received.astype(F32)


def across(halves):
    keep, send = halves
    return keep, swap(send, "dp", 1)


def first_fold(name, halves, scalars, after, dp_first=False):
    n_path, n_dp = lax.axis_size("path"), lax.axis_size("dp")
    block, lanes = halves[0].shape[1:]
    shape = (n_path, n_dp // 4, 2, block, lanes)
    keep, got = (half.reshape(shape) for half in halves)
    dim, slot = (2, 4) if dp_first else (0, 3)
    send, hold = fold(name, [(keep, got, dim, slot, lanes, 0)], scalars, after)
    return hold, swap(send, *(("dp", 2) if dp_first else ("path", 1))), dp_first


def second_fold(name, part, scalars, after):
    hold, got, path_next = part
    dim, slot = (0, 3) if path_next else (1, 4)
    send, hold = fold(name, [(hold, got, dim, slot, hold.shape[-1], 0)], scalars, after)
    return hold, swap(send, *(("path", 1) if path_next else ("dp", 2)))


def last_sum(hold, got):
    n_dp, me_dp = lax.axis_size("dp"), lax.axis_index("dp")
    value = hold.astype(F32) + got.astype(F32)
    size = value.shape[0]
    b = 2
    while size > 1:
        size //= 2
        shape = (size, 2) + value.shape[1:]
        value = halve(value.astype(BF16).reshape(shape), 1, "dp", 1 << b, (me_dp >> b) & 1)
        b += 1
    return value[0]


def summed_at_once(value, axis):
    return sum(gathered(value, axis))


def summed(value, axes):
    for axis in axes:
        apart = 1
        while apart < lax.axis_size(axis):
            value = value + swap(value, axis, apart)
            apart *= 2
    return value


def body(
    tokens,
    hires,
    valid_rows,
    cotangent,
    attention_norm_gain,
    attention_norm_bias,
    w_qkv,
    qv_bias,
    w_out,
    out_bias,
    mlp_norm_gain,
    mlp_norm_bias,
    w_fc1,
    fc1_bias,
    down_weight,
    fc2_bias,
    w_adapt,
    gate_param,
    dw_kernel,
    dw_bias,
    channel_norm_gain,
    channel_norm_bias,
    w_pw1,
    pw1_bias,
    w_pw2,
    pw2_bias,
    layer_scale,
):
    path = lax.axis_index("path")
    n_path = lax.axis_size("path")
    dp = lax.axis_index("dp")
    mp = lax.axis_index("mp")
    n_mp = lax.axis_size("mp")
    groups = n_path * lax.axis_size("dp")
    assert tokens.shape[0] == n_path == 2
    width = tokens.shape[2]
    heads_width = w_qkv.shape[2]
    features = width // n_mp
    channels = hires.shape[3]
    all_channels = w_pw1.shape[0]
    part_rows = TOKENS // n_mp
    chunk_rows = GRID_HI // CHUNKS

    valid = pick(valid_rows, 0, path)
    hi_valid = (valid * GRID_HI + GRID_LO - 1) // GRID_LO
    rank = path * lax.axis_size("dp") + dp
    scalars = jnp.stack([valid, mp, dp & 1, path, (dp >> 1) & 1, hi_valid, rank])
    gate = jnp.tanh(gate_param)

    def my_features(v):
        return lax.dynamic_slice_in_dim(v, mp * features, features, v.ndim - 1)

    rows, rows_all, pooled_field, d_pooled, d_adapted = [], [], [], [], []
    front_sums, ranks = 0.0, []
    last = ()
    for c in range(CHUNKS):
        send, *chunk, sums, rank_out = front(
            hires,
            dw_kernel,
            dw_bias,
            cotangent,
            gate,
            w_adapt,
            layer_scale,
            scalars,
            c * chunk_rows,
            chunk_rows,
            last,
        )
        last = (sums,)
        front_sums = front_sums + sums
        ranks.append(rank_out)
        rows.append(send)
        rows_all.append(lax.all_gather(send, "mp", axis=0, tiled=False))
        for kept, value in zip((pooled_field, d_pooled, d_adapted), chunk):
            kept.append(value)

    rank = ranks[-1][0, 0]
    out_rows, adapt_rows = heads_width // groups, channels // groups
    scaled = w_adapt.astype(F32) * layer_scale[:, None]
    share = jnp.concatenate(
        [
            lax.dynamic_slice_in_dim(w_out, rank * out_rows, out_rows, 0),
            lax.dynamic_slice_in_dim(scaled, rank * adapt_rows, adapt_rows, 0).astype(BF16),
        ]
    )
    shares = gathered(share, "mp")
    chips = [("dp", 1 << b, -3) for b in range(lax.axis_size("dp").bit_length() - 2, 0, -1)]
    w_out_pieces = spread(
        jnp.stack([v[:out_rows] for v in shares]), [("path", 1, -3)] + chips + [("dp", 1, -3)]
    )
    w_adapt_all = spread(
        jnp.stack(in_order([v[out_rows:] for v in shares], "mp")),
        chips + [("path", 1, 1), ("dp", 1, -3)],
    ).reshape(all_channels, width)

    w_flat = w_qkv.reshape(width, 3 * heads_width)
    normed1, query, keys, values, attended = attention_forward(
        tokens, attention_norm_gain, attention_norm_bias, w_flat, qv_bias, scalars, last + tuple(rows_all[:1])
    )
    attended_pieces = gathered(attended, "mp")
    last = (attended,)

    def conv(c, after):
        out = conv_mlp(
            rows_all[c],
            channel_norm_gain,
            channel_norm_bias,
            w_pw1,
            pw1_bias,
            w_pw2,
            w_adapt_all,
            d_adapted[c],
            c,
            scalars,
            after,
        )
        return out, lax.psum_scatter(out[4], "mp", scatter_dimension=0, tiled=False), (out[7],)

    conv_out, received = [], []
    out, got, last = conv(0, last)
    conv_out.append(out)
    received.append(got)
    hidden1, normed2, fc_active, d_fc_inner, g_fc1_bias, *sends = vit_mlp(
        tokens,
        attended_pieces,
        w_out_pieces,
        out_bias,
        mlp_norm_gain,
        mlp_norm_bias,
        w_fc1,
        fc1_bias,
        down_weight,
        cotangent,
        scalars,
        last,
    )
    d_normed2_pieces = exchanged(sends, "mp")
    last = (g_fc1_bias,)
    for c in range(1, CHUNKS):
        out, got, last = conv(c, last)
        conv_out.append(out)
        received.append(got)
    (
        conv_normed,
        conv_inner,
        pooled_active,
        backs,
        _,
        means,
        invs,
        bias_sums,
        branches,
        adapted_parts,
        scale_sums,
    ) = zip(*conv_out)
    g_pw1_bias = sum(bias_sums)

    pooled, g_gate, send = adapter(
        n_mp,
        adapted_parts,
        pooled_field,
        pw2_bias,
        layer_scale,
        w_adapt,
        fc_active,
        down_weight,
        gate,
        cotangent,
        scalars,
        last + tuple(received[:-1]),
    )
    branch_sum = lax.psum_scatter(send, "mp", scatter_dimension=0, tiled=False)
    d_attn_part, norm2_sums = norm2_backward(
        d_normed2_pieces, hidden1, cotangent, mlp_norm_gain, scalars, (g_gate,)
    )
    d_attn_pieces = gathered(d_attn_part, "mp")
    dy = pick(cotangent, 0, path)
    fc_halves = across(
        weight_grads(
            "grad_fc",
            groups,
            [[(normed2, d_fc_inner)], [(dy, fc_active)]],
            scalars,
            (norm2_sums,),
        )
    )
    pooled_rows = d_adapted[0].shape[0]
    pooled_cuts = [pooled[c * pooled_rows : (c + 1) * pooled_rows] for c in range(CHUNKS)]
    adapt_halves = across(
        weight_grads(
            "grad_adapt",
            groups,
            [list(zip(d_adapted, branches)), list(zip(d_adapted, pooled_cuts))],
            scalars,
            fc_halves[:1],
        )
    )
    pw2_halves = across(
        weight_grads(
            "grad_pw2", groups, [list(zip(backs, pooled_active))], scalars, adapt_halves[:1]
        )
    )
    pw1_halves = across(
        weight_grads(
            "grad_pw1", groups, [list(zip(conv_normed, conv_inner))], scalars, pw2_halves[:1]
        )
    )

    d_attn, d_query, d_keys, d_values, send = attention_backward(
        n_mp,
        tokens,
        attention_norm_gain,
        d_attn_pieces,
        w_out,
        query,
        keys,
        values,
        w_flat,
        scalars,
        pw1_halves[:1],
    )
    d_normed1 = lax.psum_scatter(send, "mp", scatter_dimension=0, tiled=False)
    fc_part = first_fold("fold_fc", fc_halves, scalars, (d_query, *received[1:]))
    adapt_part = first_fold("fold_adapt", adapt_halves, scalars, fc_part[:1], True)
    pw2_part = first_fold("fold_pw2", pw2_halves, scalars, adapt_part[:1], True)
    pw1_part = first_fold("fold_pw1", pw1_halves, scalars, pw2_part[:1])
    qkv_halves = across(
        weight_grads(
            "grad_qkv",
            groups,
            [
                [(normed1, d_query)],
                [(normed1, d_keys)],
                [(normed1, d_values)],
                [(d_attn, attended)],
            ],
            scalars,
            pw1_part[:1],
        )
    )
    g_qv_bias = jnp.stack(
        [jnp.sum(d_query.astype(F32), axis=0), jnp.sum(d_values.astype(F32), axis=0)]
    )

    tokens_keep, tokens_send, norm1_sums = norm1_backward(
        [d_normed1],
        tokens,
        d_attn,
        attention_norm_gain,
        cotangent,
        scalars,
        qkv_halves[:1],
    )

    def placed(v):
        return lax.dynamic_update_slice(jnp.zeros((width,), F32), v, (mp * features,))

    scale_rows = jnp.pad(sum(scale_sums).reshape(n_mp, channels), ((0, 0), (0, width - channels)))
    wide = jnp.concatenate(
        [norm2_sums[:3]]
        + [placed(norm1_sums[i])[None] for i in range(3)]
        + [g_gate, scale_rows]
    )
    wide_pieces = gathered(wide, "mp")
    d_field, g_kernel, conv_sums = conv_backward(
        received,
        rows,
        means,
        invs,
        d_pooled,
        hires,
        dw_kernel,
        lax.dynamic_slice_in_dim(channel_norm_gain, mp * channels, channels, 0),
        all_channels,
        scalars,
        (norm1_sums, fc_part[1], adapt_part[1]),
    )

    packed, slots = pack(
        wide_pieces,
        front_sums,
        pw2_bias,
        layer_scale,
        [g_qv_bias, g_fc1_bias, g_pw1_bias, g_kernel, conv_sums],
        (2, 1, 1, 49, 3),
        scalars,
        (conv_sums,),
    )
    packed_first = packed
    packed = summed(packed, ("dp",))
    output_keep, output_send = output_halves(
        [branch_sum], hidden1, fc2_bias, scalars, (packed_first, pw2_part[1], pw1_part[1])
    )
    adapt_part = second_fold("fold_adapt_last", adapt_part, scalars, (output_keep,))
    fc_part = second_fold("fold_fc_last", fc_part, scalars, adapt_part[:1])
    pw2_part = second_fold("fold_pw2_last", pw2_part, scalars, fc_part[:1])
    pw1_part = second_fold("fold_pw1_last", pw1_part, scalars, pw2_part[:1])
    qkv_part = first_fold("fold_qkv", qkv_halves, scalars, pw1_part[:1], True)
    qkv_part = second_fold("fold_qkv_last", qkv_part, scalars, qkv_part[:1])

    def both_images(mine, send):
        other = swap(send, "path", 1)
        first = path == 0
        return jnp.stack([jnp.where(first, mine, other), jnp.where(first, other, mine)])

    def keep_half(rows):
        halves = rows.reshape((2, rows.shape[0] // 2) + rows.shape[1:])
        return both_images(pick(halves, 0, path), pick(halves, 0, 1 - path))

    output = both_images(output_keep, output_send)
    tokens_grad = both_images(tokens_keep, tokens_send)
    hires_grad = keep_half(d_field)

    g_adapt = last_sum(*adapt_part)
    g_adapt_mine = sum(
        piece.astype(F32)
        for piece in exchanged(
            [
                lax.dynamic_slice_in_dim(g_adapt, (mp ^ k) * channels, channels, 1).astype(BF16)
                for k in range(n_mp)
            ],
            "mp",
        )
    )
    g_adapt_mine = g_adapt_mine * layer_scale + g_adapt[:, all_channels:]
    g_fc = last_sum(*fc_part)
    g_fc1_mine, g_fc2_mine = g_fc[:, : w_fc1.shape[1]], g_fc[:, w_fc1.shape[1] :]
    g_pw1_mine, g_pw2_mine = last_sum(*pw1_part), last_sum(*pw2_part)
    g_rest = last_sum(*qkv_part)
    g_qkv_mine = g_rest[:, : 3 * heads_width].reshape(-1, 3, heads_width)
    g_out_mine = g_rest[:, 3 * heads_width :]

    small = unpack(packed, swap(packed, "path", 1), slots)
    wide, g_scale, g_pw2_bias, g_qv_bias, g_fc1_bias, g_pw1_bias, g_kernel, conv_sums = small
    g_out_bias, g_norm2_gain, g_norm2_bias, g_norm1_gain, g_norm1_bias, g_fc2_bias, g_gate = wide
    g_dw_bias, g_cnorm_gain, g_cnorm_bias = conv_sums
    return (
        output,
        tokens_grad,
        hires_grad,
        g_norm1_gain,
        g_norm1_bias,
        g_qkv_mine,
        g_qv_bias,
        g_out_mine.T,
        g_out_bias,
        g_norm2_gain,
        g_norm2_bias,
        g_fc1_mine,
        g_fc1_bias[0],
        g_fc2_mine.T,
        g_fc2_bias,
        g_adapt_mine.T,
        g_gate,
        g_kernel,
        g_dw_bias,
        g_cnorm_gain,
        g_cnorm_bias,
        g_pw1_mine,
        g_pw1_bias[0],
        g_pw2_mine.T,
        g_pw2_bias[0],
        g_scale[0],
    )


def solution(mesh):
    in_specs = (
        P("dp", None, None),
        P("dp", None, None, "mp"),
        P("dp"),
        P("dp", None, None),
        P(),
        P(),
        P(None, None, "mp"),
        P(None, "mp"),
        P("mp", None),
        P(),
        P(),
        P(),
        P(None, "mp"),
        P("mp"),
        P("mp", None),
        P(),
        P("mp", None),
        P(),
        P(None, "mp"),
        P("mp"),
        P(),
        P(),
        P(None, "mp"),
        P("mp"),
        P("mp", None),
        P("mp"),
        P("mp"),
    )
    out_specs = (
        P("dp", "path", "mp"),
        P("dp", "path", "mp"),
        P("dp", "path", None, "mp"),
        P(),
        P(),
        P(("path", "dp"), None, "mp"),
        P(None, "mp"),
        P("mp", ("path", "dp")),
        P(),
        P(),
        P(),
        P(("path", "dp"), "mp"),
        P("mp"),
        P("mp", ("path", "dp")),
        P(),
        P("mp", ("path", "dp")),
        P(),
        P(None, "mp"),
        P("mp"),
        P("mp"),
        P("mp"),
        P(("path", "dp"), "mp"),
        P("mp"),
        P("mp", ("path", "dp")),
        P("mp"),
        P("mp"),
    )
    return jax.shard_map(body, mesh=mesh, in_specs=in_specs, out_specs=out_specs, check_vma=False)
```

```python
import functools

import jax
import jax.numpy as jnp
import numpy as np
from jax import lax
from jax.experimental import pallas as pl
from jax.experimental.pallas import tpu as pltpu
from jax.sharding import PartitionSpec as P

HEAD_DIM = 64
GRID_LO = 24
GRID_HI = 32
TOKENS = GRID_LO * GRID_LO
CELLS = GRID_HI * GRID_HI
LANES = 128
STAT_ROWS = 16
CELL_BLOCK = 256
POOL_BLOCK = CELL_BLOCK * 9 // 16

norm_epsilon = 1e-05
channel_epsilon = 1e-06
F32 = jnp.float32
BF16 = jnp.bfloat16
VMEM_BYTES = 60 * 1024 * 1024
CHUNKS = 2


def gelu_pair(v):
    c = 0.7978845608028654
    square = v * v
    t = jnp.tanh(c * v * (1.0 + 0.044715 * square))
    half = 0.5 + 0.5 * t
    return v * half, half + (0.5 * c) * v * (1.0 - t * t) * (1.0 + 3 * 0.044715 * square)


def pool_rows(lo, hi):
    ratio = hi / lo
    target = np.arange(lo, dtype=np.float64)[:, None]
    source = np.arange(hi, dtype=np.float64)[None, :]
    lower = np.maximum(source, target * ratio)
    upper = np.minimum(source + 1.0, (target + 1.0) * ratio)
    return np.round(np.maximum(upper - lower, 0.0) / ratio * 4) / 4


def pool_block():
    rows = CELL_BLOCK // GRID_HI
    return jnp.asarray(np.kron(pool_rows(rows * 3 // 4, rows), pool_rows(GRID_LO, GRID_HI)), BF16)


def dot(a, b):
    return jnp.dot(a, b, preferred_element_type=F32)


def dot_nt(a, b):
    return lax.dot_general(a, b, (((1,), (1,)), ((), ())), preferred_element_type=F32)


def dot_tn(a, b):
    return lax.dot_general(a, b, (((0,), (0,)), ((), ())), preferred_element_type=F32)


def standardize(v, eps):
    centred = v - jnp.mean(v, axis=-1, keepdims=True)
    inv = lax.rsqrt(jnp.mean(centred * centred, axis=-1, keepdims=True) + eps)
    return centred * inv, inv


KERNEL_US = {
    "front": 0.5,
    "attention_forward": 10,
    "conv_mlp": 0.5,
    "vit_mlp": 33,
    "norm2_backward": 0.5,
    "attention_backward": 31,
    "norm1_backward": 0.5,
    "adapter": 0.5,
    "conv_backward": 0.5,
    "output_halves": 3,
    "pack": 3,
    "unpack": 3,
    "grad_fc": 0.5,
    "grad_pw1": 0.5,
    "grad_pw2": 0.5,
    "grad_qkv": 0.5,
    "grad_adapt": 0.5,
    "fold_fc": 0.5,
    "fold_pw1": 0.5,
    "fold_pw2": 0.5,
    "fold_qkv": 3,
    "fold_adapt": 0.5,
    "fold_fc_last": 3,
    "fold_pw1_last": 3,
    "fold_pw2_last": 3,
    "fold_qkv_last": 3,
    "fold_adapt_last": 3,
}
FLOPS_PER_US = 1.15e9


def call(
    kernel, name, grid, ins, outs, operands, scratch=(), after=(), prefetch=None
):
    lead = 0 if prefetch is None else 1
    count = lead + len(ins)

    def run(*refs):
        kernel(*refs[:count], *refs[count + len(after) :])

    in_specs = list(ins) + [pl.BlockSpec(memory_space=pl.ANY)] * len(after)
    return pl.pallas_call(
        run,
        grid_spec=pltpu.PrefetchScalarGridSpec(
            num_scalar_prefetch=lead,
            grid=grid,
            in_specs=in_specs,
            out_specs=[spec for spec, _ in outs],
            scratch_shapes=list(scratch),
        ),
        out_shape=[shape for _, shape in outs],
        compiler_params=pltpu.CompilerParams(
            dimension_semantics=("arbitrary",) * len(grid), vmem_limit_bytes=VMEM_BYTES
        ),
        name=name,
        cost_estimate=pl.CostEstimate(
            flops=int(KERNEL_US[name] * FLOPS_PER_US), bytes_accessed=1, transcendentals=0
        ),
    )(*(() if prefetch is None else (prefetch,)), *operands, *after)


SCALARS = pl.BlockSpec(memory_space=pltpu.SMEM)


def array(shape, dtype=BF16):
    return jax.ShapeDtypeStruct(shape, dtype)


def held(shape):
    return pl.BlockSpec(shape, lambda *_: (0,) * len(shape), pipeline_mode=pl.Buffered(1))


def whole(shape):
    return pl.BlockSpec(shape, lambda *_: (0,) * len(shape))


def rows_to_lanes(columns):
    rows = columns[0].shape[0]
    lane = lax.broadcasted_iota(jnp.int32, (rows, LANES), 1)
    packed = jnp.zeros((rows, LANES), F32)
    for i, column in enumerate(columns):
        packed = jnp.where(lane == i, column, packed)
    return packed.T


def stat_rows(columns, width):
    lanes = rows_to_lanes(columns)
    pieces = [
        lanes[i : i + 1, t * LANES : (t + 1) * LANES]
        for i in range(2)
        for t in range(lanes.shape[1] // LANES)
    ]
    pieces.append(jnp.zeros((STAT_ROWS - len(pieces), LANES), F32))
    stats = jnp.concatenate(pieces, axis=0).astype(BF16)
    if width % LANES:
        return jnp.concatenate([stats, jnp.zeros((STAT_ROWS, width - LANES), BF16)], axis=1)
    return jnp.concatenate([stats] * (width // LANES), axis=1)


def channel_block(channels):
    return LANES if channels % LANES == 0 else channels


def store_shifted(shifted, a, row):
    column = lax.broadcasted_iota(jnp.int32, row.shape, 0)
    for s in range(7):
        move = s - 3
        if move == 0:
            shifted[s, a] = row
        else:
            rolled = pltpu.roll(row, (-move) % GRID_HI, 0)
            inside = (column + move >= 0) & (column + move < GRID_HI)
            shifted[s, a] = jnp.where(inside, rolled, 0.0)


def correlate(shifted, a0, count, taps, start):
    sums = [start] * count
    for r_in in range(count + 6):
        for s in range(7):
            value = shifted[s, a0 + r_in]
            for o in range(count):
                r = r_in - o
                if 0 <= r < 7:
                    sums[o] = sums[o] + value * taps(r, s)
    return sums


def front_kernel(
    base, count, s_ref, field_ref, k_ref, bias_ref, pool_ref, dy_ref, gate_ref, wa_ref, scale_ref,
    send_ref, field_pooled_ref, d_pooled_ref, d_adapted_ref, sums_ref, rank_ref, shifted,
):
    hi_valid = s_ref[5]
    cb = field_ref.shape[2]
    rank_ref[...] = jnp.full(rank_ref.shape, s_ref[6], jnp.int32)

    @pl.when(pl.program_id(0) == 0)
    def _():
        d_adapted_ref[...] = (gate_ref[...] * dy_ref[...].astype(F32)).astype(BF16)

    @pl.loop(0, count + 6)
    def _(a):
        source = base + a - 3
        keep = (source >= 0) & (source < hi_valid)
        row = field_ref[jnp.clip(source, 0, GRID_HI - 1)].astype(F32)
        store_shifted(shifted, a, jnp.where(keep, row, 0.0))

    start = jnp.broadcast_to(bias_ref[...], (GRID_HI, cb))

    @pl.loop(0, count, step=4)
    def _(a0):
        sums = correlate(
            shifted, a0, 4, lambda r, s: k_ref[r * 7 + s : r * 7 + s + 1, :], start
        )
        for o in range(4):
            at = pl.multiple_of((a0 + o) * GRID_HI, GRID_HI)
            send_ref[pl.ds(at, GRID_HI), :] = sums[o].astype(BF16)

    block_rows = CELL_BLOCK // GRID_HI
    for i in range(count // block_rows):
        first = base + i * block_rows
        rows = field_ref[first : first + block_rows]
        row = lax.broadcasted_iota(jnp.int32, rows.shape, 0) + first
        rows = jnp.where(row < hi_valid, rows.astype(F32), 0.0).astype(BF16)
        field_pooled_ref[i * POOL_BLOCK : (i + 1) * POOL_BLOCK] = dot(
            pool_ref[...], rows.reshape(CELL_BLOCK, cb)
        )
    d_pooled = dot_nt(d_adapted_ref[...], wa_ref[...]).astype(BF16).astype(F32)
    row = lax.broadcasted_iota(jnp.int32, d_pooled.shape, 0) + base * GRID_HI * 9 // 16
    d_pooled = jnp.where(row < s_ref[0] * GRID_LO, d_pooled, 0.0)
    d_pooled_ref[...] = d_pooled.astype(BF16)
    scaled = (d_pooled * scale_ref[...]).astype(BF16)
    sums_ref[0:1, :] = jnp.sum(scaled.astype(F32), axis=0, keepdims=True)
    sums_ref[1:2, :] = jnp.sum(d_pooled, axis=0, keepdims=True)
    sums_ref[2:, :] = jnp.zeros((6, cb), F32)


def front(hires, kernel, bias, cotangent, gate, w_adapt, layer_scale, scalars, base, count, after=()):
    channels = hires.shape[3]
    width = cotangent.shape[2]
    cb = channel_block(channels)
    cells = count * GRID_HI
    pooled_rows = cells * 9 // 16
    chunk = base // count

    def column(rows):
        return pl.BlockSpec((rows, cb), lambda j, s: (0, j))

    return call(
        functools.partial(front_kernel, base, count),
        "front",
        (channels // cb,),
        [
            pl.BlockSpec((None, GRID_HI, GRID_HI, cb), lambda j, s: (s[3], 0, 0, j)),
            column(49),
            column(1),
            held((POOL_BLOCK, CELL_BLOCK)),
            pl.BlockSpec((None, pooled_rows, width), lambda j, s: (s[3], chunk, 0)),
            held((1, width)),
            pl.BlockSpec((cb, width), lambda j, s: (j, 0)),
            column(1),
        ],
        [
            (column(cells), array((cells, channels))),
            (column(pooled_rows), array((pooled_rows, channels), F32)),
            (column(pooled_rows), array((pooled_rows, channels))),
            (whole((pooled_rows, width)), array((pooled_rows, width))),
            (column(8), array((8, channels), F32)),
            (whole((8, LANES)), array((8, LANES), jnp.int32)),
        ],
        (hires, kernel, bias.reshape(1, -1), pool_block(), cotangent, gate.reshape(1, -1), w_adapt)
        + (layer_scale.reshape(1, -1),),
        [pltpu.VMEM((7, count + 6, GRID_HI, cb), F32)],
        after,
        prefetch=scalars,
    )


def softmax_rows(q, k, key_valid):
    scores = jnp.where(key_valid, dot_nt(q, k) * HEAD_DIM ** (-0.5), -1e30)
    e = jnp.exp(scores - jnp.max(scores, axis=-1, keepdims=True))
    return e * (1.0 / jnp.sum(e, axis=-1, keepdims=True))


def attention_kernel(
    s_ref, x_ref, gain_ref, shift_ref, wq_ref, wk_ref, wv_ref, bias_ref,
    normed_ref, q_ref, k_ref, v_ref, att_ref,
):
    @pl.when(pl.program_id(0) == 0)
    def _():
        xhat, _ = standardize(x_ref[...].astype(F32), norm_epsilon)
        normed_ref[...] = (xhat * gain_ref[...] + shift_ref[...]).astype(BF16)

    normed = normed_ref[...]
    q_ref[...] = (dot(normed, wq_ref[...]) + bias_ref[0:1]).astype(BF16)
    k_ref[...] = dot(normed, wk_ref[...]).astype(BF16)
    v_ref[...] = (dot(normed, wv_ref[...]) + bias_ref[1:2]).astype(BF16)
    key = lax.broadcasted_iota(jnp.int32, (1, TOKENS), 1)
    key_valid = key < s_ref[0] * GRID_LO
    for h in range(q_ref.shape[1] // HEAD_DIM):
        cut = slice(h * HEAD_DIM, (h + 1) * HEAD_DIM)
        probs = softmax_rows(q_ref[:, cut], k_ref[:, cut], key_valid)
        att_ref[:, cut] = dot(probs.astype(BF16), v_ref[:, cut]).astype(BF16)


def image(width):
    return pl.BlockSpec((None, TOKENS, width), lambda j, s: (s[3], 0, 0))


def attention_forward(tokens, gain, shift, w_flat, qv_bias, scalars, after=()):
    width = tokens.shape[2]
    heads_width = w_flat.shape[1] // 3
    blocks = heads_width // LANES
    column = (pl.BlockSpec((TOKENS, LANES), lambda j, s: (0, j)), array((TOKENS, heads_width)))

    def weight(t):
        return pl.BlockSpec((width, LANES), lambda j, s: (0, t * blocks + j))

    return call(
        attention_kernel,
        "attention_forward",
        (blocks,),
        [image(width), held((1, width)), held((1, width)), weight(0), weight(1), weight(2)]
        + [pl.BlockSpec((2, LANES), lambda j, s: (0, j))],
        [(whole((TOKENS, width)), array((TOKENS, width)))] + [column] * 4,
        (tokens, gain.reshape(1, -1), shift.reshape(1, -1)) + (w_flat,) * 3 + (qv_bias,),
        after=after,
        prefetch=scalars,
    )


def attention_back_kernel(n_mp, scalars_ref, *refs):
    pieces, refs = refs[:n_mp], refs[n_mp:]
    x_ref, gain_ref, w_out_ref, q_ref, k_ref, v_ref, wq_ref, wk_ref, wv_ref = refs[:9]
    d_attn_ref, dq_ref, dk_ref, dv_ref = refs[9:13]
    send_ref, total = refs[13:]
    step = pl.program_id(0)
    mp = scalars_ref[1]
    part = pieces[0].shape[0]

    @pl.when(step == 0)
    def _():
        for k in range(n_mp):
            at = pl.multiple_of((mp ^ k) * part, part)
            total[pl.ds(at, part), :] = pieces[k][...].astype(F32)
        d_attn_ref[...] = total[...].astype(BF16)

    d_att_all = dot_nt(d_attn_ref[...], w_out_ref[...]).astype(BF16)
    key = lax.broadcasted_iota(jnp.int32, (1, TOKENS), 1)
    key_valid = key < scalars_ref[0] * GRID_LO
    scale = HEAD_DIM ** (-0.5)
    for h in range(q_ref.shape[1] // HEAD_DIM):
        cut = slice(h * HEAD_DIM, (h + 1) * HEAD_DIM)
        q, k, v, d_att = q_ref[:, cut], k_ref[:, cut], v_ref[:, cut], d_att_all[:, cut]
        probs = softmax_rows(q, k, key_valid)
        d_probs = dot_nt(d_att, v)
        delta = jnp.sum(probs * d_probs, axis=-1, keepdims=True)
        d_scores = (probs * (d_probs - delta)).astype(BF16)
        dq_ref[:, cut] = (dot(d_scores, k) * scale).astype(BF16)
        dk_ref[:, cut] = (dot_tn(d_scores, q) * scale).astype(BF16)
        dv_ref[:, cut] = dot_tn(probs.astype(BF16), d_att).astype(BF16)
    share = dot_nt(dq_ref[...], wq_ref[...]) + dot_nt(dk_ref[...], wk_ref[...])
    share = share + dot_nt(dv_ref[...], wv_ref[...])

    @pl.when(step == 0)
    def _():
        total[...] = share

    @pl.when(step > 0)
    def _():
        total[...] += share

    @pl.when(step == pl.num_programs(0) - 1)
    def _():
        features = send_ref.shape[2]
        xhat, _ = standardize(x_ref[...].astype(F32), norm_epsilon)
        weighted = total[...] * gain_ref[...]
        ones = jnp.sum(weighted, axis=-1, keepdims=True)
        twos = jnp.sum(weighted * xhat, axis=-1, keepdims=True)
        pad = jnp.zeros((-TOKENS % LANES, 1), F32)
        stats = stat_rows([jnp.concatenate([ones, pad]), jnp.concatenate([twos, pad])], features)
        for g in range(n_mp):
            mine = slice(g * features, (g + 1) * features)
            send_ref[g, :TOKENS, :] = total[:, mine].astype(BF16)
            send_ref[g, TOKENS:, :] = stats


def attention_backward(
    n_mp, tokens, gain, d_attn_pieces, w_out, q, k, v, w_flat, scalars, after=()
):
    width = tokens.shape[2]
    heads_width = q.shape[1]
    blocks = heads_width // LANES
    column = pl.BlockSpec((TOKENS, LANES), lambda j, s: (0, j))

    def weight(t):
        return pl.BlockSpec((width, LANES), lambda j, s: (0, t * blocks + j))

    send_shape = (n_mp, TOKENS + STAT_ROWS, width // n_mp)
    return call(
        functools.partial(attention_back_kernel, n_mp),
        "attention_backward",
        (blocks,),
        [held(d_attn_pieces[0].shape)] * n_mp
        + [image(width), held((1, width)), pl.BlockSpec((LANES, width), lambda j, s: (j, 0))]
        + [column, column, column, weight(0), weight(1), weight(2)],
        [(whole((TOKENS, width)), array((TOKENS, width)))]
        + [(column, array((TOKENS, heads_width)))] * 3
        + [(held(send_shape), array(send_shape))],
        (*d_attn_pieces, tokens, gain.reshape(1, -1), w_out, q, k, v, w_flat, w_flat, w_flat),
        [pltpu.VMEM((TOKENS, width), F32)],
        after,
        prefetch=scalars,
    )


def conv_mlp_kernel(
    n_mp, chunk, s_ref, rows_ref, gain_ref, shift_ref, w1_hbm, b_ref, w2_hbm, wa_hbm, d_adapted_ref, pool_ref,
    normed_ref, inner_ref, pooled_ref, back_ref, send_ref, mean_ref, inv_ref, bias_ref,
    branch_ref, adapted_ref, scale_ref, full, w1_ref, w2_ref, wa_ref, sems,
):
    cells, channels = rows_ref.shape[1:]
    cut = 256
    steps = w1_ref.shape[1] // cut
    cuts = [slice(j * cut, (j + 1) * cut) for j in range(steps)]
    loads = [pltpu.make_async_copy(wa_hbm, wa_ref, sems.at[2 * steps])]
    for j, at in enumerate(cuts):
        loads.append(pltpu.make_async_copy(w1_hbm.at[:, at], w1_ref.at[:, at], sems.at[j]))
        loads.append(pltpu.make_async_copy(w2_hbm.at[at, :], w2_ref.at[at, :], sems.at[steps + j]))
    for load in loads:
        load.start()
    for g in range(n_mp):
        full[:, g * channels : (g + 1) * channels] = rows_ref[g].astype(F32)
    spatial = full[...]
    mean = jnp.mean(spatial, axis=-1, keepdims=True)
    centred = spatial - mean
    inv = lax.rsqrt(jnp.mean(centred * centred, axis=-1, keepdims=True) + channel_epsilon)
    xhat = centred * inv
    full[...] = xhat
    mean_ref[...] = jnp.broadcast_to(mean, mean_ref.shape)
    inv_ref[...] = jnp.broadcast_to(inv, inv_ref.shape)
    normed_ref[...] = (xhat * gain_ref[...] + shift_ref[...]).astype(BF16)
    loads[0].wait()
    count = back_ref.shape[0]
    valid = lax.broadcasted_iota(jnp.int32, (count, 1), 0) + chunk * count < s_ref[0] * GRID_LO
    back = dot_nt(d_adapted_ref[...], wa_ref[...])
    back_ref[...] = jnp.where(valid, back, 0.0).astype(BF16)
    for j, at in enumerate(cuts):
        loads[2 * j + 1].wait()
        active, slope = gelu_pair(dot(normed_ref[...], w1_ref[:, at]) + b_ref[:, at])
        active = active.astype(BF16)
        loads[2 * j + 2].wait()
        d_active = dot_nt(back_ref[...], w2_ref[at, :]).astype(BF16)
        backs = []
        for i in range(cells // CELL_BLOCK):
            lo = slice(i * POOL_BLOCK, (i + 1) * POOL_BLOCK)
            hi = slice(i * CELL_BLOCK, (i + 1) * CELL_BLOCK)
            pooled_ref[lo, at] = dot(pool_ref[...], active[hi]).astype(BF16)
            backs.append(dot_tn(pool_ref[...], d_active[lo]))
        d_inner = (slope * jnp.concatenate(backs, axis=0)).astype(BF16)
        inner_ref[:, at] = d_inner
        bias_ref[:, at] = jnp.sum(d_inner.astype(F32), axis=0, keepdims=True)

    d_normed = dot_nt(inner_ref[...], w1_ref[...])
    weighted = d_normed * gain_ref[...]
    ones = jnp.sum(weighted, axis=-1, keepdims=True)
    twos = jnp.sum(weighted * full[...], axis=-1, keepdims=True)
    stats = stat_rows([ones, twos], channels)
    for g in range(n_mp):
        send_ref[g, :cells, :] = d_normed[:, g * channels : (g + 1) * channels].astype(BF16)
        send_ref[g, cells:, :] = stats
    branch = dot(pooled_ref[...], w2_ref[...])
    scale_ref[...] = jnp.sum(back_ref[...].astype(F32) * branch, axis=0, keepdims=True)
    branch_ref[...] = jnp.where(valid, branch, 0.0).astype(BF16)
    adapted_ref[...] = dot(branch_ref[...], wa_ref[...])


def conv_mlp(rows, gain, shift, w1, b, w2, wa, d_adapted, chunk, scalars, after=()):
    n_mp, cells, channels = rows.shape
    total, hidden = w1.shape
    width = wa.shape[1]
    pooled = cells * 9 // 16
    send_shape = (n_mp, cells + STAT_ROWS, channels)
    anywhere = pl.BlockSpec(memory_space=pl.ANY)

    def out(shape, dtype=BF16):
        return (held(shape), array(shape, dtype))

    return call(
        functools.partial(conv_mlp_kernel, n_mp, chunk),
        "conv_mlp",
        (1,),
        [held((n_mp, cells, channels)), held((1, total)), held((1, total)), anywhere]
        + [held((1, hidden)), anywhere, anywhere, held((pooled, width))]
        + [held((POOL_BLOCK, CELL_BLOCK))],
        [
            out((cells, total)),
            out((cells, hidden)),
            out((pooled, hidden)),
            out((pooled, total)),
            out(send_shape),
            out((cells, LANES), F32),
            out((cells, LANES), F32),
            out((1, hidden), F32),
            out((pooled, total)),
            out((pooled, width), F32),
            out((1, total), F32),
        ],
        (rows, gain.reshape(1, -1), shift.reshape(1, -1), w1, b.reshape(1, -1), w2, wa, d_adapted)
        + (pool_block(),),
        [
            pltpu.VMEM((cells, total), F32),
            pltpu.VMEM((total, hidden), BF16),
            pltpu.VMEM((hidden, total), BF16),
            pltpu.VMEM((total, width), BF16),
            pltpu.SemaphoreType.DMA((2 * (hidden // 256) + 1,)),
        ],
        after,
        prefetch=scalars,
    )


def conv_back_kernel(chunks, total_channels, s_ref, *refs):
    (received, spatial, means, invs, d_pooled) = (
        refs[i * chunks : (i + 1) * chunks] for i in range(5)
    )
    refs = refs[5 * chunks :]
    field_ref, k_ref, gain_ref, pool_ref, out_ref, g_kernel_ref, sums_ref, shifted, moved = refs
    hi_valid = s_ref[5]
    cb = field_ref.shape[2]
    gain = gain_ref[...]
    zeros = jnp.zeros((GRID_HI, cb), F32)
    for a in (0, 1, 2, GRID_HI + 3, GRID_HI + 4, GRID_HI + 5):
        for s in range(7):
            shifted[s, a] = zeros
            moved[s, a] = zeros
    g_gain = jnp.zeros((1, cb), F32)
    g_shift = jnp.zeros((1, cb), F32)
    g_bias = jnp.zeros((1, cb), F32)
    block_rows = CELL_BLOCK // GRID_HI
    first = 0
    for c in range(chunks):
        cells = means[c].shape[0]
        per = cells // LANES
        stats = received[c][cells : cells + STAT_ROWS, :LANES].astype(F32)
        rows = [
            jnp.concatenate([stats[k * per + t : k * per + t + 1] for t in range(per)], axis=1)
            for k in range(2)
        ]
        rows.append(jnp.zeros((LANES - 2, cells), F32))
        columns = jnp.concatenate(rows, axis=0).T * (1.0 / total_channels)
        for i in range(cells // CELL_BLOCK):
            at = slice(i * CELL_BLOCK, (i + 1) * CELL_BLOCK)
            d_normed = received[c][at, :].astype(F32)
            column = columns[at]
            if cb > LANES:
                mean, inv = means[c][at, :1], invs[c][at, :1]
            else:
                mean, inv = means[c][at], invs[c][at]
            xhat = (spatial[c][at].astype(F32) - mean) * inv
            d_spatial = inv * (d_normed * gain - column[:, 0:1] - xhat * column[:, 1:2])
            g_gain = g_gain + jnp.sum(d_normed * xhat, axis=0, keepdims=True)
            g_shift = g_shift + jnp.sum(d_normed, axis=0, keepdims=True)
            g_bias = g_bias + jnp.sum(d_spatial, axis=0, keepdims=True)
            for a in range(block_rows):
                store_shifted(moved, first + a + 3, d_spatial[a * GRID_HI : (a + 1) * GRID_HI])
            first += block_rows

    @pl.loop(0, GRID_HI)
    def _(a):
        row = jnp.where(a < hi_valid, field_ref[a].astype(F32), 0.0)
        store_shifted(shifted, a + 3, row)

    g_kernel_ref[...] = jnp.zeros(g_kernel_ref.shape, F32)
    for s in range(7):
        def rows_of(i, sums):
            a0 = i * 2
            grads = [moved[3, a0 + o + 3] for o in range(2)]
            sums = list(sums)
            for r_in in range(8):
                value = shifted[s, a0 + r_in]
                for o in range(2):
                    r = r_in - o
                    if 0 <= r < 7:
                        product = value * grads[o]
                        sums[r] = sums[r] + jnp.sum(product.reshape(GRID_HI // 8, 8, cb), axis=0)
            return tuple(sums)

        sums = lax.fori_loop(0, GRID_HI // 2, rows_of, tuple(jnp.zeros((8, cb), F32) for _ in range(7)))
        for r in range(7):
            t = r * 7 + s
            g_kernel_ref[t : t + 1, :] = jnp.sum(sums[r], axis=0, keepdims=True)
    sums_ref[...] = jnp.concatenate([g_bias, g_gain, g_shift, jnp.zeros((5, cb), F32)], axis=0)

    for i in range(CELLS // CELL_BLOCK):
        each = CELLS // CELL_BLOCK // chunks
        lo = slice((i % each) * POOL_BLOCK, (i % each + 1) * POOL_BLOCK)
        refined = dot_tn(pool_ref[...], d_pooled[i // each][lo, :])
        shifted[0, i * block_rows : (i + 1) * block_rows] = refined.reshape(block_rows, GRID_HI, cb)

    @pl.loop(0, GRID_HI, step=4)
    def _(a0):
        sums = correlate(
            moved, a0, 4, lambda r, s: k_ref[48 - (r * 7 + s) : 49 - (r * 7 + s), :], jnp.zeros((GRID_HI, cb), F32)
        )
        for o in range(4):
            value = sums[o] + shifted[0, a0 + o]
            out_ref[a0 + o] = jnp.where(a0 + o < hi_valid, value, 0.0).astype(BF16)


def conv_backward(
    received, spatial, means, invs, d_pooled, hires, kernel, my_gain, total_channels, scalars, after=()
):
    chunks = len(received)
    channels = hires.shape[3]
    cb = channel_block(channels)
    cells = means[0].shape[0]

    def column(rows):
        return pl.BlockSpec((rows, cb), lambda j, s: (0, j))

    map_block = pl.BlockSpec((GRID_HI, GRID_HI, cb), lambda j, s: (0, 0, j))
    return call(
        functools.partial(conv_back_kernel, chunks, total_channels),
        "conv_backward",
        (channels // cb,),
        [column(cells + STAT_ROWS)] * chunks
        + [column(cells)] * chunks
        + [held((cells, LANES))] * (2 * chunks)
        + [column(d_pooled[0].shape[0])] * chunks
        + [
            pl.BlockSpec((None, GRID_HI, GRID_HI, cb), lambda j, s: (s[3], 0, 0, j)),
            column(49),
            column(1),
            held((POOL_BLOCK, CELL_BLOCK)),
        ],
        [
            (map_block, array((GRID_HI, GRID_HI, channels))),
            (column(49), array((49, channels), F32)),
            (column(8), array((8, channels), F32)),
        ],
        (*received, *spatial, *means, *invs, *d_pooled)
        + (hires, kernel, my_gain.reshape(1, -1), pool_block()),
        [pltpu.VMEM((7, GRID_HI + 6, GRID_HI, cb), F32)] * 2,
        after,
        prefetch=scalars,
    )


def vit_mlp_kernel(n_mp, scalars_ref, *refs):
    pieces, refs = refs[:n_mp], refs[n_mp:]
    x_ref, wo_hbm, ob_ref, gain_ref, shift_ref, w1_hbm, b1_ref, w2_hbm, dy_ref = refs[:9]
    hidden_ref, normed_ref, active_ref, inner_ref, bias_ref = refs[9:14]
    sends, refs = refs[14 : 14 + n_mp], refs[14 + n_mp :]
    d_normed, wo_ref, w1_ref, w2_ref, sems = refs
    step = pl.program_id(0)
    rows = x_ref.shape[0]
    cut = 256
    cuts = [slice(j * cut, (j + 1) * cut) for j in range(w1_ref.shape[1] // cut)]
    loads = [pltpu.make_async_copy(wo_hbm, wo_ref, sems.at[0])]
    for j, at in enumerate(cuts):
        loads.append(pltpu.make_async_copy(w1_hbm.at[:, at], w1_ref.at[:, at], sems.at[2 * j + 1]))
        loads.append(pltpu.make_async_copy(w2_hbm.at[at, :], w2_ref.at[at, :], sems.at[2 * j + 2]))

    @pl.when(step == 0)
    def _():
        for load in loads:
            load.start()
        loads[0].wait()

    hidden = x_ref[...].astype(F32) + ob_ref[...]
    for k in range(n_mp):
        hidden = hidden + dot(pieces[k][...], wo_ref[k])
    hidden_ref[...] = hidden
    xhat, _ = standardize(hidden, norm_epsilon)
    normed_ref[...] = (xhat * gain_ref[...] + shift_ref[...]).astype(BF16)

    @pl.when(step == 0)
    def _():
        for load in loads[1:]:
            load.wait()

    for j, at in enumerate(cuts):
        active, slope = gelu_pair(dot(normed_ref[...], w1_ref[:, at]) + b1_ref[:, at])
        active_ref[:, at] = active.astype(BF16)
        d_inner = (slope * dot_nt(dy_ref[...], w2_ref[at, :])).astype(BF16)
        inner_ref[:, at] = d_inner
        sums = jnp.sum(d_inner.astype(F32), axis=0, keepdims=True)

        @pl.when(step == 0)
        def _():
            bias_ref[:, at] = sums

        @pl.when(step > 0)
        def _():
            bias_ref[:, at] += sums

    d_normed[pl.ds(pl.multiple_of(step * rows, rows), rows), :] = dot_nt(inner_ref[...], w1_ref[...])

    @pl.when(step == pl.num_programs(0) - 1)
    def _():
        part = sends[0].shape[0]
        for k in range(n_mp):
            at = pl.multiple_of((scalars_ref[1] ^ k) * part, part)
            sends[k][...] = d_normed[pl.ds(at, part), :].astype(BF16)


def vit_mlp(
    tokens, attended_pieces, w_out_pieces, out_bias, gain, shift, w1, b1, w2, cotangent, scalars, after=()
):
    n_mp = len(attended_pieces)
    heads_width = attended_pieces[0].shape[1]
    width, hidden = w1.shape
    rows = TOKENS // 2
    image_rows = pl.BlockSpec((None, rows, width), lambda j, s: (s[3], j, 0))
    row = pl.BlockSpec((rows, width), lambda j, s: (j, 0))
    row_hidden = pl.BlockSpec((rows, hidden), lambda j, s: (j, 0))
    one = held((1, width))
    anywhere = pl.BlockSpec(memory_space=pl.ANY)
    send_shape = (TOKENS // n_mp, width)
    return call(
        functools.partial(vit_mlp_kernel, n_mp),
        "vit_mlp",
        (TOKENS // rows,),
        [pl.BlockSpec((rows, heads_width), lambda j, s: (j, 0))] * n_mp
        + [image_rows, anywhere, one, one, one, anywhere, held((1, hidden)), anywhere, image_rows],
        [
            (row, array((TOKENS, width), F32)),
            (row, array((TOKENS, width))),
            (row_hidden, array((TOKENS, hidden))),
            (row_hidden, array((TOKENS, hidden))),
            (whole((1, hidden)), array((1, hidden), F32)),
        ]
        + [(whole(send_shape), array(send_shape))] * n_mp,
        (*attended_pieces, tokens, w_out_pieces, out_bias.reshape(1, -1), gain.reshape(1, -1))
        + (shift.reshape(1, -1), w1, b1.reshape(1, -1), w2, cotangent),
        [
            pltpu.VMEM((TOKENS, width), F32),
            pltpu.VMEM((n_mp, heads_width, width), BF16),
            pltpu.VMEM((width, hidden), BF16),
            pltpu.VMEM((hidden, width), BF16),
            pltpu.SemaphoreType.DMA((1 + 2 * (hidden // 256),)),
        ],
        after,
        prefetch=scalars,
    )


def adapter_kernel(chunks, scalars_ref, *refs):
    parts, fields = refs[:chunks], refs[chunks : 2 * chunks]
    refs = refs[2 * chunks :]
    pb_ref, scale_ref, wa_ref, active_ref, w2_ref, gate_ref, dy_ref = refs[:7]
    pooled_ref, gate_sum_ref = refs[7:9]
    send_ref, total = refs[9:]
    first = 0
    for field in fields:
        rows = slice(first, first + field.shape[0])
        value = field[...] + scale_ref[...] * pb_ref[...]
        row = lax.broadcasted_iota(jnp.int32, value.shape, 0) + first
        value = jnp.where(row < scalars_ref[0] * GRID_LO, value, 0.0)
        pooled_ref[rows, :] = value.astype(BF16)
        first += field.shape[0]
    total[...] = dot(pooled_ref[...], wa_ref[...])
    first = 0
    for part in parts:
        total[first : first + part.shape[0], :] += part[...]
        first += part.shape[0]
    gate = gate_ref[...]
    adapted = total[...]
    sums = jnp.sum(dy_ref[...].astype(F32) * adapted, axis=0, keepdims=True)
    gate_sum_ref[...] = (1.0 - gate * gate) * sums
    total[...] = dot(active_ref[...], w2_ref[...]) + gate * adapted
    features = send_ref.shape[2]
    for g in range(send_ref.shape[0]):
        send_ref[g] = total[:, g * features : (g + 1) * features].astype(BF16)


def adapter(n_mp, parts, fields, pw2_bias, layer_scale, w_adapt, active, w2, gate, cotangent, scalars, after=()):
    channels, width = w_adapt.shape
    hidden = w2.shape[0]
    send_shape = (n_mp, TOKENS, width // n_mp)
    return call(
        functools.partial(adapter_kernel, len(fields)),
        "adapter",
        (1,),
        [held(v.shape) for v in (*parts, *fields)]
        + [held((1, channels)), held((1, channels)), held((channels, width))]
        + [held((TOKENS, hidden)), held((hidden, width)), held((1, width)), image(width)],
        [
            (held((TOKENS, channels)), array((TOKENS, channels))),
            (held((1, width)), array((1, width), F32)),
            (held(send_shape), array(send_shape)),
        ],
        (*parts, *fields, pw2_bias.reshape(1, -1), layer_scale.reshape(1, -1), w_adapt)
        + (active, w2, gate.reshape(1, -1), cotangent),
        [pltpu.VMEM((TOKENS, width), F32)],
        after,
        prefetch=scalars,
    )


def weight_grad_kernel(counts, block, scalars_ref, *refs):
    pairs = sum(counts)
    lefts, rights = refs[:pairs], refs[pairs : 2 * pairs]
    keep_ref, send_ref = refs[2 * pairs :]
    core = scalars_ref[2]
    at = 0
    used = sum(refs[pairs + sum(counts[:i])].shape[1] for i in range(len(counts)))
    if used < keep_ref.shape[2]:
        rest = jnp.zeros(keep_ref.shape[:2] + (keep_ref.shape[2] - used,), BF16)
        keep_ref[:, :, used:] = rest
        send_ref[:, :, used:] = rest
    first = 0
    for count in counts:
        total = dot_tn(lefts[first][...], rights[first][...])
        for i in range(first + 1, first + count):
            total = total + dot_tn(lefts[i][...], rights[i][...])
        first += count
        lanes = slice(at, at + total.shape[1])
        at += total.shape[1]
        total = total.astype(BF16)
        for q in range(keep_ref.shape[0]):
            halves = [total[(2 * q + h) * block : (2 * q + h + 1) * block] for h in range(2)]

            @pl.when(core == 0)
            def _():
                keep_ref[q, :, lanes] = halves[0]
                send_ref[q, :, lanes] = halves[1]

            @pl.when(core != 0)
            def _():
                keep_ref[q, :, lanes] = halves[1]
                send_ref[q, :, lanes] = halves[0]


def weight_grads(name, groups, grads, scalars, after=(), lanes=None):
    block = grads[0][0][0].shape[1] // groups
    pairs = [pair for grad in grads for pair in grad]
    quads = 1
    while (2 * block * quads) % LANES:
        quads += 1
    total = lanes or sum(grad[0][1].shape[1] for grad in grads)
    out = (
        pl.BlockSpec((quads, block, total), lambda j: (j, 0, 0)),
        array((groups // 2, block, total)),
    )
    return call(
        functools.partial(weight_grad_kernel, [len(grad) for grad in grads], block),
        name,
        (groups // 2 // quads,),
        [SCALARS]
        + [pl.BlockSpec((left.shape[0], 2 * block * quads), lambda j: (0, j)) for left, _ in pairs]
        + [held(right.shape) for _, right in pairs],
        [out, out],
        (scalars, *(left for left, _ in pairs), *(right for _, right in pairs)),
        after=after,
    )


def fold_kernel(_, *refs):
    count = len(refs) // 4
    for p in range(count):
        keep, got = refs[2 * p : 2 * p + 2]
        send, hold = refs[2 * (count + p) : 2 * (count + p) + 2]

        def total():
            return (keep[...].astype(F32) + got[...].astype(F32)).astype(BF16)

        @pl.when(pl.program_id(0) == 0)
        def _():
            send[...] = total().reshape(send.shape)

        @pl.when(pl.program_id(0) == 1)
        def _():
            hold[...] = total().reshape(hold.shape)


def fold(name, parts, scalars, after=()):
    ins, operands, outs = [], [], []
    for keep, got, dim, slot, lanes, block in parts:
        shape = list(keep.shape)
        shape[dim] //= 2
        shape[-1] = lanes
        assert keep.shape[dim] == 2

        def at(j, s, dim=dim, slot=slot, rank=len(shape), block=block):
            index = [0] * rank
            index[dim] = s[slot] ^ (1 - j)
            index[-1] = block
            return tuple(index)

        ins += [pl.BlockSpec(tuple(shape), at)] * 2
        operands += [keep, got]
        out = tuple(shape[:dim] + shape[dim + 1 :])
        outs += [(whole(out), array(out))] * 2
    return call(
        fold_kernel, name, (2,), ins, outs, operands, after=after, prefetch=scalars
    )


def norm2_back_kernel(n_mp, scalars_ref, *refs):
    got, refs = refs[:n_mp], refs[n_mp:]
    hidden_ref, dy_ref, gain_ref, d_attn_ref, sums_ref = refs
    d_normed = got[0][...].astype(F32)
    for value in got[1:]:
        d_normed = d_normed + value[...].astype(F32)
    xhat, inv = standardize(hidden_ref[...], norm_epsilon)
    dxhat = d_normed * gain_ref[...]
    d_hidden = dy_ref[...].astype(F32) + inv * (
        dxhat
        - jnp.mean(dxhat, axis=-1, keepdims=True)
        - xhat * jnp.mean(dxhat * xhat, axis=-1, keepdims=True)
    )
    d_attn = d_hidden.astype(BF16)
    d_attn_ref[...] = d_attn
    sums_ref[0:1, :] = jnp.sum(d_attn.astype(F32), axis=0, keepdims=True)
    sums_ref[1:2, :] = jnp.sum(d_normed * xhat, axis=0, keepdims=True)
    sums_ref[2:3, :] = jnp.sum(d_normed, axis=0, keepdims=True)
    sums_ref[3:, :] = jnp.zeros((5, sums_ref.shape[1]), F32)


def norm2_backward(got, hidden, cotangent, gain, scalars, after=()):
    n_mp = len(got)
    rows, width = got[0].shape
    mine = pl.BlockSpec((None, rows, width), lambda j, s: (s[1], 0, 0))
    image_rows = pl.BlockSpec((None, None, rows, width), lambda j, s: (s[3], s[1], 0, 0))
    return call(
        functools.partial(norm2_back_kernel, n_mp),
        "norm2_backward",
        (1,),
        [held((rows, width))] * n_mp + [mine, image_rows, held((1, width))],
        [
            (held((rows, width)), array((rows, width))),
            (held((8, width)), array((8, width), F32)),
        ],
        (*got, hidden.reshape(n_mp, rows, width), cotangent.reshape(-1, n_mp, rows, width))
        + (gain.reshape(1, -1),),
        after=after,
        prefetch=scalars,
    )


def norm1_back_kernel(n_mp, scalars_ref, *refs):
    got, refs = refs[:n_mp], refs[n_mp:]
    x_ref, mine_ref, d_attn_ref, gain_ref, dy_ref, keep_ref, send_ref, sums_ref, total = refs
    width = x_ref.shape[1]
    value = got[0][...].astype(F32)
    for piece in got[1:]:
        value = value + piece[...].astype(F32)
    d_normed, stats = value[:TOKENS], value[TOKENS:, :LANES]
    count = -(-TOKENS // LANES)
    rows = [
        jnp.concatenate([stats[k * count + t : k * count + t + 1] for t in range(count)], axis=1)
        for k in range(2)
    ]
    rows.append(jnp.zeros((LANES - 2, count * LANES), F32))
    columns = jnp.concatenate(rows, axis=0).T[:TOKENS] * (1.0 / width)
    x = x_ref[...].astype(F32)
    mean = jnp.mean(x, axis=-1, keepdims=True)
    inv = lax.rsqrt(jnp.mean((x - mean) * (x - mean), axis=-1, keepdims=True) + norm_epsilon)
    xhat = (mine_ref[...].astype(F32) - mean) * inv
    total[...] = d_attn_ref[...].astype(F32) + inv * (
        d_normed * gain_ref[...] - columns[:, 0:1] - xhat * columns[:, 1:2]
    )
    half = TOKENS // 2
    path = scalars_ref[3]
    keep_ref[...] = total[pl.ds(pl.multiple_of(path * half, half), half), :].astype(BF16)
    send_ref[...] = total[pl.ds(pl.multiple_of((1 - path) * half, half), half), :].astype(BF16)
    sums_ref[0:1, :] = jnp.sum(d_normed * xhat, axis=0, keepdims=True)
    sums_ref[1:2, :] = jnp.sum(d_normed, axis=0, keepdims=True)
    sums_ref[2:3, :] = jnp.sum(dy_ref[...].astype(F32), axis=0, keepdims=True)
    sums_ref[3:, :] = jnp.zeros((5, sums_ref.shape[1]), F32)


def norm1_backward(got, tokens, d_attn, gain, cotangent, scalars, after=()):
    rows, features = got[0].shape
    width = tokens.shape[2]
    mine = pl.BlockSpec((TOKENS, features), lambda j, s: (0, s[1]))
    mine_of = pl.BlockSpec((None, TOKENS, features), lambda j, s: (s[3], 0, s[1]))
    half = (held((TOKENS // 2, features)), array((TOKENS // 2, features)))
    return call(
        functools.partial(norm1_back_kernel, len(got)),
        "norm1_backward",
        (1,),
        [held((rows, features))] * len(got)
        + [image(width), mine_of, mine]
        + [pl.BlockSpec((1, features), lambda j, s: (0, s[1])), mine_of],
        [half, half, (held((8, features)), array((8, features), F32))],
        (*got, tokens, tokens, d_attn, gain.reshape(1, -1), cotangent),
        [pltpu.VMEM((TOKENS, features), F32)],
        after=after,
        prefetch=scalars,
    )


def output_kernel(n_mp, scalars_ref, *refs):
    got, refs = refs[:n_mp], refs[n_mp:]
    hidden_ref, bias_ref, keep_ref, send_ref, total = refs
    value = hidden_ref[...] + bias_ref[...]
    for piece in got:
        value = value + piece[...].astype(F32)
    total[...] = value
    half = TOKENS // 2
    path = scalars_ref[3]
    keep_ref[...] = total[pl.ds(pl.multiple_of(path * half, half), half), :].astype(BF16)
    send_ref[...] = total[pl.ds(pl.multiple_of((1 - path) * half, half), half), :].astype(BF16)


def output_halves(got, hidden, fc2_bias, scalars, after=()):
    n_mp = len(got)
    features = got[0].shape[1]
    half = (held((TOKENS // 2, features)), array((TOKENS // 2, features)))
    return call(
        functools.partial(output_kernel, n_mp),
        "output_halves",
        (1,),
        [held((TOKENS, features))] * n_mp
        + [pl.BlockSpec((TOKENS, features), lambda j, s: (0, s[1]))]
        + [pl.BlockSpec((1, features), lambda j, s: (0, s[1]))],
        [half, half],
        (*got, hidden, fc2_bias.reshape(1, -1)),
        [pltpu.VMEM((TOKENS, features), F32)],
        after=after,
        prefetch=scalars,
    )


WIDE_ROWS = 7


def slots_of(shapes, width):
    row, lane, slots = 0, 0, []
    for rows, n in shapes:
        mine = []
        for _ in range(rows):
            pieces = []
            for at in range(0, n, width):
                size = min(width, n - at)
                if lane + size > width:
                    row, lane = row + 1, 0
                pieces.append((row, lane, at, size))
                lane += size
            mine.append(pieces)
        slots.append(mine)
    return slots, -(-(row + 1) // 8) * 8


def pack_kernel(n_mp, slots, s_ref, *refs):
    wide, refs = refs[:n_mp], refs[n_mp:]
    sums_ref, bias_ref, scale_ref, *arrays, packed_ref, total_ref = refs
    packed_ref[...] = jnp.zeros(packed_ref.shape, F32)
    total = wide[0][...]
    for piece in wide[1:]:
        total = total + piece[...]
    total_ref[...] = total
    channels = scale_ref.shape[1]
    mine = total_ref[pl.ds(WIDE_ROWS + s_ref[1], 1), :][:, :channels]
    g_scale = mine / scale_ref[...] + bias_ref[...] * sums_ref[1:2, :]
    values = [total[:WIDE_ROWS], g_scale, sums_ref[0:1, :]] + [v[...] for v in arrays]
    for value, mine in zip(values, slots):
        for r, pieces in enumerate(mine):
            for row, lane, at, n in pieces:
                packed_ref[row : row + 1, lane : lane + n] = value[r : r + 1, at : at + n]


def pack(wide_pieces, sums, pw2_bias, layer_scale, arrays, rows, scalars, after=()):
    n_mp = len(wide_pieces)
    width = wide_pieces[0].shape[1]
    channels = sums.shape[1]
    shapes = [(WIDE_ROWS, width), (1, channels), (1, channels)]
    shapes += [(count, v.shape[1]) for v, count in zip(arrays, rows)]
    slots, total = slots_of(shapes, width)
    operands = (*wide_pieces, sums, pw2_bias.reshape(1, -1), layer_scale.reshape(1, -1), *arrays)
    packed = call(
        functools.partial(pack_kernel, n_mp, slots),
        "pack",
        (1,),
        [held(v.shape) for v in operands],
        [(held((total, width)), array((total, width), F32))],
        operands,
        [pltpu.VMEM(wide_pieces[0].shape, F32)],
        after=after,
        prefetch=scalars,
    )[0]
    return packed, slots


def unpack_kernel(slots, a_ref, b_ref, *outs):
    for out, mine in zip(outs, slots):
        for r, pieces in enumerate(mine):
            for row, lane, at, n in pieces:
                out[r : r + 1, at : at + n] = (
                    a_ref[row : row + 1, lane : lane + n] + b_ref[row : row + 1, lane : lane + n]
                )


def unpack(a, b, slots, after=()):
    shapes = [(len(mine), sum(n for *_, n in mine[0])) for mine in slots]
    return call(
        functools.partial(unpack_kernel, slots),
        "unpack",
        (1,),
        [held(a.shape)] * 2,
        [(held(shape), array(shape, F32)) for shape in shapes],
        (a, b),
        after=after,
    )


def swap(value, axis, apart):
    n = lax.axis_size(axis)
    return lax.ppermute(value, axis, [(i, i ^ apart) for i in range(n)])


def pick(value, axis, index):
    return lax.dynamic_index_in_dim(value, index, axis, keepdims=False)


def gathered(value, axis):
    return [value] + [swap(value, axis, k) for k in range(1, lax.axis_size(axis))]


def exchanged(blocks, axis):
    return blocks[:1] + [swap(block, axis, k) for k, block in enumerate(blocks) if k]


def in_order(values, axis):
    me = lax.axis_index(axis)
    apart = 1
    while apart < len(values):
        turned = (me & apart) > 0
        values = [jnp.where(turned, values[i ^ apart], values[i]) for i in range(len(values))]
        apart *= 2
    return values


def spread(value, steps):
    for axis, apart, place in steps:
        other = swap(value, axis, apart)
        turned = (lax.axis_index(axis) & apart) > 0
        pair = [jnp.where(turned, other, value), jnp.where(turned, value, other)]
        value = jnp.stack(pair, axis=place)
    return value.reshape(value.shape[0], -1, value.shape[-1])


def halve(value, dim, axis, apart, bit):
    received = swap(pick(value, dim, 1 - bit), axis, apart)
    return pick(value, dim, bit).astype(F32) + received.astype(F32)


def across(halves):
    keep, send = halves
    return keep, swap(send, "dp", 1)


def first_fold(name, halves, scalars, after, dp_first=False):
    n_path, n_dp = lax.axis_size("path"), lax.axis_size("dp")
    block, lanes = halves[0].shape[1:]
    shape = (n_path, n_dp // 4, 2, block, lanes)
    keep, got = (half.reshape(shape) for half in halves)
    dim, slot = (2, 4) if dp_first else (0, 3)
    send, hold = fold(name, [(keep, got, dim, slot, lanes, 0)], scalars, after)
    return hold, swap(send, *(("dp", 2) if dp_first else ("path", 1))), dp_first


def second_fold(name, part, scalars, after):
    hold, got, path_next = part
    dim, slot = (0, 3) if path_next else (1, 4)
    send, hold = fold(name, [(hold, got, dim, slot, hold.shape[-1], 0)], scalars, after)
    return hold, swap(send, *(("path", 1) if path_next else ("dp", 2)))


def last_sum(hold, got):
    n_dp, me_dp = lax.axis_size("dp"), lax.axis_index("dp")
    value = hold.astype(F32) + got.astype(F32)
    size = value.shape[0]
    b = 2
    while size > 1:
        size //= 2
        shape = (size, 2) + value.shape[1:]
        value = halve(value.astype(BF16).reshape(shape), 1, "dp", 1 << b, (me_dp >> b) & 1)
        b += 1
    return value[0]


def summed_at_once(value, axis):
    return sum(gathered(value, axis))


def summed(value, axes):
    for axis in axes:
        apart = 1
        while apart < lax.axis_size(axis):
            value = value + swap(value, axis, apart)
            apart *= 2
    return value


def body(
    tokens,
    hires,
    valid_rows,
    cotangent,
    attention_norm_gain,
    attention_norm_bias,
    w_qkv,
    qv_bias,
    w_out,
    out_bias,
    mlp_norm_gain,
    mlp_norm_bias,
    w_fc1,
    fc1_bias,
    down_weight,
    fc2_bias,
    w_adapt,
    gate_param,
    dw_kernel,
    dw_bias,
    channel_norm_gain,
    channel_norm_bias,
    w_pw1,
    pw1_bias,
    w_pw2,
    pw2_bias,
    layer_scale,
):
    path = lax.axis_index("path")
    n_path = lax.axis_size("path")
    dp = lax.axis_index("dp")
    mp = lax.axis_index("mp")
    n_mp = lax.axis_size("mp")
    groups = n_path * lax.axis_size("dp")
    assert tokens.shape[0] == n_path == 2
    width = tokens.shape[2]
    heads_width = w_qkv.shape[2]
    features = width // n_mp
    channels = hires.shape[3]
    all_channels = w_pw1.shape[0]
    part_rows = TOKENS // n_mp
    chunk_rows = GRID_HI // CHUNKS

    valid = pick(valid_rows, 0, path)
    hi_valid = (valid * GRID_HI + GRID_LO - 1) // GRID_LO
    rank = path * lax.axis_size("dp") + dp
    scalars = jnp.stack([valid, mp, dp & 1, path, (dp >> 1) & 1, hi_valid, rank])
    gate = jnp.tanh(gate_param)

    def my_features(v):
        return lax.dynamic_slice_in_dim(v, mp * features, features, v.ndim - 1)

    rows, rows_all, pooled_field, d_pooled, d_adapted = [], [], [], [], []
    front_sums, ranks = 0.0, []
    last = ()
    for c in range(CHUNKS):
        send, *chunk, sums, rank_out = front(
            hires,
            dw_kernel,
            dw_bias,
            cotangent,
            gate,
            w_adapt,
            layer_scale,
            scalars,
            c * chunk_rows,
            chunk_rows,
            last,
        )
        last = (sums,)
        front_sums = front_sums + sums
        ranks.append(rank_out)
        rows.append(send)
        rows_all.append(lax.all_gather(send, "mp", axis=0, tiled=False))
        for kept, value in zip((pooled_field, d_pooled, d_adapted), chunk):
            kept.append(value)

    rank = ranks[-1][0, 0]
    out_rows, adapt_rows = heads_width // groups, channels // groups
    scaled = w_adapt.astype(F32) * layer_scale[:, None]
    share = jnp.concatenate(
        [
            lax.dynamic_slice_in_dim(w_out, rank * out_rows, out_rows, 0),
            lax.dynamic_slice_in_dim(scaled, rank * adapt_rows, adapt_rows, 0).astype(BF16),
        ]
    )
    shares = gathered(share, "mp")
    chips = [("dp", 1 << b, -3) for b in range(lax.axis_size("dp").bit_length() - 2, 0, -1)]
    w_out_pieces = spread(
        jnp.stack([v[:out_rows] for v in shares]), [("path", 1, -3)] + chips + [("dp", 1, -3)]
    )
    w_adapt_all = spread(
        jnp.stack(in_order([v[out_rows:] for v in shares], "mp")),
        chips + [("path", 1, 1), ("dp", 1, -3)],
    ).reshape(all_channels, width)

    w_flat = w_qkv.reshape(width, 3 * heads_width)
    normed1, query, keys, values, attended = attention_forward(
        tokens, attention_norm_gain, attention_norm_bias, w_flat, qv_bias, scalars, last + tuple(rows_all[:1])
    )
    attended_pieces = gathered(attended, "mp")
    last = (attended,)

    def conv(c, after):
        out = conv_mlp(
            rows_all[c],
            channel_norm_gain,
            channel_norm_bias,
            w_pw1,
            pw1_bias,
            w_pw2,
            w_adapt_all,
            d_adapted[c],
            c,
            scalars,
            after,
        )
        return out, lax.psum_scatter(out[4], "mp", scatter_dimension=0, tiled=False), (out[7],)

    conv_out, received = [], []
    out, got, last = conv(0, last)
    conv_out.append(out)
    received.append(got)
    hidden1, normed2, fc_active, d_fc_inner, g_fc1_bias, *sends = vit_mlp(
        tokens,
        attended_pieces,
        w_out_pieces,
        out_bias,
        mlp_norm_gain,
        mlp_norm_bias,
        w_fc1,
        fc1_bias,
        down_weight,
        cotangent,
        scalars,
        last,
    )
    d_normed2_pieces = exchanged(sends, "mp")
    last = (g_fc1_bias,)
    for c in range(1, CHUNKS):
        out, got, last = conv(c, last)
        conv_out.append(out)
        received.append(got)
    (
        conv_normed,
        conv_inner,
        pooled_active,
        backs,
        _,
        means,
        invs,
        bias_sums,
        branches,
        adapted_parts,
        scale_sums,
    ) = zip(*conv_out)
    g_pw1_bias = sum(bias_sums)

    pooled, g_gate, send = adapter(
        n_mp,
        adapted_parts,
        pooled_field,
        pw2_bias,
        layer_scale,
        w_adapt,
        fc_active,
        down_weight,
        gate,
        cotangent,
        scalars,
        last + tuple(received[:-1]),
    )
    branch_sum = lax.psum_scatter(send, "mp", scatter_dimension=0, tiled=False)
    d_attn_part, norm2_sums = norm2_backward(
        d_normed2_pieces, hidden1, cotangent, mlp_norm_gain, scalars, (g_gate,)
    )
    d_attn_pieces = gathered(d_attn_part, "mp")
    dy = pick(cotangent, 0, path)
    fc_halves = across(
        weight_grads(
            "grad_fc",
            groups,
            [[(normed2, d_fc_inner)], [(dy, fc_active)]],
            scalars,
            (norm2_sums,),
        )
    )
    pooled_rows = d_adapted[0].shape[0]
    pooled_cuts = [pooled[c * pooled_rows : (c + 1) * pooled_rows] for c in range(CHUNKS)]
    adapt_halves = across(
        weight_grads(
            "grad_adapt",
            groups,
            [list(zip(d_adapted, branches)), list(zip(d_adapted, pooled_cuts))],
            scalars,
            fc_halves[:1],
        )
    )
    pw2_halves = across(
        weight_grads(
            "grad_pw2", groups, [list(zip(backs, pooled_active))], scalars, adapt_halves[:1]
        )
    )
    pw1_halves = across(
        weight_grads(
            "grad_pw1", groups, [list(zip(conv_normed, conv_inner))], scalars, pw2_halves[:1]
        )
    )

    d_attn, d_query, d_keys, d_values, send = attention_backward(
        n_mp,
        tokens,
        attention_norm_gain,
        d_attn_pieces,
        w_out,
        query,
        keys,
        values,
        w_flat,
        scalars,
        pw1_halves[:1],
    )
    d_normed1 = lax.psum_scatter(send, "mp", scatter_dimension=0, tiled=False)
    fc_part = first_fold("fold_fc", fc_halves, scalars, (d_query, *received[1:]))
    adapt_part = first_fold("fold_adapt", adapt_halves, scalars, fc_part[:1], True)
    pw2_part = first_fold("fold_pw2", pw2_halves, scalars, adapt_part[:1], True)
    pw1_part = first_fold("fold_pw1", pw1_halves, scalars, pw2_part[:1])
    qkv_halves = across(
        weight_grads(
            "grad_qkv",
            groups,
            [
                [(normed1, d_query)],
                [(normed1, d_keys)],
                [(normed1, d_values)],
                [(d_attn, attended)],
            ],
            scalars,
            pw1_part[:1],
        )
    )
    g_qv_bias = jnp.stack(
        [jnp.sum(d_query.astype(F32), axis=0), jnp.sum(d_values.astype(F32), axis=0)]
    )

    tokens_keep, tokens_send, norm1_sums = norm1_backward(
        [d_normed1],
        tokens,
        d_attn,
        attention_norm_gain,
        cotangent,
        scalars,
        qkv_halves[:1],
    )

    def placed(v):
        return lax.dynamic_update_slice(jnp.zeros((width,), F32), v, (mp * features,))

    scale_rows = jnp.pad(sum(scale_sums).reshape(n_mp, channels), ((0, 0), (0, width - channels)))
    wide = jnp.concatenate(
        [norm2_sums[:3]]
        + [placed(norm1_sums[i])[None] for i in range(3)]
        + [g_gate, scale_rows]
    )
    wide_pieces = gathered(wide, "mp")
    d_field, g_kernel, conv_sums = conv_backward(
        received,
        rows,
        means,
        invs,
        d_pooled,
        hires,
        dw_kernel,
        lax.dynamic_slice_in_dim(channel_norm_gain, mp * channels, channels, 0),
        all_channels,
        scalars,
        (norm1_sums, fc_part[1], adapt_part[1]),
    )

    packed, slots = pack(
        wide_pieces,
        front_sums,
        pw2_bias,
        layer_scale,
        [g_qv_bias, g_fc1_bias, g_pw1_bias, g_kernel, conv_sums],
        (2, 1, 1, 49, 3),
        scalars,
        (conv_sums,),
    )
    packed_first = packed
    packed = summed(packed, ("dp",))
    output_keep, output_send = output_halves(
        [branch_sum], hidden1, fc2_bias, scalars, (packed_first, pw2_part[1], pw1_part[1])
    )
    qkv_part = first_fold("fold_qkv", qkv_halves, scalars, (output_keep,), True)
    adapt_part = second_fold("fold_adapt_last", adapt_part, scalars, qkv_part[:1])
    fc_part = second_fold("fold_fc_last", fc_part, scalars, adapt_part[:1])
    pw2_part = second_fold("fold_pw2_last", pw2_part, scalars, fc_part[:1])
    pw1_part = second_fold("fold_pw1_last", pw1_part, scalars, pw2_part[:1])
    qkv_part = second_fold("fold_qkv_last", qkv_part, scalars, pw1_part[:1])

    def both_images(mine, send):
        other = swap(send, "path", 1)
        first = path == 0
        return jnp.stack([jnp.where(first, mine, other), jnp.where(first, other, mine)])

    def keep_half(rows):
        halves = rows.reshape((2, rows.shape[0] // 2) + rows.shape[1:])
        return both_images(pick(halves, 0, path), pick(halves, 0, 1 - path))

    output = both_images(output_keep, output_send)
    tokens_grad = both_images(tokens_keep, tokens_send)
    hires_grad = keep_half(d_field)

    g_adapt = last_sum(*adapt_part)
    g_adapt_mine = sum(
        piece.astype(F32)
        for piece in exchanged(
            [
                lax.dynamic_slice_in_dim(g_adapt, (mp ^ k) * channels, channels, 1).astype(BF16)
                for k in range(n_mp)
            ],
            "mp",
        )
    )
    g_adapt_mine = g_adapt_mine * layer_scale + g_adapt[:, all_channels:]
    g_fc = last_sum(*fc_part)
    g_fc1_mine, g_fc2_mine = g_fc[:, : w_fc1.shape[1]], g_fc[:, w_fc1.shape[1] :]
    g_pw1_mine, g_pw2_mine = last_sum(*pw1_part), last_sum(*pw2_part)
    g_rest = last_sum(*qkv_part)
    g_qkv_mine = g_rest[:, : 3 * heads_width].reshape(-1, 3, heads_width)
    g_out_mine = g_rest[:, 3 * heads_width :]

    small = unpack(packed, swap(packed, "path", 1), slots)
    wide, g_scale, g_pw2_bias, g_qv_bias, g_fc1_bias, g_pw1_bias, g_kernel, conv_sums = small
    g_out_bias, g_norm2_gain, g_norm2_bias, g_norm1_gain, g_norm1_bias, g_fc2_bias, g_gate = wide
    g_dw_bias, g_cnorm_gain, g_cnorm_bias = conv_sums
    return (
        output,
        tokens_grad,
        hires_grad,
        g_norm1_gain,
        g_norm1_bias,
        g_qkv_mine,
        g_qv_bias,
        g_out_mine.T,
        g_out_bias,
        g_norm2_gain,
        g_norm2_bias,
        g_fc1_mine,
        g_fc1_bias[0],
        g_fc2_mine.T,
        g_fc2_bias,
        g_adapt_mine.T,
        g_gate,
        g_kernel,
        g_dw_bias,
        g_cnorm_gain,
        g_cnorm_bias,
        g_pw1_mine,
        g_pw1_bias[0],
        g_pw2_mine.T,
        g_pw2_bias[0],
        g_scale[0],
    )


def solution(mesh):
    in_specs = (
        P("dp", None, None),
        P("dp", None, None, "mp"),
        P("dp"),
        P("dp", None, None),
        P(),
        P(),
        P(None, None, "mp"),
        P(None, "mp"),
        P("mp", None),
        P(),
        P(),
        P(),
        P(None, "mp"),
        P("mp"),
        P("mp", None),
        P(),
        P("mp", None),
        P(),
        P(None, "mp"),
        P("mp"),
        P(),
        P(),
        P(None, "mp"),
        P("mp"),
        P("mp", None),
        P("mp"),
        P("mp"),
    )
    out_specs = (
        P("dp", "path", "mp"),
        P("dp", "path", "mp"),
        P("dp", "path", None, "mp"),
        P(),
        P(),
        P(("path", "dp"), None, "mp"),
        P(None, "mp"),
        P("mp", ("path", "dp")),
        P(),
        P(),
        P(),
        P(("path", "dp"), "mp"),
        P("mp"),
        P("mp", ("path", "dp")),
        P(),
        P("mp", ("path", "dp")),
        P(),
        P(None, "mp"),
        P("mp"),
        P("mp"),
        P("mp"),
        P(("path", "dp"), "mp"),
        P("mp"),
        P("mp", ("path", "dp")),
        P("mp"),
        P("mp"),
    )
    return jax.shard_map(body, mesh=mesh, in_specs=in_specs, out_specs=out_specs, check_vma=False)
```

```python
import functools

import jax
import jax.numpy as jnp
import numpy as np
from jax import lax
from jax.experimental import pallas as pl
from jax.experimental.pallas import tpu as pltpu
from jax.sharding import PartitionSpec as P

HEAD_DIM = 64
GRID_LO = 24
GRID_HI = 32
TOKENS = GRID_LO * GRID_LO
CELLS = GRID_HI * GRID_HI
LANES = 128
STAT_ROWS = 16
CELL_BLOCK = 256
POOL_BLOCK = CELL_BLOCK * 9 // 16

norm_epsilon = 1e-05
channel_epsilon = 1e-06
F32 = jnp.float32
BF16 = jnp.bfloat16
VMEM_BYTES = 60 * 1024 * 1024
CHUNKS = 2


def gelu_pair(v):
    c = 0.7978845608028654
    square = v * v
    t = jnp.tanh(c * v * (1.0 + 0.044715 * square))
    half = 0.5 + 0.5 * t
    return v * half, half + (0.5 * c) * v * (1.0 - t * t) * (1.0 + 3 * 0.044715 * square)


def pool_rows(lo, hi):
    ratio = hi / lo
    target = np.arange(lo, dtype=np.float64)[:, None]
    source = np.arange(hi, dtype=np.float64)[None, :]
    lower = np.maximum(source, target * ratio)
    upper = np.minimum(source + 1.0, (target + 1.0) * ratio)
    return np.round(np.maximum(upper - lower, 0.0) / ratio * 4) / 4


def pool_block():
    rows = CELL_BLOCK // GRID_HI
    return jnp.asarray(np.kron(pool_rows(rows * 3 // 4, rows), pool_rows(GRID_LO, GRID_HI)), BF16)


def dot(a, b):
    return jnp.dot(a, b, preferred_element_type=F32)


def dot_nt(a, b):
    return lax.dot_general(a, b, (((1,), (1,)), ((), ())), preferred_element_type=F32)


def dot_tn(a, b):
    return lax.dot_general(a, b, (((0,), (0,)), ((), ())), preferred_element_type=F32)


def standardize(v, eps):
    centred = v - jnp.mean(v, axis=-1, keepdims=True)
    inv = lax.rsqrt(jnp.mean(centred * centred, axis=-1, keepdims=True) + eps)
    return centred * inv, inv


KERNEL_US = {
    "front": 0.5,
    "attention_forward": 10,
    "conv_mlp": 0.5,
    "vit_mlp": 33,
    "norm2_backward": 0.5,
    "attention_backward": 31,
    "norm1_backward": 0.5,
    "adapter": 0.5,
    "conv_backward": 0.5,
    "output_halves": 3,
    "pack": 3,
    "unpack": 3,
    "grad_fc": 0.5,
    "grad_pw1": 0.5,
    "grad_pw2": 0.5,
    "grad_qkv": 0.5,
    "grad_adapt": 0.5,
    "fold_fc": 0.5,
    "fold_pw1": 0.5,
    "fold_pw2": 0.5,
    "fold_qkv": 3,
    "fold_adapt": 0.5,
    "fold_fc_last": 3,
    "fold_pw1_last": 3,
    "fold_pw2_last": 3,
    "fold_qkv_last": 3,
    "fold_adapt_last": 3,
}
FLOPS_PER_US = 1.15e9


def call(
    kernel, name, grid, ins, outs, operands, scratch=(), after=(), prefetch=None
):
    lead = 0 if prefetch is None else 1
    count = lead + len(ins)

    def run(*refs):
        kernel(*refs[:count], *refs[count + len(after) :])

    in_specs = list(ins) + [pl.BlockSpec(memory_space=pl.ANY)] * len(after)
    return pl.pallas_call(
        run,
        grid_spec=pltpu.PrefetchScalarGridSpec(
            num_scalar_prefetch=lead,
            grid=grid,
            in_specs=in_specs,
            out_specs=[spec for spec, _ in outs],
            scratch_shapes=list(scratch),
        ),
        out_shape=[shape for _, shape in outs],
        compiler_params=pltpu.CompilerParams(
            dimension_semantics=("arbitrary",) * len(grid), vmem_limit_bytes=VMEM_BYTES
        ),
        name=name,
        cost_estimate=pl.CostEstimate(
            flops=int(KERNEL_US[name] * FLOPS_PER_US), bytes_accessed=1, transcendentals=0
        ),
    )(*(() if prefetch is None else (prefetch,)), *operands, *after)


SCALARS = pl.BlockSpec(memory_space=pltpu.SMEM)


def array(shape, dtype=BF16):
    return jax.ShapeDtypeStruct(shape, dtype)


def held(shape):
    return pl.BlockSpec(shape, lambda *_: (0,) * len(shape), pipeline_mode=pl.Buffered(1))


def whole(shape):
    return pl.BlockSpec(shape, lambda *_: (0,) * len(shape))


def rows_to_lanes(columns):
    rows = columns[0].shape[0]
    lane = lax.broadcasted_iota(jnp.int32, (rows, LANES), 1)
    packed = jnp.zeros((rows, LANES), F32)
    for i, column in enumerate(columns):
        packed = jnp.where(lane == i, column, packed)
    return packed.T


def stat_rows(columns, width):
    lanes = rows_to_lanes(columns)
    pieces = [
        lanes[i : i + 1, t * LANES : (t + 1) * LANES]
        for i in range(2)
        for t in range(lanes.shape[1] // LANES)
    ]
    pieces.append(jnp.zeros((STAT_ROWS - len(pieces), LANES), F32))
    stats = jnp.concatenate(pieces, axis=0).astype(BF16)
    if width % LANES:
        return jnp.concatenate([stats, jnp.zeros((STAT_ROWS, width - LANES), BF16)], axis=1)
    return jnp.concatenate([stats] * (width // LANES), axis=1)


def channel_block(channels):
    return LANES if channels % LANES == 0 else channels


def store_shifted(shifted, a, row):
    column = lax.broadcasted_iota(jnp.int32, row.shape, 0)
    for s in range(7):
        move = s - 3
        if move == 0:
            shifted[s, a] = row
        else:
            rolled = pltpu.roll(row, (-move) % GRID_HI, 0)
            inside = (column + move >= 0) & (column + move < GRID_HI)
            shifted[s, a] = jnp.where(inside, rolled, 0.0)


def correlate(shifted, a0, count, taps, start):
    sums = [start] * count
    for r_in in range(count + 6):
        for s in range(7):
            value = shifted[s, a0 + r_in]
            for o in range(count):
                r = r_in - o
                if 0 <= r < 7:
                    sums[o] = sums[o] + value * taps(r, s)
    return sums


def front_kernel(
    base, count, s_ref, field_ref, k_ref, bias_ref, pool_ref, dy_ref, gate_ref, wa_ref, scale_ref,
    send_ref, field_pooled_ref, d_pooled_ref, d_adapted_ref, sums_ref, rank_ref, shifted,
):
    hi_valid = s_ref[5]
    cb = field_ref.shape[2]
    rank_ref[...] = jnp.full(rank_ref.shape, s_ref[6], jnp.int32)

    @pl.when(pl.program_id(0) == 0)
    def _():
        d_adapted_ref[...] = (gate_ref[...] * dy_ref[...].astype(F32)).astype(BF16)

    @pl.loop(0, count + 6)
    def _(a):
        source = base + a - 3
        keep = (source >= 0) & (source < hi_valid)
        row = field_ref[jnp.clip(source, 0, GRID_HI - 1)].astype(F32)
        store_shifted(shifted, a, jnp.where(keep, row, 0.0))

    start = jnp.broadcast_to(bias_ref[...], (GRID_HI, cb))

    @pl.loop(0, count, step=4)
    def _(a0):
        sums = correlate(
            shifted, a0, 4, lambda r, s: k_ref[r * 7 + s : r * 7 + s + 1, :], start
        )
        for o in range(4):
            at = pl.multiple_of((a0 + o) * GRID_HI, GRID_HI)
            send_ref[pl.ds(at, GRID_HI), :] = sums[o].astype(BF16)

    block_rows = CELL_BLOCK // GRID_HI
    for i in range(count // block_rows):
        first = base + i * block_rows
        rows = field_ref[first : first + block_rows]
        row = lax.broadcasted_iota(jnp.int32, rows.shape, 0) + first
        rows = jnp.where(row < hi_valid, rows.astype(F32), 0.0).astype(BF16)
        field_pooled_ref[i * POOL_BLOCK : (i + 1) * POOL_BLOCK] = dot(
            pool_ref[...], rows.reshape(CELL_BLOCK, cb)
        )
    d_pooled = dot_nt(d_adapted_ref[...], wa_ref[...]).astype(BF16).astype(F32)
    row = lax.broadcasted_iota(jnp.int32, d_pooled.shape, 0) + base * GRID_HI * 9 // 16
    d_pooled = jnp.where(row < s_ref[0] * GRID_LO, d_pooled, 0.0)
    d_pooled_ref[...] = d_pooled.astype(BF16)
    scaled = (d_pooled * scale_ref[...]).astype(BF16)
    sums_ref[0:1, :] = jnp.sum(scaled.astype(F32), axis=0, keepdims=True)
    sums_ref[1:2, :] = jnp.sum(d_pooled, axis=0, keepdims=True)
    sums_ref[2:, :] = jnp.zeros((6, cb), F32)


def front(hires, kernel, bias, cotangent, gate, w_adapt, layer_scale, scalars, base, count, after=()):
    channels = hires.shape[3]
    width = cotangent.shape[2]
    cb = channel_block(channels)
    cells = count * GRID_HI
    pooled_rows = cells * 9 // 16
    chunk = base // count

    def column(rows):
        return pl.BlockSpec((rows, cb), lambda j, s: (0, j))

    return call(
        functools.partial(front_kernel, base, count),
        "front",
        (channels // cb,),
        [
            pl.BlockSpec((None, GRID_HI, GRID_HI, cb), lambda j, s: (s[3], 0, 0, j)),
            column(49),
            column(1),
            held((POOL_BLOCK, CELL_BLOCK)),
            pl.BlockSpec((None, pooled_rows, width), lambda j, s: (s[3], chunk, 0)),
            held((1, width)),
            pl.BlockSpec((cb, width), lambda j, s: (j, 0)),
            column(1),
        ],
        [
            (column(cells), array((cells, channels))),
            (column(pooled_rows), array((pooled_rows, channels), F32)),
            (column(pooled_rows), array((pooled_rows, channels))),
            (whole((pooled_rows, width)), array((pooled_rows, width))),
            (column(8), array((8, channels), F32)),
            (whole((8, LANES)), array((8, LANES), jnp.int32)),
        ],
        (hires, kernel, bias.reshape(1, -1), pool_block(), cotangent, gate.reshape(1, -1), w_adapt)
        + (layer_scale.reshape(1, -1),),
        [pltpu.VMEM((7, count + 6, GRID_HI, cb), F32)],
        after,
        prefetch=scalars,
    )


def softmax_rows(q, k, key_valid):
    scores = jnp.where(key_valid, dot_nt(q, k) * HEAD_DIM ** (-0.5), -1e30)
    e = jnp.exp(scores - jnp.max(scores, axis=-1, keepdims=True))
    return e * (1.0 / jnp.sum(e, axis=-1, keepdims=True))


def attention_kernel(
    s_ref, x_ref, gain_ref, shift_ref, wq_ref, wk_ref, wv_ref, bias_ref,
    normed_ref, q_ref, k_ref, v_ref, att_ref,
):
    @pl.when(pl.program_id(0) == 0)
    def _():
        xhat, _ = standardize(x_ref[...].astype(F32), norm_epsilon)
        normed_ref[...] = (xhat * gain_ref[...] + shift_ref[...]).astype(BF16)

    normed = normed_ref[...]
    q_ref[...] = (dot(normed, wq_ref[...]) + bias_ref[0:1]).astype(BF16)
    k_ref[...] = dot(normed, wk_ref[...]).astype(BF16)
    v_ref[...] = (dot(normed, wv_ref[...]) + bias_ref[1:2]).astype(BF16)
    key = lax.broadcasted_iota(jnp.int32, (1, TOKENS), 1)
    key_valid = key < s_ref[0] * GRID_LO
    for h in range(q_ref.shape[1] // HEAD_DIM):
        cut = slice(h * HEAD_DIM, (h + 1) * HEAD_DIM)
        probs = softmax_rows(q_ref[:, cut], k_ref[:, cut], key_valid)
        att_ref[:, cut] = dot(probs.astype(BF16), v_ref[:, cut]).astype(BF16)


def image(width):
    return pl.BlockSpec((None, TOKENS, width), lambda j, s: (s[3], 0, 0))


def attention_forward(tokens, gain, shift, w_flat, qv_bias, scalars, after=()):
    width = tokens.shape[2]
    heads_width = w_flat.shape[1] // 3
    blocks = heads_width // LANES
    column = (pl.BlockSpec((TOKENS, LANES), lambda j, s: (0, j)), array((TOKENS, heads_width)))

    def weight(t):
        return pl.BlockSpec((width, LANES), lambda j, s: (0, t * blocks + j))

    return call(
        attention_kernel,
        "attention_forward",
        (blocks,),
        [image(width), held((1, width)), held((1, width)), weight(0), weight(1), weight(2)]
        + [pl.BlockSpec((2, LANES), lambda j, s: (0, j))],
        [(whole((TOKENS, width)), array((TOKENS, width)))] + [column] * 4,
        (tokens, gain.reshape(1, -1), shift.reshape(1, -1)) + (w_flat,) * 3 + (qv_bias,),
        after=after,
        prefetch=scalars,
    )


def attention_back_kernel(n_mp, scalars_ref, *refs):
    pieces, refs = refs[:n_mp], refs[n_mp:]
    x_ref, gain_ref, w_out_ref, q_ref, k_ref, v_ref, wq_ref, wk_ref, wv_ref = refs[:9]
    d_attn_ref, dq_ref, dk_ref, dv_ref = refs[9:13]
    send_ref, total = refs[13:]
    step = pl.program_id(0)
    mp = scalars_ref[1]
    part = pieces[0].shape[0]

    @pl.when(step == 0)
    def _():
        for k in range(n_mp):
            at = pl.multiple_of((mp ^ k) * part, part)
            total[pl.ds(at, part), :] = pieces[k][...].astype(F32)
        d_attn_ref[...] = total[...].astype(BF16)

    d_att_all = dot_nt(d_attn_ref[...], w_out_ref[...]).astype(BF16)
    key = lax.broadcasted_iota(jnp.int32, (1, TOKENS), 1)
    key_valid = key < scalars_ref[0] * GRID_LO
    scale = HEAD_DIM ** (-0.5)
    for h in range(q_ref.shape[1] // HEAD_DIM):
        cut = slice(h * HEAD_DIM, (h + 1) * HEAD_DIM)
        q, k, v, d_att = q_ref[:, cut], k_ref[:, cut], v_ref[:, cut], d_att_all[:, cut]
        probs = softmax_rows(q, k, key_valid)
        d_probs = dot_nt(d_att, v)
        delta = jnp.sum(probs * d_probs, axis=-1, keepdims=True)
        d_scores = (probs * (d_probs - delta)).astype(BF16)
        dq_ref[:, cut] = (dot(d_scores, k) * scale).astype(BF16)
        dk_ref[:, cut] = (dot_tn(d_scores, q) * scale).astype(BF16)
        dv_ref[:, cut] = dot_tn(probs.astype(BF16), d_att).astype(BF16)
    share = dot_nt(dq_ref[...], wq_ref[...]) + dot_nt(dk_ref[...], wk_ref[...])
    share = share + dot_nt(dv_ref[...], wv_ref[...])

    @pl.when(step == 0)
    def _():
        total[...] = share

    @pl.when(step > 0)
    def _():
        total[...] += share

    @pl.when(step == pl.num_programs(0) - 1)
    def _():
        features = send_ref.shape[2]
        xhat, _ = standardize(x_ref[...].astype(F32), norm_epsilon)
        weighted = total[...] * gain_ref[...]
        ones = jnp.sum(weighted, axis=-1, keepdims=True)
        twos = jnp.sum(weighted * xhat, axis=-1, keepdims=True)
        pad = jnp.zeros((-TOKENS % LANES, 1), F32)
        stats = stat_rows([jnp.concatenate([ones, pad]), jnp.concatenate([twos, pad])], features)
        for g in range(n_mp):
            mine = slice(g * features, (g + 1) * features)
            send_ref[g, :TOKENS, :] = total[:, mine].astype(BF16)
            send_ref[g, TOKENS:, :] = stats


def attention_backward(
    n_mp, tokens, gain, d_attn_pieces, w_out, q, k, v, w_flat, scalars, after=()
):
    width = tokens.shape[2]
    heads_width = q.shape[1]
    blocks = heads_width // LANES
    column = pl.BlockSpec((TOKENS, LANES), lambda j, s: (0, j))

    def weight(t):
        return pl.BlockSpec((width, LANES), lambda j, s: (0, t * blocks + j))

    send_shape = (n_mp, TOKENS + STAT_ROWS, width // n_mp)
    return call(
        functools.partial(attention_back_kernel, n_mp),
        "attention_backward",
        (blocks,),
        [held(d_attn_pieces[0].shape)] * n_mp
        + [image(width), held((1, width)), pl.BlockSpec((LANES, width), lambda j, s: (j, 0))]
        + [column, column, column, weight(0), weight(1), weight(2)],
        [(whole((TOKENS, width)), array((TOKENS, width)))]
        + [(column, array((TOKENS, heads_width)))] * 3
        + [(held(send_shape), array(send_shape))],
        (*d_attn_pieces, tokens, gain.reshape(1, -1), w_out, q, k, v, w_flat, w_flat, w_flat),
        [pltpu.VMEM((TOKENS, width), F32)],
        after,
        prefetch=scalars,
    )


def conv_mlp_kernel(
    n_mp, chunk, s_ref, rows_ref, gain_ref, shift_ref, w1_hbm, b_ref, w2_hbm, wa_hbm, d_adapted_ref, pool_ref,
    normed_ref, inner_ref, pooled_ref, back_ref, send_ref, mean_ref, inv_ref, bias_ref,
    branch_ref, adapted_ref, scale_ref, full, w1_ref, w2_ref, wa_ref, sems,
):
    cells, channels = rows_ref.shape[1:]
    cut = 256
    steps = w1_ref.shape[1] // cut
    cuts = [slice(j * cut, (j + 1) * cut) for j in range(steps)]
    loads = [pltpu.make_async_copy(wa_hbm, wa_ref, sems.at[2 * steps])]
    for j, at in enumerate(cuts):
        loads.append(pltpu.make_async_copy(w1_hbm.at[:, at], w1_ref.at[:, at], sems.at[j]))
        loads.append(pltpu.make_async_copy(w2_hbm.at[at, :], w2_ref.at[at, :], sems.at[steps + j]))
    for load in loads:
        load.start()
    for g in range(n_mp):
        full[:, g * channels : (g + 1) * channels] = rows_ref[g].astype(F32)
    spatial = full[...]
    mean = jnp.mean(spatial, axis=-1, keepdims=True)
    centred = spatial - mean
    inv = lax.rsqrt(jnp.mean(centred * centred, axis=-1, keepdims=True) + channel_epsilon)
    xhat = centred * inv
    full[...] = xhat
    mean_ref[...] = jnp.broadcast_to(mean, mean_ref.shape)
    inv_ref[...] = jnp.broadcast_to(inv, inv_ref.shape)
    normed_ref[...] = (xhat * gain_ref[...] + shift_ref[...]).astype(BF16)
    loads[0].wait()
    count = back_ref.shape[0]
    valid = lax.broadcasted_iota(jnp.int32, (count, 1), 0) + chunk * count < s_ref[0] * GRID_LO
    back = dot_nt(d_adapted_ref[...], wa_ref[...])
    back_ref[...] = jnp.where(valid, back, 0.0).astype(BF16)
    for j, at in enumerate(cuts):
        loads[2 * j + 1].wait()
        active, slope = gelu_pair(dot(normed_ref[...], w1_ref[:, at]) + b_ref[:, at])
        active = active.astype(BF16)
        loads[2 * j + 2].wait()
        d_active = dot_nt(back_ref[...], w2_ref[at, :]).astype(BF16)
        backs = []
        for i in range(cells // CELL_BLOCK):
            lo = slice(i * POOL_BLOCK, (i + 1) * POOL_BLOCK)
            hi = slice(i * CELL_BLOCK, (i + 1) * CELL_BLOCK)
            pooled_ref[lo, at] = dot(pool_ref[...], active[hi]).astype(BF16)
            backs.append(dot_tn(pool_ref[...], d_active[lo]))
        d_inner = (slope * jnp.concatenate(backs, axis=0)).astype(BF16)
        inner_ref[:, at] = d_inner
        bias_ref[:, at] = jnp.sum(d_inner.astype(F32), axis=0, keepdims=True)

    d_normed = dot_nt(inner_ref[...], w1_ref[...])
    weighted = d_normed * gain_ref[...]
    ones = jnp.sum(weighted, axis=-1, keepdims=True)
    twos = jnp.sum(weighted * full[...], axis=-1, keepdims=True)
    stats = stat_rows([ones, twos], channels)
    for g in range(n_mp):
        send_ref[g, :cells, :] = d_normed[:, g * channels : (g + 1) * channels].astype(BF16)
        send_ref[g, cells:, :] = stats
    branch = dot(pooled_ref[...], w2_ref[...])
    scale_ref[...] = jnp.sum(back_ref[...].astype(F32) * branch, axis=0, keepdims=True)
    branch_ref[...] = jnp.where(valid, branch, 0.0).astype(BF16)
    adapted_ref[...] = dot(branch_ref[...], wa_ref[...])


def conv_mlp(rows, gain, shift, w1, b, w2, wa, d_adapted, chunk, scalars, after=()):
    n_mp, cells, channels = rows.shape
    total, hidden = w1.shape
    width = wa.shape[1]
    pooled = cells * 9 // 16
    send_shape = (n_mp, cells + STAT_ROWS, channels)
    anywhere = pl.BlockSpec(memory_space=pl.ANY)

    def out(shape, dtype=BF16):
        return (held(shape), array(shape, dtype))

    return call(
        functools.partial(conv_mlp_kernel, n_mp, chunk),
        "conv_mlp",
        (1,),
        [held((n_mp, cells, channels)), held((1, total)), held((1, total)), anywhere]
        + [held((1, hidden)), anywhere, anywhere, held((pooled, width))]
        + [held((POOL_BLOCK, CELL_BLOCK))],
        [
            out((cells, total)),
            out((cells, hidden)),
            out((pooled, hidden)),
            out((pooled, total)),
            out(send_shape),
            out((cells, LANES), F32),
            out((cells, LANES), F32),
            out((1, hidden), F32),
            out((pooled, total)),
            out((pooled, width), F32),
            out((1, total), F32),
        ],
        (rows, gain.reshape(1, -1), shift.reshape(1, -1), w1, b.reshape(1, -1), w2, wa, d_adapted)
        + (pool_block(),),
        [
            pltpu.VMEM((cells, total), F32),
            pltpu.VMEM((total, hidden), BF16),
            pltpu.VMEM((hidden, total), BF16),
            pltpu.VMEM((total, width), BF16),
            pltpu.SemaphoreType.DMA((2 * (hidden // 256) + 1,)),
        ],
        after,
        prefetch=scalars,
    )


def conv_back_kernel(chunks, total_channels, s_ref, *refs):
    (received, spatial, means, invs, d_pooled) = (
        refs[i * chunks : (i + 1) * chunks] for i in range(5)
    )
    refs = refs[5 * chunks :]
    field_ref, k_ref, gain_ref, pool_ref, out_ref, g_kernel_ref, sums_ref, shifted, moved = refs
    hi_valid = s_ref[5]
    cb = field_ref.shape[2]
    gain = gain_ref[...]
    zeros = jnp.zeros((GRID_HI, cb), F32)
    for a in (0, 1, 2, GRID_HI + 3, GRID_HI + 4, GRID_HI + 5):
        for s in range(7):
            shifted[s, a] = zeros
            moved[s, a] = zeros
    g_gain = jnp.zeros((1, cb), F32)
    g_shift = jnp.zeros((1, cb), F32)
    g_bias = jnp.zeros((1, cb), F32)
    block_rows = CELL_BLOCK // GRID_HI
    first = 0
    for c in range(chunks):
        cells = means[c].shape[0]
        per = cells // LANES
        stats = received[c][cells : cells + STAT_ROWS, :LANES].astype(F32)
        rows = [
            jnp.concatenate([stats[k * per + t : k * per + t + 1] for t in range(per)], axis=1)
            for k in range(2)
        ]
        rows.append(jnp.zeros((LANES - 2, cells), F32))
        columns = jnp.concatenate(rows, axis=0).T * (1.0 / total_channels)
        for i in range(cells // CELL_BLOCK):
            at = slice(i * CELL_BLOCK, (i + 1) * CELL_BLOCK)
            d_normed = received[c][at, :].astype(F32)
            column = columns[at]
            if cb > LANES:
                mean, inv = means[c][at, :1], invs[c][at, :1]
            else:
                mean, inv = means[c][at], invs[c][at]
            xhat = (spatial[c][at].astype(F32) - mean) * inv
            d_spatial = inv * (d_normed * gain - column[:, 0:1] - xhat * column[:, 1:2])
            g_gain = g_gain + jnp.sum(d_normed * xhat, axis=0, keepdims=True)
            g_shift = g_shift + jnp.sum(d_normed, axis=0, keepdims=True)
            g_bias = g_bias + jnp.sum(d_spatial, axis=0, keepdims=True)
            for a in range(block_rows):
                store_shifted(moved, first + a + 3, d_spatial[a * GRID_HI : (a + 1) * GRID_HI])
            first += block_rows

    @pl.loop(0, GRID_HI)
    def _(a):
        row = jnp.where(a < hi_valid, field_ref[a].astype(F32), 0.0)
        store_shifted(shifted, a + 3, row)

    g_kernel_ref[...] = jnp.zeros(g_kernel_ref.shape, F32)
    for s in range(7):
        def rows_of(i, sums):
            a0 = i * 2
            grads = [moved[3, a0 + o + 3] for o in range(2)]
            sums = list(sums)
            for r_in in range(8):
                value = shifted[s, a0 + r_in]
                for o in range(2):
                    r = r_in - o
                    if 0 <= r < 7:
                        product = value * grads[o]
                        sums[r] = sums[r] + jnp.sum(product.reshape(GRID_HI // 8, 8, cb), axis=0)
            return tuple(sums)

        sums = lax.fori_loop(0, GRID_HI // 2, rows_of, tuple(jnp.zeros((8, cb), F32) for _ in range(7)))
        for r in range(7):
            t = r * 7 + s
            g_kernel_ref[t : t + 1, :] = jnp.sum(sums[r], axis=0, keepdims=True)
    sums_ref[...] = jnp.concatenate([g_bias, g_gain, g_shift, jnp.zeros((5, cb), F32)], axis=0)

    for i in range(CELLS // CELL_BLOCK):
        each = CELLS // CELL_BLOCK // chunks
        lo = slice((i % each) * POOL_BLOCK, (i % each + 1) * POOL_BLOCK)
        refined = dot_tn(pool_ref[...], d_pooled[i // each][lo, :])
        shifted[0, i * block_rows : (i + 1) * block_rows] = refined.reshape(block_rows, GRID_HI, cb)

    @pl.loop(0, GRID_HI, step=4)
    def _(a0):
        sums = correlate(
            moved, a0, 4, lambda r, s: k_ref[48 - (r * 7 + s) : 49 - (r * 7 + s), :], jnp.zeros((GRID_HI, cb), F32)
        )
        for o in range(4):
            value = sums[o] + shifted[0, a0 + o]
            out_ref[a0 + o] = jnp.where(a0 + o < hi_valid, value, 0.0).astype(BF16)


def conv_backward(
    received, spatial, means, invs, d_pooled, hires, kernel, my_gain, total_channels, scalars, after=()
):
    chunks = len(received)
    channels = hires.shape[3]
    cb = channel_block(channels)
    cells = means[0].shape[0]

    def column(rows):
        return pl.BlockSpec((rows, cb), lambda j, s: (0, j))

    map_block = pl.BlockSpec((GRID_HI, GRID_HI, cb), lambda j, s: (0, 0, j))
    return call(
        functools.partial(conv_back_kernel, chunks, total_channels),
        "conv_backward",
        (channels // cb,),
        [column(cells + STAT_ROWS)] * chunks
        + [column(cells)] * chunks
        + [held((cells, LANES))] * (2 * chunks)
        + [column(d_pooled[0].shape[0])] * chunks
        + [
            pl.BlockSpec((None, GRID_HI, GRID_HI, cb), lambda j, s: (s[3], 0, 0, j)),
            column(49),
            column(1),
            held((POOL_BLOCK, CELL_BLOCK)),
        ],
        [
            (map_block, array((GRID_HI, GRID_HI, channels))),
            (column(49), array((49, channels), F32)),
            (column(8), array((8, channels), F32)),
        ],
        (*received, *spatial, *means, *invs, *d_pooled)
        + (hires, kernel, my_gain.reshape(1, -1), pool_block()),
        [pltpu.VMEM((7, GRID_HI + 6, GRID_HI, cb), F32)] * 2,
        after,
        prefetch=scalars,
    )


def vit_mlp_kernel(n_mp, scalars_ref, *refs):
    pieces, refs = refs[:n_mp], refs[n_mp:]
    x_ref, wo_hbm, ob_ref, gain_ref, shift_ref, w1_hbm, b1_ref, w2_hbm, dy_ref = refs[:9]
    hidden_ref, normed_ref, active_ref, inner_ref, bias_ref = refs[9:14]
    sends, refs = refs[14 : 14 + n_mp], refs[14 + n_mp :]
    d_normed, wo_ref, w1_ref, w2_ref, sems = refs
    step = pl.program_id(0)
    rows = x_ref.shape[0]
    cut = 256
    cuts = [slice(j * cut, (j + 1) * cut) for j in range(w1_ref.shape[1] // cut)]
    loads = [pltpu.make_async_copy(wo_hbm, wo_ref, sems.at[0])]
    for j, at in enumerate(cuts):
        loads.append(pltpu.make_async_copy(w1_hbm.at[:, at], w1_ref.at[:, at], sems.at[2 * j + 1]))
        loads.append(pltpu.make_async_copy(w2_hbm.at[at, :], w2_ref.at[at, :], sems.at[2 * j + 2]))

    @pl.when(step == 0)
    def _():
        for load in loads:
            load.start()
        loads[0].wait()

    hidden = x_ref[...].astype(F32) + ob_ref[...]
    for k in range(n_mp):
        hidden = hidden + dot(pieces[k][...], wo_ref[k])
    hidden_ref[...] = hidden
    xhat, _ = standardize(hidden, norm_epsilon)
    normed_ref[...] = (xhat * gain_ref[...] + shift_ref[...]).astype(BF16)

    @pl.when(step == 0)
    def _():
        for load in loads[1:]:
            load.wait()

    for j, at in enumerate(cuts):
        active, slope = gelu_pair(dot(normed_ref[...], w1_ref[:, at]) + b1_ref[:, at])
        active_ref[:, at] = active.astype(BF16)
        d_inner = (slope * dot_nt(dy_ref[...], w2_ref[at, :])).astype(BF16)
        inner_ref[:, at] = d_inner
        sums = jnp.sum(d_inner.astype(F32), axis=0, keepdims=True)

        @pl.when(step == 0)
        def _():
            bias_ref[:, at] = sums

        @pl.when(step > 0)
        def _():
            bias_ref[:, at] += sums

    d_normed[pl.ds(pl.multiple_of(step * rows, rows), rows), :] = dot_nt(inner_ref[...], w1_ref[...])

    @pl.when(step == pl.num_programs(0) - 1)
    def _():
        part = sends[0].shape[0]
        for k in range(n_mp):
            at = pl.multiple_of((scalars_ref[1] ^ k) * part, part)
            sends[k][...] = d_normed[pl.ds(at, part), :].astype(BF16)


def vit_mlp(
    tokens, attended_pieces, w_out_pieces, out_bias, gain, shift, w1, b1, w2, cotangent, scalars, after=()
):
    n_mp = len(attended_pieces)
    heads_width = attended_pieces[0].shape[1]
    width, hidden = w1.shape
    rows = TOKENS // 2
    image_rows = pl.BlockSpec((None, rows, width), lambda j, s: (s[3], j, 0))
    row = pl.BlockSpec((rows, width), lambda j, s: (j, 0))
    row_hidden = pl.BlockSpec((rows, hidden), lambda j, s: (j, 0))
    one = held((1, width))
    anywhere = pl.BlockSpec(memory_space=pl.ANY)
    send_shape = (TOKENS // n_mp, width)
    return call(
        functools.partial(vit_mlp_kernel, n_mp),
        "vit_mlp",
        (TOKENS // rows,),
        [pl.BlockSpec((rows, heads_width), lambda j, s: (j, 0))] * n_mp
        + [image_rows, anywhere, one, one, one, anywhere, held((1, hidden)), anywhere, image_rows],
        [
            (row, array((TOKENS, width), F32)),
            (row, array((TOKENS, width))),
            (row_hidden, array((TOKENS, hidden))),
            (row_hidden, array((TOKENS, hidden))),
            (whole((1, hidden)), array((1, hidden), F32)),
        ]
        + [(whole(send_shape), array(send_shape))] * n_mp,
        (*attended_pieces, tokens, w_out_pieces, out_bias.reshape(1, -1), gain.reshape(1, -1))
        + (shift.reshape(1, -1), w1, b1.reshape(1, -1), w2, cotangent),
        [
            pltpu.VMEM((TOKENS, width), F32),
            pltpu.VMEM((n_mp, heads_width, width), BF16),
            pltpu.VMEM((width, hidden), BF16),
            pltpu.VMEM((hidden, width), BF16),
            pltpu.SemaphoreType.DMA((1 + 2 * (hidden // 256),)),
        ],
        after,
        prefetch=scalars,
    )


def adapter_kernel(chunks, scalars_ref, *refs):
    parts, fields = refs[:chunks], refs[chunks : 2 * chunks]
    refs = refs[2 * chunks :]
    pb_ref, scale_ref, wa_ref, active_ref, w2_ref, gate_ref, dy_ref = refs[:7]
    pooled_ref, gate_sum_ref = refs[7:9]
    send_ref, total = refs[9:]
    first = 0
    for field in fields:
        rows = slice(first, first + field.shape[0])
        value = field[...] + scale_ref[...] * pb_ref[...]
        row = lax.broadcasted_iota(jnp.int32, value.shape, 0) + first
        value = jnp.where(row < scalars_ref[0] * GRID_LO, value, 0.0)
        pooled_ref[rows, :] = value.astype(BF16)
        first += field.shape[0]
    total[...] = dot(pooled_ref[...], wa_ref[...])
    first = 0
    for part in parts:
        total[first : first + part.shape[0], :] += part[...]
        first += part.shape[0]
    gate = gate_ref[...]
    adapted = total[...]
    sums = jnp.sum(dy_ref[...].astype(F32) * adapted, axis=0, keepdims=True)
    gate_sum_ref[...] = (1.0 - gate * gate) * sums
    total[...] = dot(active_ref[...], w2_ref[...]) + gate * adapted
    features = send_ref.shape[2]
    for g in range(send_ref.shape[0]):
        send_ref[g] = total[:, g * features : (g + 1) * features].astype(BF16)


def adapter(n_mp, parts, fields, pw2_bias, layer_scale, w_adapt, active, w2, gate, cotangent, scalars, after=()):
    channels, width = w_adapt.shape
    hidden = w2.shape[0]
    send_shape = (n_mp, TOKENS, width // n_mp)
    return call(
        functools.partial(adapter_kernel, len(fields)),
        "adapter",
        (1,),
        [held(v.shape) for v in (*parts, *fields)]
        + [held((1, channels)), held((1, channels)), held((channels, width))]
        + [held((TOKENS, hidden)), held((hidden, width)), held((1, width)), image(width)],
        [
            (held((TOKENS, channels)), array((TOKENS, channels))),
            (held((1, width)), array((1, width), F32)),
            (held(send_shape), array(send_shape)),
        ],
        (*parts, *fields, pw2_bias.reshape(1, -1), layer_scale.reshape(1, -1), w_adapt)
        + (active, w2, gate.reshape(1, -1), cotangent),
        [pltpu.VMEM((TOKENS, width), F32)],
        after,
        prefetch=scalars,
    )


def weight_grad_kernel(counts, block, scalars_ref, *refs):
    pairs = sum(counts)
    lefts, rights = refs[:pairs], refs[pairs : 2 * pairs]
    keep_ref, send_ref = refs[2 * pairs :]
    core = scalars_ref[2]
    at = 0
    used = sum(refs[pairs + sum(counts[:i])].shape[1] for i in range(len(counts)))
    if used < keep_ref.shape[2]:
        rest = jnp.zeros(keep_ref.shape[:2] + (keep_ref.shape[2] - used,), BF16)
        keep_ref[:, :, used:] = rest
        send_ref[:, :, used:] = rest
    first = 0
    for count in counts:
        total = dot_tn(lefts[first][...], rights[first][...])
        for i in range(first + 1, first + count):
            total = total + dot_tn(lefts[i][...], rights[i][...])
        first += count
        lanes = slice(at, at + total.shape[1])
        at += total.shape[1]
        total = total.astype(BF16)
        for q in range(keep_ref.shape[0]):
            halves = [total[(2 * q + h) * block : (2 * q + h + 1) * block] for h in range(2)]

            @pl.when(core == 0)
            def _():
                keep_ref[q, :, lanes] = halves[0]
                send_ref[q, :, lanes] = halves[1]

            @pl.when(core != 0)
            def _():
                keep_ref[q, :, lanes] = halves[1]
                send_ref[q, :, lanes] = halves[0]


def weight_grads(name, groups, grads, scalars, after=(), lanes=None):
    block = grads[0][0][0].shape[1] // groups
    pairs = [pair for grad in grads for pair in grad]
    quads = 1
    while (2 * block * quads) % LANES:
        quads += 1
    total = lanes or sum(grad[0][1].shape[1] for grad in grads)
    out = (
        pl.BlockSpec((quads, block, total), lambda j: (j, 0, 0)),
        array((groups // 2, block, total)),
    )
    return call(
        functools.partial(weight_grad_kernel, [len(grad) for grad in grads], block),
        name,
        (groups // 2 // quads,),
        [SCALARS]
        + [pl.BlockSpec((left.shape[0], 2 * block * quads), lambda j: (0, j)) for left, _ in pairs]
        + [held(right.shape) for _, right in pairs],
        [out, out],
        (scalars, *(left for left, _ in pairs), *(right for _, right in pairs)),
        after=after,
    )


def fold_kernel(_, *refs):
    count = len(refs) // 4
    for p in range(count):
        keep, got = refs[2 * p : 2 * p + 2]
        send, hold = refs[2 * (count + p) : 2 * (count + p) + 2]

        def total():
            return (keep[...].astype(F32) + got[...].astype(F32)).astype(BF16)

        @pl.when(pl.program_id(0) == 0)
        def _():
            send[...] = total().reshape(send.shape)

        @pl.when(pl.program_id(0) == 1)
        def _():
            hold[...] = total().reshape(hold.shape)


def fold(name, parts, scalars, after=()):
    ins, operands, outs = [], [], []
    for keep, got, dim, slot, lanes, block in parts:
        shape = list(keep.shape)
        shape[dim] //= 2
        shape[-1] = lanes
        assert keep.shape[dim] == 2

        def at(j, s, dim=dim, slot=slot, rank=len(shape), block=block):
            index = [0] * rank
            index[dim] = s[slot] ^ (1 - j)
            index[-1] = block
            return tuple(index)

        ins += [pl.BlockSpec(tuple(shape), at)] * 2
        operands += [keep, got]
        out = tuple(shape[:dim] + shape[dim + 1 :])
        outs += [(whole(out), array(out))] * 2
    return call(
        fold_kernel, name, (2,), ins, outs, operands, after=after, prefetch=scalars
    )


def norm2_back_kernel(n_mp, scalars_ref, *refs):
    got, refs = refs[:n_mp], refs[n_mp:]
    hidden_ref, dy_ref, gain_ref, d_attn_ref, sums_ref = refs
    d_normed = got[0][...].astype(F32)
    for value in got[1:]:
        d_normed = d_normed + value[...].astype(F32)
    xhat, inv = standardize(hidden_ref[...], norm_epsilon)
    dxhat = d_normed * gain_ref[...]
    d_hidden = dy_ref[...].astype(F32) + inv * (
        dxhat
        - jnp.mean(dxhat, axis=-1, keepdims=True)
        - xhat * jnp.mean(dxhat * xhat, axis=-1, keepdims=True)
    )
    d_attn = d_hidden.astype(BF16)
    d_attn_ref[...] = d_attn
    sums_ref[0:1, :] = jnp.sum(d_attn.astype(F32), axis=0, keepdims=True)
    sums_ref[1:2, :] = jnp.sum(d_normed * xhat, axis=0, keepdims=True)
    sums_ref[2:3, :] = jnp.sum(d_normed, axis=0, keepdims=True)
    sums_ref[3:, :] = jnp.zeros((5, sums_ref.shape[1]), F32)


def norm2_backward(got, hidden, cotangent, gain, scalars, after=()):
    n_mp = len(got)
    rows, width = got[0].shape
    mine = pl.BlockSpec((None, rows, width), lambda j, s: (s[1], 0, 0))
    image_rows = pl.BlockSpec((None, None, rows, width), lambda j, s: (s[3], s[1], 0, 0))
    return call(
        functools.partial(norm2_back_kernel, n_mp),
        "norm2_backward",
        (1,),
        [held((rows, width))] * n_mp + [mine, image_rows, held((1, width))],
        [
            (held((rows, width)), array((rows, width))),
            (held((8, width)), array((8, width), F32)),
        ],
        (*got, hidden.reshape(n_mp, rows, width), cotangent.reshape(-1, n_mp, rows, width))
        + (gain.reshape(1, -1),),
        after=after,
        prefetch=scalars,
    )


def norm1_back_kernel(n_mp, scalars_ref, *refs):
    got, refs = refs[:n_mp], refs[n_mp:]
    x_ref, mine_ref, d_attn_ref, gain_ref, dy_ref, keep_ref, send_ref, sums_ref, total = refs
    width = x_ref.shape[1]
    value = got[0][...].astype(F32)
    for piece in got[1:]:
        value = value + piece[...].astype(F32)
    d_normed, stats = value[:TOKENS], value[TOKENS:, :LANES]
    count = -(-TOKENS // LANES)
    rows = [
        jnp.concatenate([stats[k * count + t : k * count + t + 1] for t in range(count)], axis=1)
        for k in range(2)
    ]
    rows.append(jnp.zeros((LANES - 2, count * LANES), F32))
    columns = jnp.concatenate(rows, axis=0).T[:TOKENS] * (1.0 / width)
    x = x_ref[...].astype(F32)
    mean = jnp.mean(x, axis=-1, keepdims=True)
    inv = lax.rsqrt(jnp.mean((x - mean) * (x - mean), axis=-1, keepdims=True) + norm_epsilon)
    xhat = (mine_ref[...].astype(F32) - mean) * inv
    total[...] = d_attn_ref[...].astype(F32) + inv * (
        d_normed * gain_ref[...] - columns[:, 0:1] - xhat * columns[:, 1:2]
    )
    half = TOKENS // 2
    path = scalars_ref[3]
    keep_ref[...] = total[pl.ds(pl.multiple_of(path * half, half), half), :].astype(BF16)
    send_ref[...] = total[pl.ds(pl.multiple_of((1 - path) * half, half), half), :].astype(BF16)
    sums_ref[0:1, :] = jnp.sum(d_normed * xhat, axis=0, keepdims=True)
    sums_ref[1:2, :] = jnp.sum(d_normed, axis=0, keepdims=True)
    sums_ref[2:3, :] = jnp.sum(dy_ref[...].astype(F32), axis=0, keepdims=True)
    sums_ref[3:, :] = jnp.zeros((5, sums_ref.shape[1]), F32)


def norm1_backward(got, tokens, d_attn, gain, cotangent, scalars, after=()):
    rows, features = got[0].shape
    width = tokens.shape[2]
    mine = pl.BlockSpec((TOKENS, features), lambda j, s: (0, s[1]))
    mine_of = pl.BlockSpec((None, TOKENS, features), lambda j, s: (s[3], 0, s[1]))
    half = (held((TOKENS // 2, features)), array((TOKENS // 2, features)))
    return call(
        functools.partial(norm1_back_kernel, len(got)),
        "norm1_backward",
        (1,),
        [held((rows, features))] * len(got)
        + [image(width), mine_of, mine]
        + [pl.BlockSpec((1, features), lambda j, s: (0, s[1])), mine_of],
        [half, half, (held((8, features)), array((8, features), F32))],
        (*got, tokens, tokens, d_attn, gain.reshape(1, -1), cotangent),
        [pltpu.VMEM((TOKENS, features), F32)],
        after=after,
        prefetch=scalars,
    )


def output_kernel(n_mp, scalars_ref, *refs):
    got, refs = refs[:n_mp], refs[n_mp:]
    hidden_ref, bias_ref, keep_ref, send_ref, total = refs
    value = hidden_ref[...] + bias_ref[...]
    for piece in got:
        value = value + piece[...].astype(F32)
    total[...] = value
    half = TOKENS // 2
    path = scalars_ref[3]
    keep_ref[...] = total[pl.ds(pl.multiple_of(path * half, half), half), :].astype(BF16)
    send_ref[...] = total[pl.ds(pl.multiple_of((1 - path) * half, half), half), :].astype(BF16)


def output_halves(got, hidden, fc2_bias, scalars, after=()):
    n_mp = len(got)
    features = got[0].shape[1]
    half = (held((TOKENS // 2, features)), array((TOKENS // 2, features)))
    return call(
        functools.partial(output_kernel, n_mp),
        "output_halves",
        (1,),
        [held((TOKENS, features))] * n_mp
        + [pl.BlockSpec((TOKENS, features), lambda j, s: (0, s[1]))]
        + [pl.BlockSpec((1, features), lambda j, s: (0, s[1]))],
        [half, half],
        (*got, hidden, fc2_bias.reshape(1, -1)),
        [pltpu.VMEM((TOKENS, features), F32)],
        after=after,
        prefetch=scalars,
    )


WIDE_ROWS = 7


def slots_of(shapes, width):
    row, lane, slots = 0, 0, []
    for rows, n in shapes:
        mine = []
        for _ in range(rows):
            pieces = []
            for at in range(0, n, width):
                size = min(width, n - at)
                if lane + size > width:
                    row, lane = row + 1, 0
                pieces.append((row, lane, at, size))
                lane += size
            mine.append(pieces)
        slots.append(mine)
    return slots, -(-(row + 1) // 8) * 8


def pack_kernel(n_mp, slots, s_ref, *refs):
    wide, refs = refs[:n_mp], refs[n_mp:]
    sums_ref, bias_ref, scale_ref, *arrays, packed_ref, total_ref = refs
    packed_ref[...] = jnp.zeros(packed_ref.shape, F32)
    total = wide[0][...]
    for piece in wide[1:]:
        total = total + piece[...]
    total_ref[...] = total
    channels = scale_ref.shape[1]
    mine = total_ref[pl.ds(WIDE_ROWS + s_ref[1], 1), :][:, :channels]
    g_scale = mine / scale_ref[...] + bias_ref[...] * sums_ref[1:2, :]
    values = [total[:WIDE_ROWS], g_scale, sums_ref[0:1, :]] + [v[...] for v in arrays]
    for value, mine in zip(values, slots):
        for r, pieces in enumerate(mine):
            for row, lane, at, n in pieces:
                packed_ref[row : row + 1, lane : lane + n] = value[r : r + 1, at : at + n]


def pack(wide_pieces, sums, pw2_bias, layer_scale, arrays, rows, scalars, after=()):
    n_mp = len(wide_pieces)
    width = wide_pieces[0].shape[1]
    channels = sums.shape[1]
    shapes = [(WIDE_ROWS, width), (1, channels), (1, channels)]
    shapes += [(count, v.shape[1]) for v, count in zip(arrays, rows)]
    slots, total = slots_of(shapes, width)
    operands = (*wide_pieces, sums, pw2_bias.reshape(1, -1), layer_scale.reshape(1, -1), *arrays)
    packed = call(
        functools.partial(pack_kernel, n_mp, slots),
        "pack",
        (1,),
        [held(v.shape) for v in operands],
        [(held((total, width)), array((total, width), F32))],
        operands,
        [pltpu.VMEM(wide_pieces[0].shape, F32)],
        after=after,
        prefetch=scalars,
    )[0]
    return packed, slots


def unpack_kernel(slots, a_ref, b_ref, *outs):
    for out, mine in zip(outs, slots):
        for r, pieces in enumerate(mine):
            for row, lane, at, n in pieces:
                out[r : r + 1, at : at + n] = (
                    a_ref[row : row + 1, lane : lane + n] + b_ref[row : row + 1, lane : lane + n]
                )


def unpack(a, b, slots, after=()):
    shapes = [(len(mine), sum(n for *_, n in mine[0])) for mine in slots]
    return call(
        functools.partial(unpack_kernel, slots),
        "unpack",
        (1,),
        [held(a.shape)] * 2,
        [(held(shape), array(shape, F32)) for shape in shapes],
        (a, b),
        after=after,
    )


def swap(value, axis, apart):
    n = lax.axis_size(axis)
    return lax.ppermute(value, axis, [(i, i ^ apart) for i in range(n)])


def pick(value, axis, index):
    return lax.dynamic_index_in_dim(value, index, axis, keepdims=False)


def gathered(value, axis):
    return [value] + [swap(value, axis, k) for k in range(1, lax.axis_size(axis))]


def exchanged(blocks, axis):
    return blocks[:1] + [swap(block, axis, k) for k, block in enumerate(blocks) if k]


def in_order(values, axis):
    me = lax.axis_index(axis)
    apart = 1
    while apart < len(values):
        turned = (me & apart) > 0
        values = [jnp.where(turned, values[i ^ apart], values[i]) for i in range(len(values))]
        apart *= 2
    return values


def spread(value, steps):
    for axis, apart, place in steps:
        other = swap(value, axis, apart)
        turned = (lax.axis_index(axis) & apart) > 0
        pair = [jnp.where(turned, other, value), jnp.where(turned, value, other)]
        value = jnp.stack(pair, axis=place)
    return value.reshape(value.shape[0], -1, value.shape[-1])


def halve(value, dim, axis, apart, bit):
    received = swap(pick(value, dim, 1 - bit), axis, apart)
    return pick(value, dim, bit).astype(F32) + received.astype(F32)


def across(halves):
    keep, send = halves
    return keep, swap(send, "dp", 1)


def first_fold(name, halves, scalars, after, dp_first=False):
    n_path, n_dp = lax.axis_size("path"), lax.axis_size("dp")
    block, lanes = halves[0].shape[1:]
    shape = (n_path, n_dp // 4, 2, block, lanes)
    keep, got = (half.reshape(shape) for half in halves)
    dim, slot = (2, 4) if dp_first else (0, 3)
    send, hold = fold(name, [(keep, got, dim, slot, lanes, 0)], scalars, after)
    return hold, swap(send, *(("dp", 2) if dp_first else ("path", 1))), dp_first


def second_fold(name, part, scalars, after):
    hold, got, path_next = part
    dim, slot = (0, 3) if path_next else (1, 4)
    send, hold = fold(name, [(hold, got, dim, slot, hold.shape[-1], 0)], scalars, after)
    return hold, swap(send, *(("path", 1) if path_next else ("dp", 2)))


def last_sum(hold, got):
    n_dp, me_dp = lax.axis_size("dp"), lax.axis_index("dp")
    value = hold.astype(F32) + got.astype(F32)
    size = value.shape[0]
    b = 2
    while size > 1:
        size //= 2
        shape = (size, 2) + value.shape[1:]
        value = halve(value.astype(BF16).reshape(shape), 1, "dp", 1 << b, (me_dp >> b) & 1)
        b += 1
    return value[0]


def summed_at_once(value, axis):
    return sum(gathered(value, axis))


def summed(value, axes):
    for axis in axes:
        apart = 1
        while apart < lax.axis_size(axis):
            value = value + swap(value, axis, apart)
            apart *= 2
    return value


def body(
    tokens,
    hires,
    valid_rows,
    cotangent,
    attention_norm_gain,
    attention_norm_bias,
    w_qkv,
    qv_bias,
    w_out,
    out_bias,
    mlp_norm_gain,
    mlp_norm_bias,
    w_fc1,
    fc1_bias,
    down_weight,
    fc2_bias,
    w_adapt,
    gate_param,
    dw_kernel,
    dw_bias,
    channel_norm_gain,
    channel_norm_bias,
    w_pw1,
    pw1_bias,
    w_pw2,
    pw2_bias,
    layer_scale,
):
    path = lax.axis_index("path")
    n_path = lax.axis_size("path")
    dp = lax.axis_index("dp")
    mp = lax.axis_index("mp")
    n_mp = lax.axis_size("mp")
    groups = n_path * lax.axis_size("dp")
    assert tokens.shape[0] == n_path == 2
    width = tokens.shape[2]
    heads_width = w_qkv.shape[2]
    features = width // n_mp
    channels = hires.shape[3]
    all_channels = w_pw1.shape[0]
    part_rows = TOKENS // n_mp
    chunk_rows = GRID_HI // CHUNKS

    valid = pick(valid_rows, 0, path)
    hi_valid = (valid * GRID_HI + GRID_LO - 1) // GRID_LO
    rank = path * lax.axis_size("dp") + dp
    scalars = jnp.stack([valid, mp, dp & 1, path, (dp >> 1) & 1, hi_valid, rank])
    gate = jnp.tanh(gate_param)

    def my_features(v):
        return lax.dynamic_slice_in_dim(v, mp * features, features, v.ndim - 1)

    rows, rows_all, pooled_field, d_pooled, d_adapted = [], [], [], [], []
    front_sums, ranks = 0.0, []
    last = ()
    for c in range(CHUNKS):
        send, *chunk, sums, rank_out = front(
            hires,
            dw_kernel,
            dw_bias,
            cotangent,
            gate,
            w_adapt,
            layer_scale,
            scalars,
            c * chunk_rows,
            chunk_rows,
            last,
        )
        last = (sums,)
        front_sums = front_sums + sums
        ranks.append(rank_out)
        rows.append(send)
        rows_all.append(lax.all_gather(send, "mp", axis=0, tiled=False))
        for kept, value in zip((pooled_field, d_pooled, d_adapted), chunk):
            kept.append(value)

    rank = ranks[-1][0, 0]
    out_rows, adapt_rows = heads_width // groups, channels // groups
    scaled = w_adapt.astype(F32) * layer_scale[:, None]
    share = jnp.concatenate(
        [
            lax.dynamic_slice_in_dim(w_out, rank * out_rows, out_rows, 0),
            lax.dynamic_slice_in_dim(scaled, rank * adapt_rows, adapt_rows, 0).astype(BF16),
        ]
    )
    shares = gathered(share, "mp")
    chips = [("dp", 1 << b, -3) for b in range(lax.axis_size("dp").bit_length() - 2, 0, -1)]
    w_out_pieces = spread(
        jnp.stack([v[:out_rows] for v in shares]), [("path", 1, -3)] + chips + [("dp", 1, -3)]
    )
    w_adapt_all = spread(
        jnp.stack(in_order([v[out_rows:] for v in shares], "mp")),
        chips + [("path", 1, 1), ("dp", 1, -3)],
    ).reshape(all_channels, width)

    w_flat = w_qkv.reshape(width, 3 * heads_width)
    normed1, query, keys, values, attended = attention_forward(
        tokens, attention_norm_gain, attention_norm_bias, w_flat, qv_bias, scalars, last + tuple(rows_all[:1])
    )
    attended_pieces = gathered(attended, "mp")
    last = (attended,)

    def conv(c, after):
        out = conv_mlp(
            rows_all[c],
            channel_norm_gain,
            channel_norm_bias,
            w_pw1,
            pw1_bias,
            w_pw2,
            w_adapt_all,
            d_adapted[c],
            c,
            scalars,
            after,
        )
        return out, lax.psum_scatter(out[4], "mp", scatter_dimension=0, tiled=False), (out[7],)

    conv_out, received = [], []
    out, got, last = conv(0, last)
    conv_out.append(out)
    received.append(got)
    hidden1, normed2, fc_active, d_fc_inner, g_fc1_bias, *sends = vit_mlp(
        tokens,
        attended_pieces,
        w_out_pieces,
        out_bias,
        mlp_norm_gain,
        mlp_norm_bias,
        w_fc1,
        fc1_bias,
        down_weight,
        cotangent,
        scalars,
        last,
    )
    d_normed2_pieces = exchanged(sends, "mp")
    last = (g_fc1_bias,)
    for c in range(1, CHUNKS):
        out, got, last = conv(c, last)
        conv_out.append(out)
        received.append(got)
    (
        conv_normed,
        conv_inner,
        pooled_active,
        backs,
        _,
        means,
        invs,
        bias_sums,
        branches,
        adapted_parts,
        scale_sums,
    ) = zip(*conv_out)
    g_pw1_bias = sum(bias_sums)

    pooled, g_gate, send = adapter(
        n_mp,
        adapted_parts,
        pooled_field,
        pw2_bias,
        layer_scale,
        w_adapt,
        fc_active,
        down_weight,
        gate,
        cotangent,
        scalars,
        last + tuple(received[:-1]),
    )
    branch_sum = lax.psum_scatter(send, "mp", scatter_dimension=0, tiled=False)
    d_attn_part, norm2_sums = norm2_backward(
        d_normed2_pieces, hidden1, cotangent, mlp_norm_gain, scalars, (g_gate,)
    )
    d_attn_pieces = gathered(d_attn_part, "mp")
    dy = pick(cotangent, 0, path)
    fc_halves = across(
        weight_grads(
            "grad_fc",
            groups,
            [[(normed2, d_fc_inner)], [(dy, fc_active)]],
            scalars,
            (norm2_sums,),
        )
    )
    pooled_rows = d_adapted[0].shape[0]
    pooled_cuts = [pooled[c * pooled_rows : (c + 1) * pooled_rows] for c in range(CHUNKS)]
    adapt_halves = across(
        weight_grads(
            "grad_adapt",
            groups,
            [list(zip(d_adapted, branches)), list(zip(d_adapted, pooled_cuts))],
            scalars,
            fc_halves[:1],
        )
    )
    pw2_halves = across(
        weight_grads(
            "grad_pw2", groups, [list(zip(backs, pooled_active))], scalars, adapt_halves[:1]
        )
    )
    pw1_halves = across(
        weight_grads(
            "grad_pw1", groups, [list(zip(conv_normed, conv_inner))], scalars, pw2_halves[:1]
        )
    )

    d_attn, d_query, d_keys, d_values, send = attention_backward(
        n_mp,
        tokens,
        attention_norm_gain,
        d_attn_pieces,
        w_out,
        query,
        keys,
        values,
        w_flat,
        scalars,
        pw1_halves[:1],
    )
    d_normed1 = lax.psum_scatter(send, "mp", scatter_dimension=0, tiled=False)
    fc_part = first_fold("fold_fc", fc_halves, scalars, (d_query, *received[1:]))
    adapt_part = first_fold("fold_adapt", adapt_halves, scalars, fc_part[:1], True)
    pw2_part = first_fold("fold_pw2", pw2_halves, scalars, adapt_part[:1], True)
    pw1_part = first_fold("fold_pw1", pw1_halves, scalars, pw2_part[:1])
    qkv_halves = across(
        weight_grads(
            "grad_qkv",
            groups,
            [
                [(normed1, d_query)],
                [(normed1, d_keys)],
                [(normed1, d_values)],
                [(d_attn, attended)],
            ],
            scalars,
            pw1_part[:1],
        )
    )
    g_qv_bias = jnp.stack(
        [jnp.sum(d_query.astype(F32), axis=0), jnp.sum(d_values.astype(F32), axis=0)]
    )

    tokens_keep, tokens_send, norm1_sums = norm1_backward(
        [d_normed1],
        tokens,
        d_attn,
        attention_norm_gain,
        cotangent,
        scalars,
        qkv_halves[:1],
    )

    def placed(v):
        return lax.dynamic_update_slice(jnp.zeros((width,), F32), v, (mp * features,))

    scale_rows = jnp.pad(sum(scale_sums).reshape(n_mp, channels), ((0, 0), (0, width - channels)))
    wide = jnp.concatenate(
        [norm2_sums[:3]]
        + [placed(norm1_sums[i])[None] for i in range(3)]
        + [g_gate, scale_rows]
    )
    wide_pieces = gathered(wide, "mp")
    d_field, g_kernel, conv_sums = conv_backward(
        received,
        rows,
        means,
        invs,
        d_pooled,
        hires,
        dw_kernel,
        lax.dynamic_slice_in_dim(channel_norm_gain, mp * channels, channels, 0),
        all_channels,
        scalars,
        (norm1_sums, fc_part[1], adapt_part[1]),
    )

    packed, slots = pack(
        wide_pieces,
        front_sums,
        pw2_bias,
        layer_scale,
        [g_qv_bias, g_fc1_bias, g_pw1_bias, g_kernel, conv_sums],
        (2, 1, 1, 49, 3),
        scalars,
        (conv_sums,),
    )
    packed_first = packed
    packed = summed(packed, ("dp",))
    qkv_part = first_fold("fold_qkv", qkv_halves, scalars, (packed_first,), True)
    output_keep, output_send = output_halves(
        [branch_sum], hidden1, fc2_bias, scalars, (qkv_part[0], pw2_part[1], pw1_part[1])
    )
    adapt_part = second_fold("fold_adapt_last", adapt_part, scalars, (output_keep,))
    fc_part = second_fold("fold_fc_last", fc_part, scalars, adapt_part[:1])
    pw2_part = second_fold("fold_pw2_last", pw2_part, scalars, fc_part[:1])
    pw1_part = second_fold("fold_pw1_last", pw1_part, scalars, pw2_part[:1])
    qkv_part = second_fold("fold_qkv_last", qkv_part, scalars, pw1_part[:1])

    def both_images(mine, send):
        other = swap(send, "path", 1)
        first = path == 0
        return jnp.stack([jnp.where(first, mine, other), jnp.where(first, other, mine)])

    def keep_half(rows):
        halves = rows.reshape((2, rows.shape[0] // 2) + rows.shape[1:])
        return both_images(pick(halves, 0, path), pick(halves, 0, 1 - path))

    output = both_images(output_keep, output_send)
    tokens_grad = both_images(tokens_keep, tokens_send)
    hires_grad = keep_half(d_field)

    g_adapt = last_sum(*adapt_part)
    g_adapt_mine = sum(
        piece.astype(F32)
        for piece in exchanged(
            [
                lax.dynamic_slice_in_dim(g_adapt, (mp ^ k) * channels, channels, 1).astype(BF16)
                for k in range(n_mp)
            ],
            "mp",
        )
    )
    g_adapt_mine = g_adapt_mine * layer_scale + g_adapt[:, all_channels:]
    g_fc = last_sum(*fc_part)
    g_fc1_mine, g_fc2_mine = g_fc[:, : w_fc1.shape[1]], g_fc[:, w_fc1.shape[1] :]
    g_pw1_mine, g_pw2_mine = last_sum(*pw1_part), last_sum(*pw2_part)
    g_rest = last_sum(*qkv_part)
    g_qkv_mine = g_rest[:, : 3 * heads_width].reshape(-1, 3, heads_width)
    g_out_mine = g_rest[:, 3 * heads_width :]

    small = unpack(packed, swap(packed, "path", 1), slots)
    wide, g_scale, g_pw2_bias, g_qv_bias, g_fc1_bias, g_pw1_bias, g_kernel, conv_sums = small
    g_out_bias, g_norm2_gain, g_norm2_bias, g_norm1_gain, g_norm1_bias, g_fc2_bias, g_gate = wide
    g_dw_bias, g_cnorm_gain, g_cnorm_bias = conv_sums
    return (
        output,
        tokens_grad,
        hires_grad,
        g_norm1_gain,
        g_norm1_bias,
        g_qkv_mine,
        g_qv_bias,
        g_out_mine.T,
        g_out_bias,
        g_norm2_gain,
        g_norm2_bias,
        g_fc1_mine,
        g_fc1_bias[0],
        g_fc2_mine.T,
        g_fc2_bias,
        g_adapt_mine.T,
        g_gate,
        g_kernel,
        g_dw_bias,
        g_cnorm_gain,
        g_cnorm_bias,
        g_pw1_mine,
        g_pw1_bias[0],
        g_pw2_mine.T,
        g_pw2_bias[0],
        g_scale[0],
    )


def solution(mesh):
    in_specs = (
        P("dp", None, None),
        P("dp", None, None, "mp"),
        P("dp"),
        P("dp", None, None),
        P(),
        P(),
        P(None, None, "mp"),
        P(None, "mp"),
        P("mp", None),
        P(),
        P(),
        P(),
        P(None, "mp"),
        P("mp"),
        P("mp", None),
        P(),
        P("mp", None),
        P(),
        P(None, "mp"),
        P("mp"),
        P(),
        P(),
        P(None, "mp"),
        P("mp"),
        P("mp", None),
        P("mp"),
        P("mp"),
    )
    out_specs = (
        P("dp", "path", "mp"),
        P("dp", "path", "mp"),
        P("dp", "path", None, "mp"),
        P(),
        P(),
        P(("path", "dp"), None, "mp"),
        P(None, "mp"),
        P("mp", ("path", "dp")),
        P(),
        P(),
        P(),
        P(("path", "dp"), "mp"),
        P("mp"),
        P("mp", ("path", "dp")),
        P(),
        P("mp", ("path", "dp")),
        P(),
        P(None, "mp"),
        P("mp"),
        P("mp"),
        P("mp"),
        P(("path", "dp"), "mp"),
        P("mp"),
        P("mp", ("path", "dp")),
        P("mp"),
        P("mp"),
    )
    return jax.shard_map(body, mesh=mesh, in_specs=in_specs, out_specs=out_specs, check_vma=False)
```
